32 devices in a mesh: row: 4 (over y, x), col: 8 (over z, core).
Axes of the slice: x: 2, y: 2, z: 4, core: 2. Of those that a mesh axis runs over, the one named last changes fastest.
Arguments:
- tokens: bfloat16 [12608, 512], P('col', 'row'), may hold values from -3 to 3
- ln1_gain: float32 [512], P('row'), may hold values from 0.5 to 1.5
- ln1_bias: float32 [512], P('row'), may hold values from -1.5 to 1.5
- qkv_weight: bfloat16 [512, 1536], P('row', 'col'), may hold values from -0.25 to 0.25
- out_weight: bfloat16 [512, 512], P('row', 'col'), may hold values from -1 to 1
- ln2_gain: float32 [512], P('row'), may hold values from 0.5 to 1.5
- ln2_bias: float32 [512], P('row'), may hold values from -1.5 to 1.5
- router_weight: bfloat16 [512, 32], P('row'), may hold values from -0.1875 to 0.1875
- expert_in: bfloat16 [32, 512, 2048], P(None, 'row', 'col'), may hold values from -0.25 to 0.25
- expert_out: bfloat16 [32, 2048, 512], P(None, 'row', 'col'), may hold values from -2 to 2
- routes: int32 [12608, 2], P('col'), may hold values from 0 to 31, all different within a row; in each aligned block of 1576 rows (0 to 1575, 1576 to 3151, ...) at most 120 rows name the same one
- keep: int32 [12608, 2], P('col'), may hold values 0 or 1
- cotangent: bfloat16 [12608, 512], P('col', 'row'), may hold values from -6 to 6
Outputs:
- layer_out: bfloat16 [12608, 512], P('col', 'row')
- tokens_grad: float32 [12608, 512], P('col', 'row')
- ln1_gain_grad: float32 [512], P(('row', 'col'))
- ln1_bias_grad: float32 [512], P(('row', 'col'))
- qkv_grad: float32 [512, 1536], P('row', 'col')
- out_weight_grad: float32 [512, 512], P('row', 'col')
- ln2_gain_grad: float32 [512], P(('row', 'col'))
- ln2_bias_grad: float32 [512], P(('row', 'col'))
- router_grad: float32 [512, 32], P(('row', 'col'))
- expert_in_grad: float32 [32, 512, 2048], P(None, 'row', 'col')
- expert_out_grad: float32 [32, 2048, 512], P(None, 'row', 'col')
The draws below stay inside these ranges and needn't reach their ends.
Inputs may be any that keep to these rules, and one draw needn't show every extreme that they name: `routes`: each row names two different experts. In each aligned block of 1576 rows no expert is named by more than 120 rows, and in some block some expert is named by exactly 120 rows.
All inputs are finite; a program needn't handle non-finite values. No bound on the sum of `keep` on one device may be relied on, other than what follows from the above.
Results may differ from the reference program's by a relative error of at most 0.019.
Values may be sent and summed in bfloat16 or wider, within the bound.
No kernel may reach another device: no remote copies, remote signals or barrier semaphores. Data moves between devices by JAX's collectives and lax.ppermute only.
A program may use at most 192 MiB of HBM per device.

```python
import math
import jax
import jax.numpy as jnp
import numpy as np
from jax import lax

D = 512
HEADS = 8
HID = 2048
E = 32
SEQ = 197
IMG = 8
HD = 64
BLOCK_TOK = 1576
TOKENS = 12608
CAP = 120


def touch_ends(array, own_key, smallest, high):
    longest = array.shape.index(max(array.shape))
    spots = []
    for shift in (0, 1):
        where = [jax.random.randint(jax.random.fold_in(own_key, axis), (), 0, length) for axis, length in enumerate(array.shape)]
        where[longest] = (where[longest] + shift) % array.shape[longest]
        spots.append(tuple(where))
    return array.at[spots[0]].set(smallest).at[spots[1]].set(high)


def shard_levels(rng, extent, pieces, least, high):
    level, own = 1.0, jax.random.fold_in(rng, 6)
    for axis_at, parts in pieces:
        heights = jnp.exp(jax.random.uniform(jax.random.fold_in(own, axis_at), (parts,), jnp.float32, least / len(pieces), high / len(pieces)))
        level = level * jnp.repeat(heights, extent[axis_at] // parts).reshape([-1 if axis == axis_at else 1 for axis in range(len(extent))])
    return level


def shared_out(own_key, own, number, rows, number_of, top, bound, lean):
    order = jax.random.permutation(own_key, number_of)
    crowded, common = portions_of(number_of, rows * top, bound, lean, True), portions_of(number_of, rows * top, bound, lean, False)
    places = jnp.arange(number_of)

    def named(lengths, rotation):
        used = int((lengths > 0).sum())
        fixed = max(1, used // 4)
        passed = fixed + (places - fixed + rotation * (used - fixed)) % max(1, number_of - fixed)
        return jnp.zeros((number_of,), jnp.int32).at[order[jnp.where(places < fixed, places, passed)]].set(jnp.asarray(lengths, jnp.int32))

    lengths = jnp.where(number % 4 == 0, named(crowded, number // 4), named(common, number - number // 4 - 1))
    mixed = jax.random.permutation(jax.random.fold_in(own, 3), number_of)
    giver, taker = mixed[0:number_of // 2 * 2:2], mixed[1:number_of // 2 * 2:2]
    margin = jnp.minimum(lengths[giver] - 1, bound - lengths[taker]) // 2
    margin = jnp.where((giver == order[0]) | (taker == order[0]) | (lengths[taker] == 0), 0, jnp.maximum(margin, 0))
    passed = jax.random.randint(jax.random.fold_in(own, 4), (number_of // 2,), 0, 1 << 20) % (margin + 1)
    lengths = lengths.at[giver].add(-passed).at[taker].add(passed)
    items = jnp.searchsorted(jnp.cumsum(lengths), jnp.arange(rows * top), side="right").astype(jnp.int32)
    table = items.reshape(top, rows).T
    table = table[jax.random.permutation(jax.random.fold_in(own, 1), rows)]
    rotation = jax.random.randint(jax.random.fold_in(own, 2), (rows, 1), 0, top)
    return jnp.take_along_axis(table, (jnp.arange(top)[None, :] + rotation) % top, axis=1)


def portions_of(amount, total, most, skew, full):
    weights = [(1 << 20) // math.isqrt(grade ** skew) + 1 for grade in range(1, amount + 1)]
    largest = most if full else min(most, max(-(-total // amount), total * weights[0] // sum(weights)))
    least = 1 if total - largest >= amount - 1 else 0
    holding, spare = [largest] + [least] * (amount - 1), total - largest - least * (amount - 1)
    while spare > 0:
        free = [i for i in range(1, amount) if holding[i] < largest] or [i for i in range(1, amount) if holding[i] < most]
        whole, left = sum([weights[i] for i in free]), spare
        for i in free:
            more = min(most - holding[i], max(1, left * weights[i] // whole), spare)
            holding[i] = holding[i] + more
            spare = spare - more
    return np.array(holding)


def gaussian(own_key, extent, deviation, limit, shards=(), kind=jnp.bfloat16):
    drawn = deviation * jax.random.normal(own_key, extent, jnp.float32)
    if shards:
        drawn = drawn * shard_levels(own_key, extent, shards, -0.22, 0.18)
    return jnp.clip(drawn, -limit, limit).astype(kind)


def setup_inputs(seed: int = 0) -> dict:
    splits = jax.random.split(jax.random.key(seed), 14)
    tokens = gaussian(splits[0], (TOKENS, D), 0.5, 3.0, ((0, 8), (1, 4)))
    ln1_gain = jnp.clip(1.0 + 0.1 * jax.random.normal(splits[1], (D,), jnp.float32), 0.5, 1.5)
    ln1_bias = gaussian(splits[2], (D,), 0.3, 1.5, ((0, 4),), jnp.float32)
    qkv_weight = gaussian(splits[3], (D, 3 * D), D ** -0.5, 0.25, ((0, 4), (1, 8)))
    out_weight = gaussian(splits[4], (D, D), (D * 16 // SEQ) ** -0.5, 1.0, ((0, 4), (1, 8)))
    ln2_gain = jnp.clip(1.0 + 0.1 * jax.random.normal(splits[5], (D,), jnp.float32), 0.5, 1.5)
    ln2_bias = gaussian(splits[6], (D,), 0.3, 1.5, ((0, 4),), jnp.float32)
    router_weight = gaussian(splits[7], (D, E), (D * 2) ** -0.5, 0.1875, ((0, 4),))
    expert_in = gaussian(splits[8], (E, D, HID), D ** -0.5, 0.25, ((1, 4), (2, 8)))
    expert_out = gaussian(splits[9], (E, HID, D), (HID * 4 // (E * E)) ** -0.5, 2.0, ((1, 4), (2, 8)))
    routes_keys = jax.random.split(jax.random.fold_in(splits[10], 1), TOKENS // BLOCK_TOK)
    routes_turns = jax.random.permutation(jax.random.fold_in(splits[10], 3), TOKENS // BLOCK_TOK)
    routes = jax.vmap(lambda own, number: shared_out(jax.random.fold_in(splits[10], 2), own, number, BLOCK_TOK, E, 2, CAP, 1))(routes_keys, routes_turns).reshape((TOKENS, 2))
    keep = touch_ends((jax.random.randint(splits[11], (TOKENS, 2), 0, 8) < 7).astype(jnp.int32), jax.random.fold_in(splits[11], 1), 0, 1)
    cotangent = gaussian(splits[12], (TOKENS, D), 1.0, 6.0, ((0, 8), (1, 4)))
    return dict(tokens=tokens, ln1_gain=ln1_gain, ln1_bias=ln1_bias, qkv_weight=qkv_weight, out_weight=out_weight, ln2_gain=ln2_gain, ln2_bias=ln2_bias, router_weight=router_weight, expert_in=expert_in, expert_out=expert_out, routes=routes, keep=keep, cotangent=cotangent)


@jax.custom_vjp
def low(v):
    return lax.optimization_barrier(v.astype(jnp.bfloat16)).astype(jnp.float32)

@jax.custom_vjp
def low_back(v):
    return v

def low_keep(v):
    return (low(v), None)

def low_pass(kept, grad):
    return (grad,)

def back_keep(v):
    return (v, None)

def back_low(kept, grad):
    return (low(grad),)
low.defvjp(low_keep, low_pass)
low_back.defvjp(back_keep, back_low)
HIGHEST = lax.Precision.HIGHEST
EPS_NORM = 1e-06

def layer_norm(values, ln_gain, ln_bias):
    average = lax.optimization_barrier(jnp.mean(values, axis=-1, keepdims=True))
    centred = values - average
    variance = lax.optimization_barrier(jnp.mean(centred * centred, axis=-1, keepdims=True))
    return centred * lax.rsqrt(variance + EPS_NORM) * ln_gain + ln_bias

def softmax_last(scores):
    top_value = lax.optimization_barrier(jnp.max(scores, axis=-1, keepdims=True))
    powers = jnp.exp(scores - top_value)
    return powers / lax.optimization_barrier(jnp.sum(powers, axis=-1, keepdims=True))

def slot_tables(route_block, keep_block):
    pair_ids = route_block.reshape(-1).astype(jnp.int32)
    pair_count = pair_ids.shape[0]
    onehot = (pair_ids[:, None] == jnp.arange(E, dtype=jnp.int32)[None, :]).astype(jnp.int32)
    running = jnp.cumsum(onehot, axis=0)
    slot_of_pair = (pair_ids * CAP + lax.optimization_barrier(jnp.sum(running * onehot, axis=1)) - 1).astype(jnp.int32)
    pair_of_slot = jnp.full((E * CAP,), pair_count, jnp.int32).at[slot_of_pair].set(jnp.arange(pair_count, dtype=jnp.int32))
    keep_ext = jnp.concatenate([keep_block.reshape(-1).astype(jnp.int32), jnp.zeros((1,), jnp.int32)])
    slot_keep = keep_ext[pair_of_slot]
    token_of_slot = jnp.minimum(pair_of_slot // 2, pair_count // 2 - 1).astype(jnp.int32)
    return (slot_of_pair, pair_of_slot, slot_keep, token_of_slot)

def block_forward(tok_block, ln1_gain, ln1_bias, qkv_weight, out_weight, ln2_gain, ln2_bias, router_weight, expert_in, expert_out, tables, keep_block, route_block):
    slot_of_pair, pair_of_slot, slot_keep, token_of_slot = tables
    normed1 = low(layer_norm(tok_block, ln1_gain, ln1_bias))
    project = low_back(low(jnp.dot(normed1, qkv_weight, precision=HIGHEST)))
    project = project.reshape(IMG, SEQ, 3, HEADS, HD)
    queries = project[:, :, 0]
    keys_all = project[:, :, 1]
    values_all = project[:, :, 2]
    score_scale = HD ** (-0.5)
    scores = low_back(jnp.einsum('bqhd,bkhd->bhqk', queries, keys_all, precision=HIGHEST) * score_scale)
    attn_probs = low(softmax_last(scores))
    attended = jnp.einsum('bhqk,bkhd->bqhd', attn_probs, values_all, precision=HIGHEST)
    attended = low_back(low(attended)).reshape(BLOCK_TOK, D)
    attn_out = low_back(jnp.dot(attended, out_weight, precision=HIGHEST))
    residual = tok_block + attn_out
    normed2 = low(layer_norm(residual, ln2_gain, ln2_bias))
    logits = low_back(jnp.dot(normed2, router_weight, precision=HIGHEST))
    gate_probs = softmax_last(logits)
    onehot = (route_block[:, :, None] == jnp.arange(E, dtype=jnp.int32)[None, None, :]).astype(jnp.float32)
    chosen = lax.optimization_barrier(jnp.sum(onehot * gate_probs[:, None, :], axis=2)) * keep_block.astype(jnp.float32)
    dispatched = normed2[token_of_slot] * slot_keep.astype(jnp.float32)[:, None]
    pre_act = low_back(jnp.einsum('ecd,edh->ech', dispatched.reshape(E, CAP, D), expert_in, precision=HIGHEST))
    activated = low(jax.nn.gelu(pre_act, approximate=False))
    expert_res = low_back(jnp.einsum('ech,ehd->ecd', activated, expert_out, precision=HIGHEST)).reshape(E * CAP, D)
    picked = expert_res[slot_of_pair].reshape(BLOCK_TOK, 2, D)
    return residual + lax.optimization_barrier(jnp.sum(chosen[:, :, None] * picked, axis=1))

def reference(tokens, ln1_gain, ln1_bias, qkv_weight, out_weight, ln2_gain, ln2_bias, router_weight, expert_in, expert_out, routes, keep, cotangent):
    params = tuple((weight_arr.astype(jnp.float32) for weight_arr in (ln1_gain, ln1_bias, qkv_weight, out_weight, ln2_gain, ln2_bias, router_weight, expert_in, expert_out)))
    tok_blocks = tokens.reshape(-1, BLOCK_TOK, D)
    cot_blocks = cotangent.reshape(-1, BLOCK_TOK, D)
    route_blocks = routes.reshape(-1, BLOCK_TOK, 2)
    keep_blocks = keep.reshape(-1, BLOCK_TOK, 2)

    def one_block(totals, block_items):
        tok_block, cot_block, route_block, keep_block = block_items
        tables = slot_tables(route_block, keep_block)

        def forward(tok_arg, *weights):
            return block_forward(tok_arg, *weights, tables, keep_block, route_block)
        result, backward = jax.vjp(jax.checkpoint(forward), tok_block.astype(jnp.float32), *params)
        all_grads = backward(cot_block.astype(jnp.float32))
        totals = tuple((running_total + one_grad for running_total, one_grad in zip(totals, all_grads[1:])))
        return (totals, (result.astype(jnp.bfloat16), all_grads[0]))
    initial = tuple((jnp.zeros(weight_arr.shape, jnp.float32) for weight_arr in params))
    totals, (outputs, tok_grads) = lax.scan(one_block, initial, (tok_blocks, cot_blocks, route_blocks, keep_blocks))
    return (outputs.reshape(TOKENS, D), tok_grads.reshape(TOKENS, D), totals[0], totals[1], totals[2], totals[3], totals[4], totals[5], totals[6], totals[7], totals[8])
```

```python
from functools import partial

import jax
import jax.numpy as jnp
from jax import lax
from jax.sharding import PartitionSpec as P

E = 32
SEQ = 197
HD = 64
CAP = 120
EPS_NORM = 1e-06
F32 = jnp.float32
BF16 = jnp.bfloat16


def dot(a, b, dims):
    return lax.dot_general(a, b, (dims, ((), ())), preferred_element_type=F32)


def col_groups():
    rows, cols = lax.axis_size("row"), lax.axis_size("col")
    near = E // rows
    return cols // near, near


def exchange(pieces):
    groups, near = col_groups()
    if groups == 1:
        return lax.all_to_all(pieces, ("row", "col"), 0, 0, tiled=True)
    rows = lax.axis_size("row")
    index = [[g * near + c for c in range(near)] for g in range(groups)]
    parts = pieces.reshape((rows, near) + pieces.shape[1:])
    parts = lax.all_to_all(parts, "row", 0, 0, tiled=True)
    parts = lax.all_to_all(parts, "col", 1, 1, tiled=True, axis_index_groups=index)
    return parts.reshape(pieces.shape)


def far_groups():
    groups, near = col_groups()
    return [[g * near + c for g in range(groups)] for c in range(near)]


def collect_far(x):
    if col_groups()[0] == 1:
        return x[None]
    return lax.all_gather(x, "col", axis=0, axis_index_groups=far_groups())


def reduce_far(x):
    if col_groups()[0] == 1:
        return x[0]
    return lax.psum_scatter(x, "col", scatter_dimension=0, axis_index_groups=far_groups())


def spread(x, axis, groups=None):
    n = len(groups[0]) if groups else lax.axis_size(axis)
    return lax.all_to_all(
        jnp.broadcast_to(x[None], (n,) + x.shape), axis, 0, 0, tiled=True, axis_index_groups=groups
    )


def gather_all(x):
    half = lax.axis_size("col") // 2
    far = spread(x, "col", [[2 * i + k for i in range(half)] for k in range(2)])
    mine = spread(far, "row")
    swap = [(i, i ^ 1) for i in range(2 * half)]
    other = lax.ppermute(mine, "col", swap)
    first = lax.axis_index("col") % 2 == 0
    both = jnp.stack([jnp.where(first, mine, other), jnp.where(first, other, mine)], axis=2)
    return both.reshape((both.shape[0], 2 * half) + x.shape)


def to_tokens(x):
    rows = lax.axis_size("row")
    t, w = x.shape
    y = lax.all_to_all(x.reshape(rows, t // rows, w), "row", 0, 0, tiled=True)
    return y.transpose(1, 0, 2).reshape(t // rows, rows * w)


def to_features(x):
    rows = lax.axis_size("row")
    t, w = x.shape
    y = x.reshape(t, rows, w // rows).transpose(1, 0, 2)
    return lax.all_to_all(y, "row", 0, 0, tiled=True).reshape(t * rows, w // rows)


def normalize(values):
    average = jnp.mean(values, axis=1, keepdims=True)
    centred = values - average
    inverse = lax.rsqrt(jnp.mean(centred * centred, axis=1, keepdims=True) + EPS_NORM)
    return centred * inverse, inverse


def norm_backward(grad_normed, normalized, inverse, gain):
    scaled = grad_normed * gain
    plain = jnp.mean(scaled, axis=1, keepdims=True)
    cross = jnp.mean(scaled * normalized, axis=1, keepdims=True)
    return inverse * (scaled - plain - normalized * cross)


def softmax_last(scores):
    top_value = jnp.max(scores, axis=-1, keepdims=True)
    powers = jnp.exp(scores - top_value)
    return powers / jnp.sum(powers, axis=-1, keepdims=True)


def slot_table(routes, keep):
    t = routes.shape[0]
    experts = jnp.arange(E, dtype=jnp.int32)
    onehot = routes[:, :, None] == experts[None, None, :]
    named = jnp.any(onehot, axis=1).astype(BF16)
    steps = jnp.arange(t, dtype=jnp.int32)
    earlier = (steps[None, :] < steps[:, None]).astype(BF16)
    counts = dot(earlier, named, ((1,), (0,))).astype(jnp.int32)
    place = jnp.sum(jnp.where(onehot, counts[:, None, :], 0), axis=2)
    return jnp.where(keep != 0, routes * CAP + place, -1)


def local(
    tokens,
    ln1_gain,
    ln1_bias,
    qkv_weight,
    out_weight,
    ln2_gain,
    ln2_bias,
    router_weight,
    expert_in,
    expert_out,
    routes,
    keep,
    cotangent,
):
    rows, cols = lax.axis_size("row"), lax.axis_size("col")
    groups, near = col_groups()
    block_tok, width_part = tokens.shape
    width = width_part * rows
    heads = width // HD
    mine = block_tok // rows
    images = mine // SEQ
    hid_part = expert_in.shape[2]
    hid = hid_part * cols
    out_part = expert_out.shape[2]
    qkv_part, mix_part = qkv_weight.shape[1], out_weight.shape[1]
    score_scale = HD ** (-0.5)

    slots = slot_table(routes, keep)
    hits = jnp.any(
        slots[:, :, None] == jnp.arange(E * CAP, dtype=jnp.int32)[None, None, :], axis=1
    ).astype(BF16)

    small = gather_all(jnp.concatenate([qkv_weight.T, out_weight.T], axis=0))
    qkv_t = small[:, :, :qkv_part].transpose(1, 2, 0, 3).reshape(3 * width, width)
    mix_t = small[:, :, qkv_part:].transpose(1, 2, 0, 3).reshape(width, width)
    norms = spread(jnp.stack([ln1_gain, ln1_bias, ln2_gain, ln2_bias]), "row")
    norms = norms.transpose(1, 0, 2).reshape(4, width)
    router_t = spread(router_weight.T, "row").transpose(1, 0, 2).reshape(E, width)
    w_in = exchange(expert_in).reshape(rows, near, width_part, hid_part)
    w_in = collect_far(w_in).transpose(1, 3, 0, 2, 4).reshape(width, hid)
    w_out_t = exchange(expert_out.transpose(0, 2, 1)).reshape(rows, near, out_part, hid // rows)
    w_out_t = collect_far(w_out_t).transpose(0, 2, 3, 1, 4).reshape(width, hid)

    def dispatch(values):
        picked = dot(hits, values, ((0,), (0,))).astype(BF16)
        got = exchange(picked.reshape(E, CAP, width_part))
        got = got.reshape(rows, near, CAP, width_part).transpose(1, 2, 0, 3)
        return got.reshape(near * CAP, width)

    def combine(values):
        sent = values.astype(BF16).reshape(near, CAP, rows, width_part).transpose(2, 0, 1, 3)
        got = exchange(sent.reshape(E, CAP, width_part))
        return dot(hits, got.reshape(E * CAP, width_part), ((1,), (0,)))

    cot_rows = dispatch(cotangent).astype(F32)
    tok_float = to_tokens(tokens).astype(F32)
    grad_out = to_tokens(cotangent).astype(F32)

    normal1, inverse1 = normalize(tok_float)
    normed1 = (normal1 * norms[0] + norms[1]).astype(BF16)
    project = dot(normed1, qkv_t, ((1,), (1,))).astype(BF16)
    split_heads = project.reshape(images, SEQ, 3, heads, HD)
    queries, keys_all, values_all = (split_heads[:, :, i] for i in range(3))
    scores = score_scale * jnp.einsum(
        "bqhd,bkhd->bhqk", queries, keys_all, preferred_element_type=F32
    )
    float_probs = softmax_last(scores)
    attn_probs = float_probs.astype(BF16)
    attended = jnp.einsum("bhqk,bkhd->bqhd", attn_probs, values_all, preferred_element_type=F32)
    attended = attended.reshape(mine, width).astype(BF16)
    attn_out = dot(attended, mix_t, ((1,), (1,)))
    residual = tok_float + attn_out
    normal2, inverse2 = normalize(residual)
    normed2 = (normal2 * norms[2] + norms[3]).astype(BF16)
    attn_part = to_features(attn_out.astype(BF16))

    x_rows = dispatch(to_features(normed2))
    flat = lax.axis_index("row") * near + lax.axis_index("col") % near
    gates = softmax_last(dot(x_rows, router_t, ((1,), (1,))))
    own = (jnp.arange(E) == flat).astype(F32)[None, :]
    chosen = jnp.sum(gates * own, axis=1, keepdims=True)
    pre_act = dot(x_rows, w_in, ((1,), (0,)))
    activated, gelu_back = jax.vjp(partial(jax.nn.gelu, approximate=False), pre_act)
    activated = activated.astype(BF16)
    expert_res = dot(activated, w_out_t, ((1,), (1,)))
    grad_chosen = jnp.sum(cot_rows * expert_res, axis=1, keepdims=True)
    grad_logits = (grad_chosen * chosen * (own - gates)).astype(BF16)
    grad_res = (chosen * cot_rows).astype(BF16)
    grad_act = dot(grad_res, w_out_t, ((1,), (0,)))
    (grad_pre,) = gelu_back(grad_act)
    grad_pre = grad_pre.astype(BF16)
    grad_rows = dot(grad_pre, w_in, ((1,), (1,))) + dot(grad_logits, router_t, ((1,), (0,)))
    grad_norm2 = to_tokens(combine(grad_rows).astype(BF16)).astype(F32)
    moved = combine(chosen * expert_res)
    layer_out = (tokens.astype(F32) + attn_part.astype(F32) + moved).astype(BF16)
    router_part = dot(grad_logits, x_rows, ((0,), (0,)))
    out_grad_t = dot(grad_res, activated, ((0,), (0,))).astype(BF16)
    in_grad = dot(x_rows, grad_pre, ((0,), (0,))).astype(BF16)
    out_grad_t = out_grad_t.reshape(groups, near, out_part, rows, hid // rows).transpose(0, 3, 1, 2, 4)
    out_grad_t = exchange(reduce_far(out_grad_t).reshape(E, out_part, hid // rows))
    in_grad = in_grad.reshape(rows, width_part, groups, near, hid_part).transpose(2, 0, 3, 1, 4)
    in_grad = exchange(reduce_far(in_grad).reshape(E, width_part, hid_part))
    expert_out_grad = out_grad_t.astype(F32).transpose(0, 2, 1)
    expert_in_grad = in_grad.astype(F32)

    gain2_part = jnp.sum(grad_norm2 * normal2, axis=0)
    bias2_part = jnp.sum(grad_norm2, axis=0)
    grad_resid = grad_out + norm_backward(grad_norm2, normal2, inverse2, norms[2])
    grad_attn = grad_resid.astype(BF16)
    mix_grad_t = dot(grad_attn, attended, ((0,), (0,)))
    grad_heads = dot(grad_attn, mix_t, ((1,), (0,))).astype(BF16).reshape(images, SEQ, heads, HD)
    grad_values = jnp.einsum(
        "bhqk,bqhd->bkhd", attn_probs, grad_heads, preferred_element_type=F32
    )
    grad_probs = jnp.einsum("bqhd,bkhd->bhqk", grad_heads, values_all, preferred_element_type=F32)
    row_dot = jnp.sum(float_probs * grad_probs, axis=-1, keepdims=True)
    grad_scores = (float_probs * (grad_probs - row_dot)).astype(BF16)
    grad_queries = score_scale * jnp.einsum(
        "bhqk,bkhd->bqhd", grad_scores, keys_all, preferred_element_type=F32
    )
    grad_keys = score_scale * jnp.einsum(
        "bhqk,bqhd->bkhd", grad_scores, queries, preferred_element_type=F32
    )
    grad_project = jnp.stack([grad_queries, grad_keys, grad_values], axis=2)
    grad_project = grad_project.reshape(mine, 3 * width).astype(BF16)
    qkv_grad_t = dot(grad_project, normed1, ((0,), (0,)))
    grad_norm1 = dot(grad_project, qkv_t, ((1,), (0,)))
    gain1_part = jnp.sum(grad_norm1 * normal1, axis=0)
    bias1_part = jnp.sum(grad_norm1, axis=0)
    tokens_grad = grad_resid + norm_backward(grad_norm1, normal1, inverse1, norms[0])
    tokens_grad = to_features(tokens_grad.astype(BF16)).astype(F32)

    shares = jnp.concatenate(
        [
            qkv_grad_t.reshape(cols, qkv_part, width),
            mix_grad_t.reshape(cols, mix_part, width),
            jnp.broadcast_to(router_part[None], (cols, E, width)),
            jnp.broadcast_to(
                jnp.stack([gain1_part, bias1_part, gain2_part, bias2_part])[None], (cols, 4, width)
            ),
        ],
        axis=1,
    ).astype(BF16)
    depth = shares.shape[1]
    shares = shares.reshape(cols, depth, rows, width_part).transpose(2, 0, 1, 3)
    shares = shares.reshape(rows * cols, depth, width_part)
    shares = lax.all_to_all(shares, ("row", "col"), 0, 0, tiled=True)
    sums = jnp.sum(shares.astype(F32), axis=0)
    thin = width_part // cols
    tail = lax.dynamic_slice_in_dim(
        sums[qkv_part + mix_part :], lax.axis_index("col") * thin, thin, axis=1
    )
    return (
        layer_out,
        tokens_grad,
        tail[E],
        tail[E + 1],
        sums[:qkv_part].T,
        sums[qkv_part : qkv_part + mix_part].T,
        tail[E + 2],
        tail[E + 3],
        tail[:E].T,
        expert_in_grad,
        expert_out_grad,
    )


def solution(mesh):
    in_specs = (
        P("col", "row"),
        P("row"),
        P("row"),
        P("row", "col"),
        P("row", "col"),
        P("row"),
        P("row"),
        P("row", None),
        P(None, "row", "col"),
        P(None, "row", "col"),
        P("col", None),
        P("col", None),
        P("col", "row"),
    )
    out_specs = (
        P("col", "row"),
        P("col", "row"),
        P(("row", "col")),
        P(("row", "col")),
        P("row", "col"),
        P("row", "col"),
        P(("row", "col")),
        P(("row", "col")),
        P(("row", "col"), None),
        P(None, "row", "col"),
        P(None, "row", "col"),
    )
    return jax.shard_map(local, mesh=mesh, in_specs=in_specs, out_specs=out_specs, check_vma=False)
```

```python
from functools import partial

import jax
import jax.numpy as jnp
from jax import lax
from jax.sharding import PartitionSpec as P

E = 32
SEQ = 197
HD = 64
CAP = 120
EPS_NORM = 1e-06
F32 = jnp.float32
BF16 = jnp.bfloat16


def dot(a, b, dims):
    return lax.dot_general(a, b, (dims, ((), ())), preferred_element_type=F32)


def col_groups():
    rows, cols = lax.axis_size("row"), lax.axis_size("col")
    near = E // rows
    return cols // near, near


def exchange(pieces):
    groups, near = col_groups()
    if groups == 1:
        return lax.all_to_all(pieces, ("row", "col"), 0, 0, tiled=True)
    rows = lax.axis_size("row")
    index = [[g * near + c for c in range(near)] for g in range(groups)]
    parts = pieces.reshape((rows, near) + pieces.shape[1:])
    parts = lax.all_to_all(parts, "row", 0, 0, tiled=True)
    parts = lax.all_to_all(parts, "col", 1, 1, tiled=True, axis_index_groups=index)
    return parts.reshape(pieces.shape)


def far_groups():
    groups, near = col_groups()
    return [[g * near + c for g in range(groups)] for c in range(near)]


def collect_far(x):
    if col_groups()[0] == 1:
        return x[None]
    return lax.all_gather(x, "col", axis=0, axis_index_groups=far_groups())


def reduce_far(x):
    if col_groups()[0] == 1:
        return x[0]
    return lax.psum_scatter(x, "col", scatter_dimension=0, axis_index_groups=far_groups())


def after(x, *earlier):
    return lax.optimization_barrier((x,) + earlier)[0]


def swaps(axis, distance):
    return [(i, i ^ distance) for i in range(lax.axis_size(axis))]


def pick(pieces, at):
    return lax.dynamic_index_in_dim(pieces, at, 0, keepdims=False)


def in_order(got, here):
    pieces, step = list(got), 1
    while step < len(pieces):
        odd = (here & step) != 0
        pieces = [jnp.where(odd, pieces[k ^ step], pieces[k]) for k in range(len(pieces))]
        step *= 2
    return pieces


def row_exchange(pieces):
    here = lax.axis_index("row")
    got = [pick(pieces, here)]
    for k in range(1, lax.axis_size("row")):
        got.append(lax.ppermute(pick(pieces, here ^ k), "row", swaps("row", k)))
    return in_order(got, here)


def row_spread(x):
    got = [x] + [lax.ppermute(x, "row", swaps("row", k)) for k in range(1, lax.axis_size("row"))]
    return jnp.stack(in_order(got, lax.axis_index("row")))


def parity_groups():
    cols = lax.axis_size("col")
    return [[2 * i + k for i in range(cols // 2)] for k in range(2)]


def far_spread(x):
    half = lax.axis_size("col") // 2
    if half > 8:
        return lax.all_gather(x, "col", axis=0, axis_index_groups=parity_groups())
    got = [x] + [lax.ppermute(x, "col", swaps("col", 2 * k)) for k in range(1, half)]
    return jnp.stack(in_order(got, lax.axis_index("col") // 2))


def far_sum(pieces):
    half = lax.axis_size("col") // 2
    if half > 8:
        got = lax.all_to_all(pieces, "col", 0, 0, tiled=True, axis_index_groups=parity_groups())
        return jnp.sum(got.astype(F32), axis=0)
    here = lax.axis_index("col") // 2
    total = pick(pieces, here).astype(F32)
    for k in range(1, half):
        sent = lax.ppermute(pick(pieces, here ^ k), "col", swaps("col", 2 * k))
        total = total + sent.astype(F32)
    return total


def gather_all(x):
    half = lax.axis_size("col") // 2
    mine = row_spread(far_spread(x))
    other = lax.ppermute(mine, "col", swaps("col", 1))
    first = lax.axis_index("col") % 2 == 0
    both = jnp.stack([jnp.where(first, mine, other), jnp.where(first, other, mine)], axis=2)
    return both.reshape((both.shape[0], 2 * half) + x.shape)


def reduce_all(x):
    cols, n, width = x.shape
    rows = lax.axis_size("row")
    core = lax.axis_index("col") % 2
    pairs = x.reshape(cols // 2, 2, n, width).transpose(1, 0, 2, 3).astype(BF16)
    sent = lax.ppermute(pick(pairs, 1 - core), "col", swaps("col", 1))
    mine = pick(pairs, core).astype(F32) + sent.astype(F32)
    mine = mine.astype(BF16).reshape(cols // 2, n, rows, width // rows).transpose(2, 0, 1, 3)
    mine = sum(piece.astype(F32) for piece in row_exchange(mine))
    return far_sum(mine.astype(BF16))


def pack_in(x, chunks):
    e, n, h = x.shape
    return x.reshape(e, chunks, n // chunks, h).transpose(0, 2, 1, 3).reshape(e, n // chunks, -1)


def unpack_in(x, chunks):
    e, n, h = x.shape
    x = x.reshape(e, n, chunks, h // chunks).transpose(0, 2, 1, 3)
    return x.reshape(e, n * chunks, h // chunks)


def to_tokens(x):
    rows = lax.axis_size("row")
    t, w = x.shape
    return jnp.concatenate(row_exchange(x.reshape(rows, t // rows, w)), axis=1)


def to_features(x):
    rows = lax.axis_size("row")
    t, w = x.shape
    y = x.reshape(t, rows, w // rows).transpose(1, 0, 2)
    return jnp.concatenate(row_exchange(y), axis=0)


def normalize(values):
    average = jnp.mean(values, axis=1, keepdims=True)
    centred = values - average
    inverse = lax.rsqrt(jnp.mean(centred * centred, axis=1, keepdims=True) + EPS_NORM)
    return centred * inverse, inverse


def norm_backward(grad_normed, normalized, inverse, gain):
    scaled = grad_normed * gain
    plain = jnp.mean(scaled, axis=1, keepdims=True)
    cross = jnp.mean(scaled * normalized, axis=1, keepdims=True)
    return inverse * (scaled - plain - normalized * cross)


def softmax_last(scores):
    top_value = jnp.max(scores, axis=-1, keepdims=True)
    powers = jnp.exp(scores - top_value)
    return powers / jnp.sum(powers, axis=-1, keepdims=True)


def slot_table(routes, keep):
    t = routes.shape[0]
    experts = jnp.arange(E, dtype=jnp.int32)
    onehot = routes[:, :, None] == experts[None, None, :]
    named = jnp.any(onehot, axis=1).astype(BF16)
    steps = jnp.arange(t, dtype=jnp.int32)
    earlier = (steps[None, :] < steps[:, None]).astype(BF16)
    counts = dot(earlier, named, ((1,), (0,))).astype(jnp.int32)
    place = jnp.sum(jnp.where(onehot, counts[:, None, :], 0), axis=2)
    return jnp.where(keep != 0, routes * CAP + place, -1)


def local(
    tokens,
    ln1_gain,
    ln1_bias,
    qkv_weight,
    out_weight,
    ln2_gain,
    ln2_bias,
    router_weight,
    expert_in,
    expert_out,
    routes,
    keep,
    cotangent,
):
    rows, cols = lax.axis_size("row"), lax.axis_size("col")
    groups, near = col_groups()
    block_tok, width_part = tokens.shape
    width = width_part * rows
    heads = width // HD
    mine = block_tok // rows
    images = mine // SEQ
    hid_part = expert_in.shape[2]
    hid = hid_part * cols
    out_part = expert_out.shape[2]
    qkv_part, mix_part = qkv_weight.shape[1], out_weight.shape[1]
    score_scale = HD ** (-0.5)

    slots = slot_table(routes, keep)
    hits = jnp.any(
        slots[:, :, None] == jnp.arange(E * CAP, dtype=jnp.int32)[None, None, :], axis=1
    ).astype(BF16)

    small = gather_all(jnp.concatenate([qkv_weight.T, out_weight.T], axis=0))
    qkv_t = small[:, :, :qkv_part].transpose(1, 2, 0, 3).reshape(3 * width, width)
    mix_t = small[:, :, qkv_part:].transpose(1, 2, 0, 3).reshape(width, width)
    norms = row_spread(jnp.stack([ln1_gain, ln1_bias, ln2_gain, ln2_bias]))
    norms = norms.transpose(1, 0, 2).reshape(4, width)
    router_t = row_spread(router_weight.T).transpose(1, 0, 2).reshape(E, width)
    chunks = width_part // out_part
    w_sent = jnp.concatenate([pack_in(expert_in, chunks), expert_out.transpose(0, 2, 1)], axis=1)
    w_got = exchange(w_sent)
    w_in = unpack_in(w_got[:, :out_part], chunks).reshape(rows, near, width_part, hid_part)
    w_in = collect_far(w_in).transpose(1, 3, 0, 2, 4).reshape(width, hid)
    w_out_t = w_got[:, out_part:].reshape(rows, near, out_part, hid // rows)
    w_out_t = collect_far(w_out_t).transpose(0, 2, 3, 1, 4).reshape(width, hid)

    def to_slots(values):
        return dot(hits, values, ((0,), (0,))).astype(BF16).reshape(E, CAP, width_part)

    def to_rows(got):
        got = got.reshape(rows, near, CAP, width_part).transpose(1, 2, 0, 3)
        return got.reshape(near * CAP, width)

    def from_rows(values):
        sent = values.astype(BF16).reshape(near, CAP, rows, width_part).transpose(2, 0, 1, 3)
        return sent.reshape(E, CAP, width_part)

    def from_slots(got):
        return dot(hits, got.reshape(E * CAP, width_part), ((1,), (0,)))

    cot_sent = to_slots(cotangent)
    tok_float = to_tokens(tokens).astype(F32)
    grad_out = to_tokens(cotangent).astype(F32)

    normal1, inverse1 = normalize(tok_float)
    normed1 = (normal1 * norms[0] + norms[1]).astype(BF16)
    project = dot(normed1, qkv_t, ((1,), (1,))).astype(BF16)
    split_heads = project.reshape(images, SEQ, 3, heads, HD)
    queries, keys_all, values_all = (split_heads[:, :, i] for i in range(3))
    scores = score_scale * jnp.einsum(
        "bqhd,bkhd->bhqk", queries, keys_all, preferred_element_type=F32
    )
    float_probs = softmax_last(scores)
    attn_probs = float_probs.astype(BF16)
    attended = jnp.einsum("bhqk,bkhd->bqhd", attn_probs, values_all, preferred_element_type=F32)
    attended = attended.reshape(mine, width).astype(BF16)
    attn_out = dot(attended, mix_t, ((1,), (1,)))
    residual = tok_float + attn_out
    normal2, inverse2 = normalize(residual)
    normed2 = (normal2 * norms[2] + norms[3]).astype(BF16)
    attn_part = to_features(attn_out.astype(BF16))

    x_got = exchange(after(to_slots(to_features(normed2)), w_got))
    x_rows = to_rows(x_got)
    cot_got = exchange(after(cot_sent, x_got))
    cot_rows = to_rows(cot_got).astype(F32)
    flat = lax.axis_index("row") * near + lax.axis_index("col") % near
    gates = softmax_last(dot(x_rows, router_t, ((1,), (1,))))
    own = (jnp.arange(E) == flat).astype(F32)[None, :]
    chosen = jnp.sum(gates * own, axis=1, keepdims=True)
    pre_act = dot(x_rows, w_in, ((1,), (0,)))
    activated, gelu_back = jax.vjp(partial(jax.nn.gelu, approximate=False), pre_act)
    activated = activated.astype(BF16)
    expert_res = dot(activated, w_out_t, ((1,), (1,)))
    grad_chosen = jnp.sum(cot_rows * expert_res, axis=1, keepdims=True)
    grad_logits = (grad_chosen * chosen * (own - gates)).astype(BF16)
    grad_res = (chosen * cot_rows).astype(BF16)
    grad_act = dot(grad_res, w_out_t, ((1,), (0,)))
    (grad_pre,) = gelu_back(grad_act)
    grad_pre = grad_pre.astype(BF16)
    grad_rows = dot(grad_pre, w_in, ((1,), (1,))) + dot(grad_logits, router_t, ((1,), (0,)))
    moved_got = exchange(after(from_rows(chosen * expert_res), cot_got))
    grad_got = exchange(after(from_rows(grad_rows), moved_got))
    grad_norm2 = to_tokens(from_slots(grad_got).astype(BF16)).astype(F32)
    layer_out = (tokens.astype(F32) + attn_part.astype(F32) + from_slots(moved_got)).astype(BF16)
    router_part = dot(grad_logits, x_rows, ((0,), (0,)))
    out_grad_t = dot(grad_res, activated, ((0,), (0,))).astype(BF16)
    in_grad = dot(x_rows, grad_pre, ((0,), (0,))).astype(BF16)
    out_grad_t = out_grad_t.reshape(groups, near, out_part, rows, hid // rows)
    out_grad_t = reduce_far(out_grad_t.transpose(0, 3, 1, 2, 4)).reshape(E, out_part, hid // rows)
    in_grad = in_grad.reshape(rows, width_part, groups, near, hid_part).transpose(2, 0, 3, 1, 4)
    in_grad = reduce_far(in_grad).reshape(E, width_part, hid_part)
    w_grads = jnp.concatenate([pack_in(in_grad, chunks), out_grad_t], axis=1)
    w_grads = exchange(after(w_grads, grad_got)).astype(F32)
    expert_out_grad = w_grads[:, out_part:].transpose(0, 2, 1)
    expert_in_grad = unpack_in(w_grads[:, :out_part], chunks)

    gain2_part = jnp.sum(grad_norm2 * normal2, axis=0)
    bias2_part = jnp.sum(grad_norm2, axis=0)
    grad_resid = grad_out + norm_backward(grad_norm2, normal2, inverse2, norms[2])
    grad_attn = grad_resid.astype(BF16)
    mix_grad_t = dot(grad_attn, attended, ((0,), (0,)))
    grad_heads = dot(grad_attn, mix_t, ((1,), (0,))).astype(BF16).reshape(images, SEQ, heads, HD)
    grad_values = jnp.einsum(
        "bhqk,bqhd->bkhd", attn_probs, grad_heads, preferred_element_type=F32
    )
    grad_probs = jnp.einsum("bqhd,bkhd->bhqk", grad_heads, values_all, preferred_element_type=F32)
    row_dot = jnp.sum(float_probs * grad_probs, axis=-1, keepdims=True)
    grad_scores = (float_probs * (grad_probs - row_dot)).astype(BF16)
    grad_queries = score_scale * jnp.einsum(
        "bhqk,bkhd->bqhd", grad_scores, keys_all, preferred_element_type=F32
    )
    grad_keys = score_scale * jnp.einsum(
        "bhqk,bqhd->bkhd", grad_scores, queries, preferred_element_type=F32
    )
    grad_project = jnp.stack([grad_queries, grad_keys, grad_values], axis=2)
    grad_project = grad_project.reshape(mine, 3 * width).astype(BF16)
    qkv_grad_t = dot(grad_project, normed1, ((0,), (0,)))
    grad_norm1 = dot(grad_project, qkv_t, ((1,), (0,)))
    gain1_part = jnp.sum(grad_norm1 * normal1, axis=0)
    bias1_part = jnp.sum(grad_norm1, axis=0)
    tokens_grad = grad_resid + norm_backward(grad_norm1, normal1, inverse1, norms[0])
    tokens_grad = to_features(tokens_grad.astype(BF16)).astype(F32)

    shares = jnp.concatenate(
        [
            qkv_grad_t.reshape(cols, qkv_part, width),
            mix_grad_t.reshape(cols, mix_part, width),
            jnp.broadcast_to(router_part[None], (cols, E, width)),
            jnp.broadcast_to(
                jnp.stack([gain1_part, bias1_part, gain2_part, bias2_part])[None], (cols, 4, width)
            ),
        ],
        axis=1,
    )
    sums = reduce_all(shares)
    thin = width_part // cols
    tail = lax.dynamic_slice_in_dim(
        sums[qkv_part + mix_part :], lax.axis_index("col") * thin, thin, axis=1
    )
    return (
        layer_out,
        tokens_grad,
        tail[E],
        tail[E + 1],
        sums[:qkv_part].T,
        sums[qkv_part : qkv_part + mix_part].T,
        tail[E + 2],
        tail[E + 3],
        tail[:E].T,
        expert_in_grad,
        expert_out_grad,
    )


def solution(mesh):
    in_specs = (
        P("col", "row"),
        P("row"),
        P("row"),
        P("row", "col"),
        P("row", "col"),
        P("row"),
        P("row"),
        P("row", None),
        P(None, "row", "col"),
        P(None, "row", "col"),
        P("col", None),
        P("col", None),
        P("col", "row"),
    )
    out_specs = (
        P("col", "row"),
        P("col", "row"),
        P(("row", "col")),
        P(("row", "col")),
        P("row", "col"),
        P("row", "col"),
        P(("row", "col")),
        P(("row", "col")),
        P(("row", "col"), None),
        P(None, "row", "col"),
        P(None, "row", "col"),
    )
    return jax.shard_map(local, mesh=mesh, in_specs=in_specs, out_specs=out_specs, check_vma=False)
```

```python
import math
from functools import partial

import jax
import jax.numpy as jnp
from jax import lax
from jax.experimental import pallas as pl
from jax.experimental.pallas import tpu as pltpu
from jax.sharding import PartitionSpec as P

E = 32
SEQ = 197
ROWS = 208
HD = 64
CAP = 120
EPS_NORM = 1e-06
VMEM = 60 * 2**20
F32 = jnp.float32
BF16 = jnp.bfloat16

def dot(a, b, dims):
    return lax.dot_general(a, b, (dims, ((), ())), preferred_element_type=F32)


def col_groups():
    rows, cols = lax.axis_size("row"), lax.axis_size("col")
    near = E // rows
    return cols // near, near


def exchange(pieces):
    groups, near = col_groups()
    if groups == 1:
        return lax.all_to_all(pieces, ("row", "col"), 0, 0, tiled=True)
    rows = lax.axis_size("row")
    index = [[g * near + c for c in range(near)] for g in range(groups)]
    parts = pieces.reshape((rows, near) + pieces.shape[1:])
    parts = lax.all_to_all(parts, "row", 0, 0, tiled=True)
    parts = lax.all_to_all(parts, "col", 1, 1, tiled=True, axis_index_groups=index)
    return parts.reshape(pieces.shape)


def far_groups():
    groups, near = col_groups()
    return [[g * near + c for g in range(groups)] for c in range(near)]


def collect_far(x):
    if col_groups()[0] == 1:
        return x[None]
    return lax.all_gather(x, "col", axis=0, axis_index_groups=far_groups())


def reduce_far(x):
    if col_groups()[0] == 1:
        return x[0]
    return lax.psum_scatter(x, "col", scatter_dimension=0, axis_index_groups=far_groups())


def after(x, *earlier):
    return lax.optimization_barrier((x,) + earlier)[0]


def swaps(axis, distance):
    return [(i, i ^ distance) for i in range(lax.axis_size(axis))]


def pick(pieces, at):
    return lax.dynamic_index_in_dim(pieces, at, 0, keepdims=False)


def in_order(got, here):
    pieces, step = list(got), 1
    while step < len(pieces):
        odd = (here & step) != 0
        pieces = [jnp.where(odd, pieces[k ^ step], pieces[k]) for k in range(len(pieces))]
        step *= 2
    return pieces


def row_exchange(pieces):
    here = lax.axis_index("row")
    got = [pick(pieces, here)]
    for k in range(1, lax.axis_size("row")):
        got.append(lax.ppermute(pick(pieces, here ^ k), "row", swaps("row", k)))
    return in_order(got, here)


def row_swap(pieces):
    got = [lax.ppermute(x, "row", swaps("row", k)) for k, x in enumerate(pieces) if k]
    return [pieces[0]] + got


def for_rows(x):
    here = lax.axis_index("row")
    return [pick(x, here ^ k) for k in range(x.shape[0])]


def row_spread(x):
    got = [x] + [lax.ppermute(x, "row", swaps("row", k)) for k in range(1, lax.axis_size("row"))]
    return jnp.stack(in_order(got, lax.axis_index("row")))


def parity_groups():
    cols = lax.axis_size("col")
    return [[2 * i + k for i in range(cols // 2)] for k in range(2)]


def far_spread(x):
    half = lax.axis_size("col") // 2
    if half > 8:
        return lax.all_gather(x, "col", axis=0, axis_index_groups=parity_groups())
    got = [x] + [lax.ppermute(x, "col", swaps("col", 2 * k)) for k in range(1, half)]
    return jnp.stack(in_order(got, lax.axis_index("col") // 2))


def far_sum(pieces):
    half = lax.axis_size("col") // 2
    if half > 8:
        got = lax.all_to_all(pieces, "col", 0, 0, tiled=True, axis_index_groups=parity_groups())
        return jnp.sum(got.astype(F32), axis=0)
    here = lax.axis_index("col") // 2
    total = pick(pieces, here).astype(F32)
    for k in range(1, half):
        sent = lax.ppermute(pick(pieces, here ^ k), "col", swaps("col", 2 * k))
        total = total + sent.astype(F32)
    return total


def gather_all(x):
    half = lax.axis_size("col") // 2
    mine = row_spread(x)
    other = lax.ppermute(mine, "col", swaps("col", 1))
    first = lax.axis_index("col") % 2 == 0
    both = jnp.stack([jnp.where(first, mine, other), jnp.where(first, other, mine)], axis=2)
    return both.reshape((both.shape[0], 2 * half) + x.shape[1:])


def reduce_all(x):
    cols, n, width = x.shape
    rows = lax.axis_size("row")
    core = lax.axis_index("col") % 2
    pairs = x.reshape(cols // 2, 2, n, width).transpose(1, 0, 2, 3).astype(BF16)
    sent = lax.ppermute(pick(pairs, 1 - core), "col", swaps("col", 1))
    mine = pick(pairs, core).astype(F32) + sent.astype(F32)
    mine = mine.astype(BF16).reshape(cols // 2, n, rows, width // rows).transpose(2, 0, 1, 3)
    mine = sum(piece.astype(F32) for piece in row_exchange(mine))
    return far_sum(mine.astype(BF16))


def pack_in(x, chunks):
    e, n, h = x.shape
    return x.reshape(e, chunks, n // chunks, h).transpose(0, 2, 1, 3).reshape(e, n // chunks, -1)


def unpack_in(x, chunks):
    e, n, h = x.shape
    x = x.reshape(e, n, chunks, h // chunks).transpose(0, 2, 1, 3)
    return x.reshape(e, n * chunks, h // chunks)


def pack_in(x, chunks):
    e, n, h = x.shape
    return x.reshape(e, chunks, n // chunks, h).transpose(0, 2, 1, 3).reshape(e, n // chunks, -1)


def unpack_in(x, chunks):
    e, n, h = x.shape
    x = x.reshape(e, n, chunks, h // chunks).transpose(0, 2, 1, 3)
    return x.reshape(e, n * chunks, h // chunks)


def all_experts(got, rows, near, chunks):
    groups = col_groups()[0]
    if groups == 1:
        return got
    m = got.shape[1] // 2
    k = got.shape[2]
    w_in = unpack_in(got[:, :m], chunks)
    _, n, h = w_in.shape
    w_in = collect_far(w_in.reshape(rows, near, n, h)).transpose(1, 3, 0, 2, 4)
    w_in = w_in.reshape(rows, n, near, groups * h).transpose(0, 2, 1, 3).reshape(E, n, groups * h)
    w_out_t = collect_far(got[:, m:].reshape(rows, near, m, k)).transpose(1, 0, 2, 3, 4)
    w_out_t = w_out_t.reshape(E, groups * m, k)
    return jnp.concatenate([pack_in(w_in, near // rows), w_out_t], axis=1)


def own_experts(sent, rows, near, chunks):
    groups = col_groups()[0]
    if groups == 1:
        return sent
    m = sent.shape[1] // 2
    k = sent.shape[2]
    w_in = unpack_in(sent[:, :m], near // rows)
    _, n, h = w_in.shape
    w_in = w_in.reshape(rows, near, n, h).transpose(0, 2, 1, 3)
    w_in = w_in.reshape(rows, n, groups, near, h // groups).transpose(2, 0, 3, 1, 4)
    w_in = reduce_far(w_in).reshape(E, n, h // groups)
    w_out_t = sent[:, m:].reshape(rows, groups, near, m // groups, k).transpose(1, 0, 2, 3, 4)
    w_out_t = reduce_far(w_out_t).reshape(E, m // groups, k)
    return jnp.concatenate([pack_in(w_in, chunks), w_out_t], axis=1)


def pad_images(x):
    t, w = x.shape
    return jnp.pad(x.reshape(t // SEQ, SEQ, w), ((0, 0), (0, ROWS - SEQ), (0, 0))).reshape(-1, w)


def cut_images(x):
    t, w = x.shape
    return x.reshape(t // ROWS, ROWS, w)[:, :SEQ].reshape(-1, w)


def call(kernel, name, out_shape, n_in, scalars=0, scratch=(), flops=0, moved=0, **kw):
    smem = pl.BlockSpec(memory_space=pltpu.SMEM)
    vmem = pl.BlockSpec(memory_space=pltpu.VMEM)
    return pl.pallas_call(
        kernel,
        name=name,
        out_shape=out_shape,
        in_specs=[smem] * scalars + [vmem] * n_in,
        out_specs=jax.tree.map(lambda _: vmem, out_shape),
        scratch_shapes=list(scratch),
        compiler_params=pltpu.CompilerParams(vmem_limit_bytes=VMEM),
        cost_estimate=pl.CostEstimate(flops=flops, bytes_accessed=moved, transcendentals=0),
        **kw,
    )


def shape(dims, dtype):
    return jax.ShapeDtypeStruct(tuple(dims), dtype)


def block(i, n):
    return pl.ds(pl.multiple_of(i * n, n), n)


def pack_kernel(chunks, in_ref, out_ref, sent_ref):
    n = in_ref.shape[1] // chunks
    h = in_ref.shape[2]
    for c in range(chunks):
        sent_ref[:, :n, c * h : (c + 1) * h] = in_ref[:, c * n : (c + 1) * n, :]
    sent_ref[:, n:, :] = out_ref[...]


def unpack_kernel(chunks, got_ref, in_ref, out_ref):
    n = in_ref.shape[1] // chunks
    h = in_ref.shape[2]
    for c in range(chunks):
        in_ref[:, c * n : (c + 1) * n, :] = got_ref[:, :n, c * h : (c + 1) * h].astype(F32)
    out_ref[...] = got_ref[:, n:, :].astype(F32)


def pack_weights(w_in, w_out_t):
    e, n, h = w_in.shape
    _, m, k = w_out_t.shape
    step = 4
    spec = lambda a, b: pl.BlockSpec((step, a, b), lambda i: (i, 0, 0))
    return pl.pallas_call(
        partial(pack_kernel, n // m),
        name="pack_weights",
        grid=(e // step,),
        out_shape=shape((e, 2 * m, k), BF16),
        in_specs=[spec(n, h), spec(m, k)],
        out_specs=spec(2 * m, k),
        cost_estimate=pl.CostEstimate(flops=0, bytes_accessed=8 * e * m * k, transcendentals=0),
    )(w_in, w_out_t)


def unpack_grads(got, n, h):
    e, m2, k = got.shape
    m = m2 // 2
    step = 4
    spec = lambda a, b: pl.BlockSpec((step, a, b), lambda i: (i, 0, 0))
    return pl.pallas_call(
        partial(unpack_kernel, n // m),
        name="unpack_grads",
        grid=(e // step,),
        out_shape=(shape((e, n, h), F32), shape((e, m, k), F32)),
        in_specs=[spec(m2, k)],
        out_specs=(spec(n, h), spec(m, k)),
        cost_estimate=pl.CostEstimate(flops=0, bytes_accessed=12 * e * m * k, transcendentals=0),
    )(got)


def slots_kernel(routes_ref, keep_ref, slots_ref):
    tokens = routes_ref.shape[1]
    experts = lax.broadcasted_iota(jnp.int32, (E, tokens), 0)
    named = [experts == routes_ref[j : j + 1, :] for j in range(2)]
    both = jnp.where(named[0] | named[1], 1.0, 0.0).astype(BF16)
    width = 128
    upper = lax.broadcasted_iota(jnp.int32, (width, width), 0) < lax.broadcasted_iota(
        jnp.int32, (width, width), 1
    )
    upper = jnp.where(upper, 1.0, 0.0).astype(BF16)
    before = jnp.zeros((E, 1), F32)
    counts = []
    for i in range(tokens // width):
        part = both[:, i * width : (i + 1) * width]
        counts.append(dot(part, upper, ((1,), (0,))) + before)
        before = before + jnp.sum(part.astype(F32), axis=1, keepdims=True)
    place = jnp.concatenate(counts, axis=1) + (experts * CAP).astype(F32)
    for j in range(2):
        slot = jnp.sum(jnp.where(named[j], place, 0.0), axis=0, keepdims=True).astype(jnp.int32)
        slots_ref[j : j + 1, :] = jnp.where(keep_ref[j : j + 1, :] != 0, slot, -1)


def slot_table(routes, keep):
    return call(slots_kernel, "slots", shape(routes.shape, jnp.int32), 2)(routes, keep)


def dispatch_kernel(n, where_ref, slots_ref, *refs):
    pieces, (sent_ref, values) = refs[:n], refs[n:]
    here = where_ref[0]
    part = pieces[0].shape[1]
    for k in range(n):
        values[block(here ^ k, part), :] = pieces[k][0]
    tokens = values.shape[0]
    step = 4

    def experts(i, carry):
        hits = []
        for j in range(step):
            first = (i * step + j) * CAP
            place = [slots_ref[p : p + 1, :] - first for p in range(2)]
            mine = [(p >= 0) & (p < CAP) for p in place]
            at = jnp.where(mine[0], place[0], jnp.where(mine[1], place[1], -1))
            rows = lax.broadcasted_iota(jnp.int32, (CAP, tokens), 0)
            hits.append(jnp.where(rows == at, 1.0, 0.0))
        hits = jnp.concatenate(hits, axis=0).astype(BF16)
        out = dot(hits, values[...], ((1,), (0,))).astype(BF16)
        sent_ref[block(i, step * CAP), :] = out
        return carry

    lax.fori_loop(0, E // step, experts, 0)


def dispatch(here, slots, pieces):
    n = len(pieces)
    _, part, w = pieces[0].shape
    return call(
        partial(dispatch_kernel, n),
        "dispatch",
        shape((E * CAP, w), BF16),
        1 + n,
        scalars=1,
        scratch=[pltpu.VMEM((n * part, w), BF16)],
        flops=2 * E * CAP * n * part * w,
        moved=2 * (E * CAP + n * part) * w,
    )(here, slots, *pieces)


def combine_rows(columns, got_ref):
    places = lax.broadcasted_iota(jnp.int32, (columns.shape[0], E * CAP), 1)
    hits = (places == columns[:, 0:1]) | (places == columns[:, 1:2])
    hits = jnp.where(hits, 1.0, 0.0).astype(BF16)
    return dot(hits, got_ref[...], ((1,), (0,)))


def combine_kernel(n, where_ref, columns_ref, got_ref, *outs):
    here = where_ref[0]
    part = outs[0].shape[0]
    tile = part // 2
    for k in range(n):
        base = (here ^ k) * part
        for half in range(2):
            rows = pl.ds(pl.multiple_of(base + half * tile, tile), tile)
            out = combine_rows(columns_ref[rows, :], got_ref)
            outs[k][half * tile : (half + 1) * tile, :] = out.astype(BF16)


def combine(here, columns, got, n):
    w = got.shape[1]
    part = columns.shape[0] // n
    return call(
        partial(combine_kernel, n),
        "combine",
        tuple(shape((part, w), BF16) for _ in range(n)),
        2,
        scalars=1,
        flops=2 * E * CAP * n * part * w,
        moved=2 * (E * CAP + n * part) * w,
    )(here, columns, got)


def finish_kernel(n, where_ref, columns_ref, got_ref, tokens_ref, *refs):
    pieces, (out_ref,) = refs[:n], refs[n:]
    here = where_ref[0]
    part = pieces[0].shape[1]
    tile = part // 2
    for k in range(n):
        base = (here ^ k) * part
        for half in range(2):
            rows = pl.ds(pl.multiple_of(base + half * tile, tile), tile)
            out = combine_rows(columns_ref[rows, :], got_ref)
            out = out + pieces[k][1, half * tile : (half + 1) * tile, :].astype(F32)
            out = out + tokens_ref[rows, :].astype(F32)
            out_ref[rows, :] = out.astype(BF16)


def finish(here, columns, got, tokens, pieces):
    n = len(pieces)
    t, w = tokens.shape
    return call(
        partial(finish_kernel, n),
        "finish",
        shape((t, w), BF16),
        3 + n,
        scalars=1,
        flops=2 * E * CAP * t * w,
        moved=2 * (E * CAP + 3 * t) * w,
    )(here, columns, got, tokens, *pieces)


def means(x):
    return jnp.mean(x, axis=1, keepdims=True)


def normalize(values):
    centred = values - means(values)
    inverse = lax.rsqrt(means(centred * centred) + EPS_NORM)
    return centred * inverse, inverse


def norm_backward(grad_normed, normalized, inverse, gain):
    scaled = grad_normed * gain
    return inverse * (scaled - means(scaled) - normalized * means(scaled * normalized))


def head_scores(q_pair, k_pair, low, head):
    keys = k_pair.shape[0]
    q_head = jnp.where(low if head % 2 == 0 else ~low, q_pair, jnp.zeros_like(q_pair))
    scores = dot(q_head, k_pair, ((1,), (1,))) * HD ** (-0.5)
    real = lax.broadcasted_iota(jnp.int32, (1, keys), 1) < SEQ
    return jnp.where(real, scores, -1e30)


def forward_kernel(n, where_ref, *refs):
    pieces = refs[:n]
    qkv_ref, mix_ref, norms_ref = refs[n : n + 3]
    sends = refs[n + 3 : 2 * n + 3]
    project_ref, attended_ref, residual_ref, totals_ref, x_s, n2_s, ao_s = refs[2 * n + 3 :]
    here = where_ref[0]
    w = pieces[0].shape[2]
    for k in range(n):
        x_s[:, block(here ^ k, w)] = pieces[k][0].astype(F32)
    width = n * w
    low = lax.broadcasted_iota(jnp.int32, (1, 2 * HD), 1) < HD
    lanes = lax.broadcasted_iota(jnp.int32, (1, 128), 1)
    for i in range(x_s.shape[0] // ROWS):
        rows = slice(i * ROWS, (i + 1) * ROWS)
        x = x_s[rows, :]
        normed = (normalize(x)[0] * norms_ref[0:1, :] + norms_ref[1:2, :]).astype(BF16)
        project = dot(normed, qkv_ref[...], ((1,), (1,))).astype(BF16)
        project_ref[rows, :] = project
        totals = jnp.zeros((ROWS, 128), F32)
        mixed = []
        for pair in range(width // (2 * HD)):
            at = [slice(j * width + pair * 2 * HD, j * width + (pair + 1) * 2 * HD) for j in range(3)]
            q_pair, k_pair, v_pair = (project[:, a] for a in at)
            heads = []
            for head in range(2):
                scores = head_scores(q_pair, k_pair, low, head)
                top = jnp.max(scores, axis=1, keepdims=True)
                powers = jnp.exp(scores - top)
                total = jnp.sum(powers, axis=1, keepdims=True)
                probs = (powers / total).astype(BF16)
                heads.append(dot(probs, v_pair, ((1,), (0,))))
                totals = jnp.where(lanes == 2 * pair + head, top + jnp.log(total), totals)
            mixed.append(jnp.where(low, heads[0], heads[1]).astype(BF16))
        attended = jnp.concatenate(mixed, axis=1)
        attended_ref[rows, :] = attended
        totals_ref[rows, :] = totals
        attn_out = dot(attended, mix_ref[...], ((1,), (1,)))
        residual = x + attn_out
        residual_ref[rows, :] = residual
        normed = normalize(residual)[0] * norms_ref[2:3, :] + norms_ref[3:4, :]
        n2_s[rows, :] = normed.astype(BF16)
        ao_s[rows, :] = attn_out.astype(BF16)
    for k in range(n):
        sends[k][0] = n2_s[:, block(here ^ k, w)]
        sends[k][1] = ao_s[:, block(here ^ k, w)]


def attention_forward(here, pieces, qkv_t, mix_t, norms):
    n = len(pieces)
    _, t, w = pieces[0].shape
    width = n * w
    out = call(
        partial(forward_kernel, n),
        "attention_forward",
        tuple(shape((2, t, w), BF16) for _ in range(n))
        + (
            shape((t, 3 * width), BF16),
            shape((t, width), BF16),
            shape((t, width), F32),
            shape((t, 128), F32),
        ),
        n + 3,
        scalars=1,
        scratch=[
            pltpu.VMEM((t, width), F32),
            pltpu.VMEM((t, width), BF16),
            pltpu.VMEM((t, width), BF16),
        ],
        flops=12 * t * width * width,
        moved=2**22,
    )(here, *pieces, qkv_t, mix_t, norms)
    return out[:n], out[n:]


def backward_kernel(n, where_ref, *refs):
    grads, pieces = refs[:n], refs[n : 2 * n]
    qkv_ref, mix_ref, norms_ref, project_ref, attended_ref, residual_ref, totals_ref = refs[
        2 * n : 2 * n + 7
    ]
    sends = refs[2 * n + 7 : 3 * n + 7]
    qkv_grad_ref, mix_grad_ref, small_ref, x_s, c_s, g_s, n1_s, ga_s, gp_s, tg_s = refs[3 * n + 7 :]
    here = where_ref[0]
    w = pieces[0].shape[2]
    for k in range(n):
        x_s[:, block(here ^ k, w)] = pieces[k][0].astype(F32)
        c_s[:, block(here ^ k, w)] = pieces[k][1].astype(F32)
        g_s[:, block(here ^ k, w)] = grads[k][...].astype(F32)
    width = n * w
    low = lax.broadcasted_iota(jnp.int32, (1, 2 * HD), 1) < HD
    sums = [jnp.zeros((1, width), F32) for _ in range(4)]
    for i in range(x_s.shape[0] // ROWS):
        rows = slice(i * ROWS, (i + 1) * ROWS)
        normal1, inverse1 = normalize(x_s[rows, :])
        n1_s[rows, :] = (normal1 * norms_ref[0:1, :] + norms_ref[1:2, :]).astype(BF16)
        normal2, inverse2 = normalize(residual_ref[rows, :])
        grad_norm2 = g_s[rows, :]
        sums[2] = sums[2] + jnp.sum(grad_norm2 * normal2, axis=0, keepdims=True)
        sums[3] = sums[3] + jnp.sum(grad_norm2, axis=0, keepdims=True)
        grad_resid = c_s[rows, :] + norm_backward(grad_norm2, normal2, inverse2, norms_ref[2:3, :])
        grad_attn = grad_resid.astype(BF16)
        ga_s[rows, :] = grad_attn
        grad_heads = dot(grad_attn, mix_ref[...], ((1,), (0,))).astype(BF16)
        project = project_ref[rows, :]
        for pair in range(width // (2 * HD)):
            at = [slice(j * width + pair * 2 * HD, j * width + (pair + 1) * 2 * HD) for j in range(3)]
            q_pair, k_pair, v_pair = (project[:, a] for a in at)
            g_pair = grad_heads[:, at[0]]
            got = []
            for head in range(2):
                scores = head_scores(q_pair, k_pair, low, head)
                lane = 2 * pair + head
                probs = jnp.exp(scores - totals_ref[rows, lane : lane + 1])
                g_head = jnp.where(low if head == 0 else ~low, g_pair, jnp.zeros_like(g_pair))
                grad_probs = dot(g_head, v_pair, ((1,), (1,)))
                row_dot = jnp.sum(probs * grad_probs, axis=1, keepdims=True)
                grad_scores = (probs * (grad_probs - row_dot)).astype(BF16)
                got.append(
                    (
                        dot(grad_scores, k_pair, ((1,), (0,))) * HD ** (-0.5),
                        dot(grad_scores, q_pair, ((0,), (0,))) * HD ** (-0.5),
                        dot(probs.astype(BF16), g_pair, ((0,), (0,))),
                    )
                )
            for j in range(3):
                gp_s[rows, at[j]] = jnp.where(low, got[0][j], got[1][j]).astype(BF16)
        grad_norm1 = dot(gp_s[rows, :], qkv_ref[...], ((1,), (0,)))
        sums[0] = sums[0] + jnp.sum(grad_norm1 * normal1, axis=0, keepdims=True)
        sums[1] = sums[1] + jnp.sum(grad_norm1, axis=0, keepdims=True)
        tokens_grad = grad_resid + norm_backward(grad_norm1, normal1, inverse1, norms_ref[0:1, :])
        tg_s[rows, :] = tokens_grad.astype(BF16)
    for k in range(n):
        sends[k][...] = tg_s[:, block(here ^ k, w)]
    qkv_grad_ref[...] = dot(gp_s[...], n1_s[...], ((0,), (0,)))
    mix_grad_ref[...] = dot(ga_s[...], attended_ref[...], ((0,), (0,)))
    for j in range(4):
        small_ref[j : j + 1, :] = sums[j]


def attention_backward(here, grads, pieces, qkv_t, mix_t, norms, saved):
    n = len(pieces)
    _, t, w = pieces[0].shape
    width = n * w
    out = call(
        partial(backward_kernel, n),
        "attention_backward",
        tuple(shape((t, w), BF16) for _ in range(n))
        + (shape((3 * width, width), F32), shape((width, width), F32), shape((4, width), F32)),
        2 * n + 7,
        scalars=1,
        scratch=[pltpu.VMEM((t, width), F32)] * 3
        + [pltpu.VMEM((t, width), BF16)] * 2
        + [pltpu.VMEM((t, 3 * width), BF16), pltpu.VMEM((t, width), BF16)],
        flops=30 * t * width * width,
        moved=2**23,
    )(here, *grads, *pieces, qkv_t, mix_t, norms, *saved)
    return out[:n], out[n:]


def hidden_block(w_ref, i, rows, near):
    m = w_ref.shape[1] // 2
    k = w_ref.shape[2]
    per = near // rows
    chunks = per
    h = k // chunks
    columns = []
    for c in range(per):
        columns.append(
            jnp.concatenate(
                [
                    w_ref[r * near + i * per + c, :m, j * h : (j + 1) * h]
                    for r in range(rows)
                    for j in range(chunks)
                ],
                axis=0,
            )
        )
    w_in = jnp.concatenate(columns, axis=1)
    w_out_t = jnp.concatenate([w_ref[i * near + c, m:, :] for c in range(near)], axis=0)
    return w_in, w_out_t


def assemble(got_ref, rows_s, rows, near):
    w = got_ref.shape[2]
    for c in range(near):
        for r in range(rows):
            rows_s[c * CAP : (c + 1) * CAP, r * w : (r + 1) * w] = got_ref[r * near + c].astype(F32)


def disperse(values_s, sent_ref, rows, near):
    w = sent_ref.shape[2]
    for c in range(near):
        for r in range(rows):
            piece = values_s[c * CAP : (c + 1) * CAP, r * w : (r + 1) * w]
            sent_ref[r * near + c] = piece.astype(BF16)


ERF = (0.254829592, -0.284496736, 1.421413741, -1.453152027, 1.061405429)


def gelu_pair(x):
    size = jnp.abs(x)
    t = 1.0 / (1.0 + (0.3275911 * 0.5**0.5) * size)
    bell = jnp.exp(-0.5 * x * x)
    tail = ERF[4]
    for coefficient in ERF[3::-1]:
        tail = tail * t + coefficient
    tail = (0.5 * tail) * (t * bell)
    below = jnp.where(x < 0, tail, 1.0 - tail)
    return x * below, below + x * bell * (0.5 / math.pi) ** 0.5


def expert_forward_kernel(
    rows, near, e_ref, got_ref, w_ref, router_ref, sent_ref, x_ref, act_ref, slope_ref, res_ref, gates_ref, f_s
):
    assemble(got_ref, f_s, rows, near)
    x_ref[...] = f_s[...].astype(BF16)
    logits = dot(x_ref[...], router_ref[...], ((1,), (1,)))
    powers = jnp.exp(logits - jnp.max(logits, axis=1, keepdims=True))
    gates = powers / jnp.sum(powers, axis=1, keepdims=True)
    gates_ref[...] = gates
    res_ref[...] = jnp.zeros_like(res_ref)

    def step(i, carry):
        w_in, w_out_t = hidden_block(w_ref, i, rows, near)
        pre = dot(x_ref[...], w_in, ((1,), (0,)))
        act, slope = gelu_pair(pre)
        act = act.astype(BF16)
        act_ref[i] = act
        slope_ref[i] = slope.astype(BF16)
        res_ref[...] += dot(act, w_out_t, ((1,), (1,)))
        return carry

    lax.fori_loop(0, rows, step, 0)
    own = lax.broadcasted_iota(jnp.int32, (1, E), 1) == e_ref[0]
    chosen = jnp.sum(jnp.where(own, gates, 0.0), axis=1, keepdims=True)
    f_s[...] = chosen * res_ref[...]
    disperse(f_s, sent_ref, rows, near)


def expert_forward(expert, got, w_got, router_t, rows, near):
    e, _, w = got.shape
    n, width, part = near * CAP, rows * w, w_got.shape[2]
    return call(
        partial(expert_forward_kernel, rows, near),
        "expert_forward",
        (
            shape(got.shape, BF16),
            shape((n, width), BF16),
            shape((rows, n, part), BF16),
            shape((rows, n, part), BF16),
            shape((n, width), F32),
            shape((n, E), F32),
        ),
        3,
        scalars=1,
        scratch=[pltpu.VMEM((n, width), F32)],
        flops=16 * n * width * rows * part // 4,
        moved=2**24,
    )(expert, got, w_got, router_t)


def expert_backward_kernel(
    rows, near, e_ref, got_ref, w_ref, router_ref, x_ref, slope_ref, res_ref, gates_ref,
    sent_ref, pre_ref, grad_res_ref, router_grad_ref, f_s,
):
    assemble(got_ref, f_s, rows, near)
    cot = f_s[...]
    gates = gates_ref[...]
    own = jnp.where(lax.broadcasted_iota(jnp.int32, (1, E), 1) == e_ref[0], 1.0, 0.0)
    chosen = jnp.sum(gates * own, axis=1, keepdims=True)
    grad_chosen = jnp.sum(cot * res_ref[...], axis=1, keepdims=True)
    grad_logits = (grad_chosen * chosen * (own - gates)).astype(BF16)
    grad_res_ref[...] = (chosen * cot).astype(BF16)
    router_grad_ref[...] = dot(grad_logits, x_ref[...], ((0,), (0,)))
    f_s[...] = dot(grad_logits, router_ref[...], ((1,), (0,)))

    def step(i, carry):
        w_in, w_out_t = hidden_block(w_ref, i, rows, near)
        grad_act = dot(grad_res_ref[...], w_out_t, ((1,), (0,)))
        grad_pre = (grad_act * slope_ref[i].astype(F32)).astype(BF16)
        pre_ref[i] = grad_pre
        f_s[...] += dot(grad_pre, w_in, ((1,), (1,)))
        return carry

    lax.fori_loop(0, rows, step, 0)
    disperse(f_s, sent_ref, rows, near)


def expert_backward(expert, got, w_got, router_t, x_rows, slope, res, gates, rows, near):
    e, _, w = got.shape
    n, width, part = near * CAP, rows * w, w_got.shape[2]
    return call(
        partial(expert_backward_kernel, rows, near),
        "expert_backward",
        (
            shape(got.shape, BF16),
            shape((rows, n, part), BF16),
            shape((n, width), BF16),
            shape((E, width), F32),
        ),
        7,
        scalars=1,
        scratch=[pltpu.VMEM((n, width), F32)],
        flops=16 * n * width * rows * part // 4,
        moved=2**24,
    )(expert, got, w_got, router_t, x_rows, slope, res, gates)


def expert_grads_kernel(rows, near, x_ref, pre_ref, grad_res_ref, act_ref, sent_ref):
    m = sent_ref.shape[1] // 2
    k = sent_ref.shape[2]
    per = near // rows
    h = k // per

    def step(i, carry):
        in_grad = dot(x_ref[...], pre_ref[i], ((0,), (0,))).astype(BF16)
        for r in range(rows):
            for c in range(per):
                for j in range(per):
                    first = (r * per + j) * m
                    sent_ref[r * near + i * per + c, :m, j * h : (j + 1) * h] = in_grad[
                        first : first + m, c * h : (c + 1) * h
                    ]
        out_grad_t = dot(grad_res_ref[...], act_ref[i], ((0,), (0,))).astype(BF16)
        for c in range(near):
            sent_ref[i * near + c, m:, :] = out_grad_t[c * m : (c + 1) * m, :]
        return carry

    lax.fori_loop(0, rows, step, 0)


def expert_grads(x_rows, grad_pre, grad_res, act, like, rows, near):
    n, width = x_rows.shape
    return call(
        partial(expert_grads_kernel, rows, near),
        "expert_grads",
        shape(like.shape, BF16),
        4,
        flops=4 * n * width * rows * like.shape[2],
        moved=2**24,
    )(x_rows, grad_pre, grad_res, act)


def local(
    tokens,
    ln1_gain,
    ln1_bias,
    qkv_weight,
    out_weight,
    ln2_gain,
    ln2_bias,
    router_weight,
    expert_in,
    expert_out,
    routes,
    keep,
    cotangent,
):
    rows, cols = lax.axis_size("row"), lax.axis_size("col")
    groups, near = col_groups()
    width_part = tokens.shape[1]
    width = width_part * rows
    hid_part = expert_in.shape[2]
    out_part = expert_out.shape[2]
    qkv_part, mix_part = qkv_weight.shape[1], out_weight.shape[1]
    chunks = width_part // out_part
    tiled = out_part % 16 == 0
    row, col = lax.axis_index("row"), lax.axis_index("col")
    here = row.astype(jnp.int32)[None]
    nowhere = jnp.zeros((1,), jnp.int32)
    expert = (row * near + col % near).astype(jnp.int32)[None]

    far = far_spread(jnp.concatenate([qkv_weight.T, out_weight.T], axis=0))
    out_t = expert_out.transpose(0, 2, 1)
    if tiled:
        w_sent = pack_weights(expert_in, out_t)
    else:
        w_sent = jnp.concatenate([pack_in(expert_in, chunks), out_t], axis=1)
    w_got = all_experts(exchange(after(w_sent, far)), rows, near, chunks)

    tok = pad_images(tokens)
    cot = pad_images(cotangent)
    pair = jnp.stack([tok.reshape(rows, -1, width_part), cot.reshape(rows, -1, width_part)], axis=1)
    pieces = row_swap(for_rows(pair))
    routes_t = jnp.pad(
        routes.T.reshape(2, -1, SEQ), ((0, 0), (0, 0), (0, ROWS - SEQ)), constant_values=-1
    ).reshape(2, -1)
    keep_t = jnp.pad(keep.T.reshape(2, -1, SEQ), ((0, 0), (0, 0), (0, ROWS - SEQ))).reshape(2, -1)
    slots = slot_table(routes_t, keep_t)
    columns = slots.T

    small = gather_all(far)
    qkv_t = small[:, :, :qkv_part].transpose(1, 2, 0, 3).reshape(3 * width, width)
    mix_t = small[:, :, qkv_part:].transpose(1, 2, 0, 3).reshape(width, width)
    norms = row_spread(
        jnp.concatenate(
            [jnp.stack([ln1_gain, ln1_bias, ln2_gain, ln2_bias]), router_weight.T.astype(F32)]
        )
    )
    norms = norms.transpose(1, 0, 2).reshape(4 + E, width)
    router_t = norms[4:].astype(BF16)
    norms = norms[:4]

    sends, saved = attention_forward(here, pieces, qkv_t, mix_t, norms)
    parts = row_swap(sends)

    def to_experts(x, *earlier):
        return exchange(after(x.reshape(E, CAP, width_part), *earlier))

    x_got = to_experts(dispatch(here, slots, parts), w_got)
    cot_got = to_experts(dispatch(nowhere, slots, [cot[None]]), x_got)
    moved, x_rows, act, slope, res, gates = expert_forward(
        expert, x_got, w_got, router_t, rows, near
    )
    moved = to_experts(moved, cot_got).reshape(E * CAP, width_part)
    grads, grad_pre, grad_res, router_part = expert_backward(
        expert, cot_got, w_got, router_t, x_rows, slope, res, gates, rows, near
    )
    grads = to_experts(grads, moved).reshape(E * CAP, width_part)
    w_grads = expert_grads(x_rows, grad_pre, grad_res, act, w_got, rows, near)
    w_grads = exchange(after(own_experts(w_grads, rows, near, chunks), grads))
    if tiled:
        expert_in_grad, out_grad_t = unpack_grads(w_grads, width_part, hid_part)
    else:
        expert_in_grad = unpack_in(w_grads[:, :out_part], chunks).astype(F32)
        out_grad_t = w_grads[:, out_part:].astype(F32)
    expert_out_grad = out_grad_t.transpose(0, 2, 1)

    back = row_swap(combine(here, columns, grads, rows))
    layer_out = cut_images(finish(here, columns, moved, tok, parts))
    sends, (qkv_grad_t, mix_grad_t, norm_parts) = attention_backward(
        here, back, pieces, qkv_t, mix_t, norms, saved
    )
    tokens_grad = jnp.concatenate(in_order(row_swap(sends), row), axis=0)
    tokens_grad = cut_images(tokens_grad).astype(F32)

    shares = jnp.concatenate(
        [
            qkv_grad_t.reshape(cols, qkv_part, width),
            mix_grad_t.reshape(cols, mix_part, width),
            jnp.broadcast_to(router_part[None], (cols, E, width)),
            jnp.broadcast_to(norm_parts[None], (cols, 4, width)),
        ],
        axis=1,
    )
    sums = reduce_all(shares)
    thin = width_part // cols
    tail = lax.dynamic_slice_in_dim(sums[qkv_part + mix_part :], col * thin, thin, axis=1)
    return (
        layer_out,
        tokens_grad,
        tail[E],
        tail[E + 1],
        sums[:qkv_part].T,
        sums[qkv_part : qkv_part + mix_part].T,
        tail[E + 2],
        tail[E + 3],
        tail[:E].T,
        expert_in_grad,
        expert_out_grad,
    )


def solution(mesh):
    in_specs = (
        P("col", "row"),
        P("row"),
        P("row"),
        P("row", "col"),
        P("row", "col"),
        P("row"),
        P("row"),
        P("row", None),
        P(None, "row", "col"),
        P(None, "row", "col"),
        P("col", None),
        P("col", None),
        P("col", "row"),
    )
    out_specs = (
        P("col", "row"),
        P("col", "row"),
        P(("row", "col")),
        P(("row", "col")),
        P("row", "col"),
        P("row", "col"),
        P(("row", "col")),
        P(("row", "col")),
        P(("row", "col"), None),
        P(None, "row", "col"),
        P(None, "row", "col"),
    )
    return jax.shard_map(local, mesh=mesh, in_specs=in_specs, out_specs=out_specs, check_vma=False)
```

```python
import math
from functools import partial

import jax
import jax.numpy as jnp
from jax import lax
from jax.experimental import pallas as pl
from jax.experimental.pallas import tpu as pltpu
from jax.sharding import PartitionSpec as P

E = 32
SEQ = 197
ROWS = 208
HD = 64
CAP = 120
EPS_NORM = 1e-06
VMEM = 60 * 2**20
TILE = 480
UNROLL = 4
F32 = jnp.float32
BF16 = jnp.bfloat16

def dot(a, b, dims):
    return lax.dot_general(a, b, (dims, ((), ())), preferred_element_type=F32)


def col_groups():
    rows, cols = lax.axis_size("row"), lax.axis_size("col")
    near = E // rows
    return cols // near, near


def exchange(pieces):
    groups, near = col_groups()
    if groups == 1:
        return lax.all_to_all(pieces, ("row", "col"), 0, 0, tiled=True)
    rows = lax.axis_size("row")
    index = [[g * near + c for c in range(near)] for g in range(groups)]
    parts = pieces.reshape((rows, near) + pieces.shape[1:])
    parts = lax.all_to_all(parts, "row", 0, 0, tiled=True)
    parts = lax.all_to_all(parts, "col", 1, 1, tiled=True, axis_index_groups=index)
    return parts.reshape(pieces.shape)


def far_groups():
    groups, near = col_groups()
    return [[g * near + c for g in range(groups)] for c in range(near)]


def collect_far(x):
    if col_groups()[0] == 1:
        return x[None]
    return lax.all_gather(x, "col", axis=0, axis_index_groups=far_groups())


def reduce_far(x):
    if col_groups()[0] == 1:
        return x[0]
    return lax.psum_scatter(x, "col", scatter_dimension=0, axis_index_groups=far_groups())


def after(x, *earlier):
    return lax.optimization_barrier((x,) + earlier)[0]


def swaps(axis, distance):
    return [(i, i ^ distance) for i in range(lax.axis_size(axis))]


def pick(pieces, at):
    return lax.dynamic_index_in_dim(pieces, at, 0, keepdims=False)


def in_order(got, here):
    pieces, step = list(got), 1
    while step < len(pieces):
        odd = (here & step) != 0
        pieces = [jnp.where(odd, pieces[k ^ step], pieces[k]) for k in range(len(pieces))]
        step *= 2
    return pieces


def row_exchange(pieces):
    here = lax.axis_index("row")
    got = [pick(pieces, here)]
    for k in range(1, lax.axis_size("row")):
        got.append(lax.ppermute(pick(pieces, here ^ k), "row", swaps("row", k)))
    return in_order(got, here)


def row_swap(pieces):
    got = [lax.ppermute(x, "row", swaps("row", k)) for k, x in enumerate(pieces) if k]
    return [pieces[0]] + got


def for_rows(x):
    here = lax.axis_index("row")
    return [pick(x, here ^ k) for k in range(x.shape[0])]


def row_spread(x):
    got = [x] + [lax.ppermute(x, "row", swaps("row", k)) for k in range(1, lax.axis_size("row"))]
    return jnp.stack(in_order(got, lax.axis_index("row")))


def far_swap(pieces):
    got = [lax.ppermute(x, "col", swaps("col", 2 * k)) for k, x in enumerate(pieces) if k]
    return [pieces[0]] + got


def core_swap(x):
    return lax.ppermute(x, "col", swaps("col", 1))


def parity_groups():
    cols = lax.axis_size("col")
    return [[2 * i + k for i in range(cols // 2)] for k in range(2)]


def far_spread(x):
    half = lax.axis_size("col") // 2
    if half > 8:
        return lax.all_gather(x, "col", axis=0, axis_index_groups=parity_groups())
    got = [x] + [lax.ppermute(x, "col", swaps("col", 2 * k)) for k in range(1, half)]
    return jnp.stack(in_order(got, lax.axis_index("col") // 2))


def far_sum(pieces):
    half = lax.axis_size("col") // 2
    if half > 8:
        got = lax.all_to_all(pieces, "col", 0, 0, tiled=True, axis_index_groups=parity_groups())
        return jnp.sum(got.astype(F32), axis=0)
    here = lax.axis_index("col") // 2
    total = pick(pieces, here).astype(F32)
    for k in range(1, half):
        sent = lax.ppermute(pick(pieces, here ^ k), "col", swaps("col", 2 * k))
        total = total + sent.astype(F32)
    return total


def gather_all(x):
    half = lax.axis_size("col") // 2
    mine = row_spread(x)
    other = lax.ppermute(mine, "col", swaps("col", 1))
    first = lax.axis_index("col") % 2 == 0
    both = jnp.stack([jnp.where(first, mine, other), jnp.where(first, other, mine)], axis=2)
    return both.reshape((both.shape[0], 2 * half) + x.shape[1:])


def reduce_all(x):
    cols, n, width = x.shape
    rows = lax.axis_size("row")
    core = lax.axis_index("col") % 2
    pairs = x.reshape(cols // 2, 2, n, width).transpose(1, 0, 2, 3).astype(BF16)
    sent = lax.ppermute(pick(pairs, 1 - core), "col", swaps("col", 1))
    mine = pick(pairs, core).astype(F32) + sent.astype(F32)
    mine = mine.astype(BF16).reshape(cols // 2, n, rows, width // rows).transpose(2, 0, 1, 3)
    mine = sum(piece.astype(F32) for piece in row_exchange(mine))
    return far_sum(mine.astype(BF16))


def pack_in(x, chunks):
    e, n, h = x.shape
    return x.reshape(e, chunks, n // chunks, h).transpose(0, 2, 1, 3).reshape(e, n // chunks, -1)


def unpack_in(x, chunks):
    e, n, h = x.shape
    x = x.reshape(e, n, chunks, h // chunks).transpose(0, 2, 1, 3)
    return x.reshape(e, n * chunks, h // chunks)


def pack_in(x, chunks):
    e, n, h = x.shape
    return x.reshape(e, chunks, n // chunks, h).transpose(0, 2, 1, 3).reshape(e, n // chunks, -1)


def unpack_in(x, chunks):
    e, n, h = x.shape
    x = x.reshape(e, n, chunks, h // chunks).transpose(0, 2, 1, 3)
    return x.reshape(e, n * chunks, h // chunks)


def all_experts(got, rows, near, chunks):
    groups = col_groups()[0]
    if groups == 1:
        return got
    m = got.shape[1] // 2
    k = got.shape[2]
    w_in = unpack_in(got[:, :m], chunks)
    _, n, h = w_in.shape
    w_in = collect_far(w_in.reshape(rows, near, n, h)).transpose(1, 3, 0, 2, 4)
    w_in = w_in.reshape(rows, n, near, groups * h).transpose(0, 2, 1, 3).reshape(E, n, groups * h)
    w_out_t = collect_far(got[:, m:].reshape(rows, near, m, k)).transpose(1, 0, 2, 3, 4)
    w_out_t = w_out_t.reshape(E, groups * m, k)
    return jnp.concatenate([pack_in(w_in, near // rows), w_out_t], axis=1)


def own_experts(sent, rows, near, chunks):
    groups = col_groups()[0]
    if groups == 1:
        return sent
    m = sent.shape[1] // 2
    k = sent.shape[2]
    w_in = unpack_in(sent[:, :m], near // rows)
    _, n, h = w_in.shape
    w_in = w_in.reshape(rows, near, n, h).transpose(0, 2, 1, 3)
    w_in = w_in.reshape(rows, n, groups, near, h // groups).transpose(2, 0, 3, 1, 4)
    w_in = reduce_far(w_in).reshape(E, n, h // groups)
    w_out_t = sent[:, m:].reshape(rows, groups, near, m // groups, k).transpose(1, 0, 2, 3, 4)
    w_out_t = reduce_far(w_out_t).reshape(E, m // groups, k)
    return jnp.concatenate([pack_in(w_in, chunks), w_out_t], axis=1)


def pad_images(x):
    t, w = x.shape
    return jnp.pad(x.reshape(t // SEQ, SEQ, w), ((0, 0), (0, ROWS - SEQ), (0, 0))).reshape(-1, w)


def cut_images(x):
    t, w = x.shape
    return x.reshape(t // ROWS, ROWS, w)[:, :SEQ].reshape(-1, w)


def call(kernel, name, out_shape, n_in, scalars=0, scratch=(), flops=0, moved=0, **kw):
    smem = pl.BlockSpec(memory_space=pltpu.SMEM)
    vmem = pl.BlockSpec(memory_space=pltpu.VMEM)
    return pl.pallas_call(
        kernel,
        name=name,
        out_shape=out_shape,
        in_specs=[smem] * scalars + [vmem] * n_in,
        out_specs=jax.tree.map(lambda _: vmem, out_shape),
        scratch_shapes=list(scratch),
        compiler_params=pltpu.CompilerParams(vmem_limit_bytes=VMEM),
        cost_estimate=pl.CostEstimate(flops=flops, bytes_accessed=moved, transcendentals=0),
        **kw,
    )


def shape(dims, dtype):
    return jax.ShapeDtypeStruct(tuple(dims), dtype)


def block(i, n):
    if isinstance(i, int):
        return slice(i * n, (i + 1) * n)
    return pl.ds(pl.multiple_of(i * n, n), n)


def pack_kernel(chunks, in_ref, out_ref, sent_ref):
    n = in_ref.shape[1] // chunks
    h = in_ref.shape[2]
    for c in range(chunks):
        sent_ref[:, :n, c * h : (c + 1) * h] = in_ref[:, c * n : (c + 1) * n, :]
    sent_ref[:, n:, :] = out_ref[...]


def unpack_kernel(chunks, got_ref, in_ref, out_ref):
    n = in_ref.shape[1] // chunks
    h = in_ref.shape[2]
    for c in range(chunks):
        in_ref[:, c * n : (c + 1) * n, :] = got_ref[:, :n, c * h : (c + 1) * h].astype(F32)
    out_ref[...] = got_ref[:, n:, :].astype(F32)


def pack_weights(w_in, w_out_t):
    e, n, h = w_in.shape
    _, m, k = w_out_t.shape
    step = 16
    spec = lambda a, b: pl.BlockSpec((step, a, b), lambda i: (i, 0, 0))
    return pl.pallas_call(
        partial(pack_kernel, n // m),
        name="pack_weights",
        grid=(e // step,),
        out_shape=shape((e, 2 * m, k), BF16),
        in_specs=[spec(n, h), spec(m, k)],
        out_specs=spec(2 * m, k),
        compiler_params=pltpu.CompilerParams(vmem_limit_bytes=VMEM),
        cost_estimate=pl.CostEstimate(flops=0, bytes_accessed=8 * e * m * k, transcendentals=0),
    )(w_in, w_out_t)


def unpack_grads(got, n, h):
    e, m2, k = got.shape
    m = m2 // 2
    step = 16
    spec = lambda a, b: pl.BlockSpec((step, a, b), lambda i: (i, 0, 0))
    return pl.pallas_call(
        partial(unpack_kernel, n // m),
        name="unpack_grads",
        grid=(e // step,),
        out_shape=(shape((e, n, h), F32), shape((e, m, k), F32)),
        in_specs=[spec(m2, k)],
        out_specs=(spec(n, h), spec(m, k)),
        compiler_params=pltpu.CompilerParams(vmem_limit_bytes=VMEM),
        cost_estimate=pl.CostEstimate(flops=0, bytes_accessed=12 * e * m * k, transcendentals=0),
    )(got)


def slots_kernel(routes_ref, keep_ref, slots_ref):
    tokens = routes_ref.shape[1]
    experts = lax.broadcasted_iota(jnp.int32, (E, tokens), 0)
    named = [experts == routes_ref[j : j + 1, :] for j in range(2)]
    both = jnp.where(named[0] | named[1], 1.0, 0.0).astype(BF16)
    width = 128
    upper = lax.broadcasted_iota(jnp.int32, (width, width), 0) < lax.broadcasted_iota(
        jnp.int32, (width, width), 1
    )
    upper = jnp.where(upper, 1.0, 0.0).astype(BF16)
    before = jnp.zeros((E, 1), F32)
    counts = []
    for i in range(tokens // width):
        part = both[:, i * width : (i + 1) * width]
        counts.append(dot(part, upper, ((1,), (0,))) + before)
        before = before + jnp.sum(part.astype(F32), axis=1, keepdims=True)
    place = jnp.concatenate(counts, axis=1) + (experts * CAP).astype(F32)
    for j in range(2):
        slot = jnp.sum(jnp.where(named[j], place, 0.0), axis=0, keepdims=True).astype(jnp.int32)
        slots_ref[j : j + 1, :] = jnp.where(keep_ref[j : j + 1, :] != 0, slot, -1)


def slot_table(routes, keep):
    return call(slots_kernel, "slots", shape(routes.shape, jnp.int32), 2)(routes, keep)


def dispatch_kernel(n, where_ref, slots_ref, *refs):
    pieces, (sent_ref, values) = refs[:n], refs[n:]
    here = where_ref[0]
    part = pieces[0].shape[0]
    for k in range(n):
        values[block(here ^ k, part), :] = pieces[k][...]
    tokens = values.shape[0]
    step = 4

    def experts(i, carry):
        hits = []
        for j in range(step):
            first = (i * step + j) * CAP
            place = [slots_ref[p : p + 1, :] - first for p in range(2)]
            mine = [(p >= 0) & (p < CAP) for p in place]
            at = jnp.where(mine[0], place[0], jnp.where(mine[1], place[1], -1))
            rows = lax.broadcasted_iota(jnp.int32, (CAP, tokens), 0)
            hits.append(jnp.where(rows == at, 1.0, 0.0))
        hits = jnp.concatenate(hits, axis=0).astype(BF16)
        out = dot(hits, values[...], ((1,), (0,))).astype(BF16)
        sent_ref[block(i, step * CAP), :] = out
        return carry

    lax.fori_loop(0, E // step, experts, 0)


def dispatch(here, slots, pieces):
    n = len(pieces)
    part, w = pieces[0].shape
    return call(
        partial(dispatch_kernel, n),
        "dispatch",
        shape((E * CAP, w), BF16),
        1 + n,
        scalars=1,
        scratch=[pltpu.VMEM((n * part, w), BF16)],
        flops=2 * E * CAP * n * part * w,
        moved=2 * (E * CAP + n * part) * w,
    )(here, slots, *pieces)


def combine_rows(columns, got_ref):
    places = lax.broadcasted_iota(jnp.int32, (columns.shape[0], E * CAP), 1)
    hits = (places == columns[:, 0:1]) | (places == columns[:, 1:2])
    hits = jnp.where(hits, 1.0, 0.0).astype(BF16)
    return dot(hits, got_ref[...], ((1,), (0,)))


def combine_kernel(n, where_ref, columns_ref, got_ref, *outs):
    here = where_ref[0]
    part = outs[0].shape[0]
    tile = part // 2
    for k in range(n):
        base = (here ^ k) * part
        for half in range(2):
            rows = pl.ds(pl.multiple_of(base + half * tile, tile), tile)
            out = combine_rows(columns_ref[rows, :], got_ref)
            outs[k][half * tile : (half + 1) * tile, :] = out.astype(BF16)


def combine(here, columns, got, n):
    w = got.shape[1]
    part = columns.shape[0] // n
    return call(
        partial(combine_kernel, n),
        "combine",
        tuple(shape((part, w), BF16) for _ in range(n)),
        2,
        scalars=1,
        flops=2 * E * CAP * n * part * w,
        moved=2 * (E * CAP + n * part) * w,
    )(here, columns, got)


def finish_kernel(n, where_ref, columns_ref, got_ref, tokens_ref, *refs):
    pieces, (out_ref,) = refs[:n], refs[n:]
    here = where_ref[0]
    part = pieces[0].shape[1]
    tile = part // 2
    for k in range(n):
        base = (here ^ k) * part
        for half in range(2):
            rows = pl.ds(pl.multiple_of(base + half * tile, tile), tile)
            out = combine_rows(columns_ref[rows, :], got_ref)
            out = out + pieces[k][0, half * tile : (half + 1) * tile, :].astype(F32)
            out = out + tokens_ref[rows, :].astype(F32)
            out_ref[rows, :] = out.astype(BF16)


def finish(here, columns, got, tokens, pieces):
    n = len(pieces)
    t, w = tokens.shape
    return call(
        partial(finish_kernel, n),
        "finish",
        shape((t, w), BF16),
        3 + n,
        scalars=1,
        flops=2 * E * CAP * t * w,
        moved=2 * (E * CAP + 3 * t) * w,
    )(here, columns, got, tokens, *pieces)


def means(x):
    return jnp.mean(x, axis=1, keepdims=True)


def normalize(values):
    centred = values - means(values)
    inverse = lax.rsqrt(means(centred * centred) + EPS_NORM)
    return centred * inverse, inverse


def norm_backward(grad_normed, normalized, inverse, gain):
    scaled = grad_normed * gain
    return inverse * (scaled - means(scaled) - normalized * means(scaled * normalized))


def head_scores(q_pair, k_pair, low, head):
    keys = k_pair.shape[0]
    q_head = jnp.where(low if head % 2 == 0 else ~low, q_pair, jnp.zeros_like(q_pair))
    scores = dot(q_head, k_pair, ((1,), (1,))) * HD ** (-0.5)
    real = lax.broadcasted_iota(jnp.int32, (1, keys), 1) < SEQ
    return jnp.where(real, scores, -1e30)


def forward_kernel(n, where_ref, *refs):
    pieces, others = refs[:n], refs[n : 2 * n]
    qkv_ref, mix_ref, norms_ref = refs[2 * n : 2 * n + 3]
    sends, laters = refs[2 * n + 3 : 3 * n + 3], refs[3 * n + 3 : 4 * n + 3]
    project_ref, attended_ref, residual_ref, totals_ref, x_s, n2_s, ao_s = refs[4 * n + 3 :]
    here = where_ref[0]
    w = pieces[0].shape[1]
    for k in range(n):
        x_s[:, block(here ^ k, w)] = pieces[k][...].astype(F32)
    width = n * w
    pairs = width // (2 * HD)
    low = lax.broadcasted_iota(jnp.int32, (1, 2 * HD), 1) < HD
    lanes = lax.broadcasted_iota(jnp.int32, (1, 128), 1)

    def image(i, carry):
        rows = block(i, ROWS)
        normed = normalize(x_s[rows, :])[0] * norms_ref[0:1, :] + norms_ref[1:2, :]
        project_ref[rows, :] = dot(normed.astype(BF16), qkv_ref[...], ((1,), (1,))).astype(BF16)

        def head_pair(pair, totals):
            q_pair, k_pair, v_pair = (
                project_ref[rows, block(j * pairs + pair, 2 * HD)] for j in range(3)
            )
            heads = []
            for head in range(2):
                scores = head_scores(q_pair, k_pair, low, head)
                top = jnp.max(scores, axis=1, keepdims=True)
                powers = jnp.exp(scores - top)
                total = jnp.sum(powers, axis=1, keepdims=True)
                probs = (powers / total).astype(BF16)
                heads.append(dot(probs, v_pair, ((1,), (0,))))
                totals = jnp.where(lanes == 2 * pair + head, top + jnp.log(total), totals)
            mixed = jnp.where(low, heads[0], heads[1])
            attended_ref[rows, block(pair, 2 * HD)] = mixed.astype(BF16)
            return totals

        totals = jnp.zeros((ROWS, 128), F32)
        for pair in range(pairs):
            totals = head_pair(pair, totals)
        totals_ref[rows, :] = totals
        attn_out = dot(attended_ref[rows, :], mix_ref[...], ((1,), (1,)))
        residual = x_s[rows, :] + attn_out
        residual_ref[rows, :] = residual
        normed = normalize(residual)[0] * norms_ref[2:3, :] + norms_ref[3:4, :]
        n2_s[rows, :] = normed.astype(BF16)
        ao_s[rows, :] = attn_out.astype(BF16)
        return carry

    lax.fori_loop(0, x_s.shape[0] // ROWS, image, 0)
    for k in range(n):
        sends[k][...] = n2_s[:, block(here ^ k, w)]
        laters[k][0] = ao_s[:, block(here ^ k, w)]
        laters[k][1] = others[k][...]


def attention_forward(where, pieces, others, qkv_t, mix_t, norms):
    n = len(pieces)
    t, w = pieces[0].shape
    width = n * w
    out = call(
        partial(forward_kernel, n),
        "attention_forward",
        tuple(shape((t, w), BF16) for _ in range(n))
        + tuple(shape((2, t, w), BF16) for _ in range(n))
        + (
            shape((t, 3 * width), BF16),
            shape((t, width), BF16),
            shape((t, width), F32),
            shape((t, 128), F32),
        ),
        2 * n + 3,
        scalars=1,
        scratch=[
            pltpu.VMEM((t, width), F32),
            pltpu.VMEM((t, width), BF16),
            pltpu.VMEM((t, width), BF16),
        ],
        flops=12 * t * width * width,
        moved=2**22,
    )(where, *pieces, *others, qkv_t, mix_t, norms)
    return out[:n], out[n : 2 * n], out[2 * n :]


def backward_kernel(n, far, parts, where_ref, *refs):
    grads, pieces, others = refs[:n], refs[n : 2 * n], refs[2 * n : 3 * n]
    (
        qkv_ref, mix_ref, norms_ref, project_ref, attended_ref, residual_ref, totals_ref, router_ref,
    ) = refs[3 * n : 3 * n + 8]
    sends = refs[3 * n + 8 : 4 * n + 8]
    refs = refs[4 * n + 8 :]
    outs, (x_s, c_s, g_s, n1_s, ga_s, gp_s, tg_s, sums_s) = refs[:-8], refs[-8:]
    here = where_ref[0]
    w = pieces[0].shape[1]
    for k in range(n):
        x_s[:, block(here ^ k, w)] = pieces[k][...].astype(F32)
        c_s[:, block(here ^ k, w)] = others[k][1].astype(F32)
        g_s[:, block(here ^ k, w)] = grads[k][...].astype(F32)
    width = n * w
    pairs = width // (2 * HD)
    low = lax.broadcasted_iota(jnp.int32, (1, 2 * HD), 1) < HD
    lanes = lax.broadcasted_iota(jnp.int32, (1, 128), 1)
    scale = HD ** (-0.5)
    sums_s[...] = jnp.zeros_like(sums_s)

    def image(i, carry):
        rows = block(i, ROWS)
        normal2, inverse2 = normalize(residual_ref[rows, :])
        grad_norm2 = g_s[rows, :]
        sums_s[2:3, :] += jnp.sum(grad_norm2 * normal2, axis=0, keepdims=True)
        sums_s[3:4, :] += jnp.sum(grad_norm2, axis=0, keepdims=True)
        grad_resid = c_s[rows, :] + norm_backward(grad_norm2, normal2, inverse2, norms_ref[2:3, :])
        c_s[rows, :] = grad_resid
        grad_attn = grad_resid.astype(BF16)
        ga_s[rows, :] = grad_attn
        tg_s[rows, :] = dot(grad_attn, mix_ref[...], ((1,), (0,))).astype(BF16)

        def head_pair(pair, carry):
            q_pair, k_pair, v_pair = (
                project_ref[rows, block(j * pairs + pair, 2 * HD)] for j in range(3)
            )
            g_pair = tg_s[rows, block(pair, 2 * HD)]
            totals = totals_ref[rows, :]
            got = []
            for head in range(2):
                scores = head_scores(q_pair, k_pair, low, head)
                total = jnp.sum(
                    jnp.where(lanes == 2 * pair + head, totals, 0.0), axis=1, keepdims=True
                )
                probs = jnp.exp(scores - total)
                g_head = jnp.where(low if head == 0 else ~low, g_pair, jnp.zeros_like(g_pair))
                grad_probs = dot(g_head, v_pair, ((1,), (1,)))
                row_dot = jnp.sum(probs * grad_probs, axis=1, keepdims=True)
                grad_scores = (probs * (grad_probs - row_dot)).astype(BF16)
                got.append(
                    (
                        dot(grad_scores, k_pair, ((1,), (0,))) * scale,
                        dot(grad_scores, q_pair, ((0,), (0,))) * scale,
                        dot(probs.astype(BF16), g_pair, ((0,), (0,))),
                    )
                )
            for j in range(3):
                out = jnp.where(low, got[0][j], got[1][j])
                gp_s[rows, block(j * pairs + pair, 2 * HD)] = out.astype(BF16)
            return carry

        lax.fori_loop(0, pairs, head_pair, 0, unroll=UNROLL)
        normal1, inverse1 = normalize(x_s[rows, :])
        n1_s[rows, :] = (normal1 * norms_ref[0:1, :] + norms_ref[1:2, :]).astype(BF16)
        grad_norm1 = dot(gp_s[rows, :], qkv_ref[...], ((1,), (0,)))
        sums_s[0:1, :] += jnp.sum(grad_norm1 * normal1, axis=0, keepdims=True)
        sums_s[1:2, :] += jnp.sum(grad_norm1, axis=0, keepdims=True)
        tokens_grad = c_s[rows, :] + norm_backward(
            grad_norm1, normal1, inverse1, norms_ref[0:1, :]
        )
        tg_s[rows, :] = tokens_grad.astype(BF16)
        return carry

    lax.fori_loop(0, x_s.shape[0] // ROWS, image, 0)
    for k in range(n):
        sends[k][...] = tg_s[:, block(here ^ k, w)]
    qkv_grad = dot(gp_s[...], n1_s[...], ((0,), (0,)))
    mix_grad = dot(ga_s[...], attended_ref[...], ((0,), (0,)))
    if parts is None:
        outs[0][...] = qkv_grad
        outs[1][...] = mix_grad
        outs[2][:E, :] = router_ref[...]
        outs[2][E : E + 8, :] = sums_s[...]
        return
    outs, (qkv_s, mix_s, small_s) = outs[:2], outs[2:]
    qkv_s[...] = qkv_grad.astype(BF16)
    mix_s[...] = mix_grad.astype(BF16)
    small_s[...] = jnp.concatenate(
        [router_ref[...], sums_s[...], jnp.zeros((8, width), F32)], axis=0
    ).astype(BF16)
    first, second = parts

    def piece(at, carry):
        k, z = at // far, at % far
        part = block(here ^ k, w)
        for p in range(2):
            c = 2 * (where_ref[1] ^ z) + (where_ref[2] ^ p)
            outs[p][k, z, :first, :] = qkv_s[block(c, first), part]
            outs[p][k, z, first : first + second, :] = mix_s[block(c, second), part]
            outs[p][k, z, first + second :, :] = small_s[:, part]
        return carry

    lax.fori_loop(0, n * far, piece, 0)


def attention_backward(
    where, grads, pieces, others, qkv_t, mix_t, norms, saved, router_part, far, parts
):
    n = len(pieces)
    t, w = pieces[0].shape
    width = n * w
    scratch = [pltpu.VMEM((t, width), F32)] * 3 + [pltpu.VMEM((t, width), BF16)] * 2
    scratch += [pltpu.VMEM((t, 3 * width), BF16), pltpu.VMEM((t, width), BF16)]
    scratch += [pltpu.VMEM((8, width), F32)]
    if parts is None:
        outs = (
            shape((3 * width, width), F32),
            shape((width, width), F32),
            shape((E + 8, width), F32),
        )
    else:
        outs = (shape((n, far, sum(parts) + E + 16, w), BF16),) * 2
        scratch = [
            pltpu.VMEM((3 * width, width), BF16),
            pltpu.VMEM((width, width), BF16),
            pltpu.VMEM((E + 16, width), BF16),
        ] + scratch
    out = call(
        partial(backward_kernel, n, far, parts),
        "attention_backward",
        tuple(shape((t, w), BF16) for _ in range(n)) + outs,
        3 * n + 8,
        scalars=1,
        scratch=scratch,
        flops=30 * t * width * width,
        moved=2**23,
    )(where, *grads, *pieces, *others, qkv_t, mix_t, norms, *saved, router_part)
    return out[:n], out[n:]


def split_three(x):
    parts = []
    for _ in range(3):
        part = lax.reduce_precision(x, 8, 7)
        parts.append(part.astype(BF16))
        x = x - part
    return parts


def gather_kernel(n, far, parts, where_ref, *refs):
    qkv_ref, mix_ref, router_ref, norms_ref = refs[2 * n :]
    first, second = parts
    depth = first + second
    w = refs[0].shape[1]
    for k in range(n):
        part = block(where_ref[0] ^ k, w)
        for p in range(2):
            piece = refs[p * n + k]
            for z in range(far):
                c = 2 * (where_ref[1] ^ z) + (where_ref[2] ^ p)
                qkv_ref[block(c, first), part] = piece[z * depth : z * depth + first, :]
                mix_ref[block(c, second), part] = piece[z * depth + first : (z + 1) * depth, :]
        router_ref[:, part] = refs[k][far * depth : far * depth + E, :]
        extra = refs[k][far * depth + E :, :].astype(F32)
        norms_ref[:, part] = extra[0:4] + extra[4:8] + extra[8:12]


def gather_weights(where, pieces, far, parts):
    n = len(pieces) // 2
    _, w = pieces[0].shape
    return call(
        partial(gather_kernel, n, far, parts),
        "gather_weights",
        tuple(shape((2 * far * part, n * w), BF16) for part in parts)
        + (shape((E, n * w), BF16), shape((4, n * w), F32)),
        2 * n,
        scalars=1,
        moved=2**22,
    )(where, *pieces)


def add_core_kernel(own_ref, got_ref, *outs):
    for k, out in enumerate(outs):
        out[...] = (own_ref[k].astype(F32) + got_ref[k].astype(F32)).astype(BF16)


def add_core(own, got):
    return call(
        add_core_kernel,
        "add_core",
        tuple(shape(own.shape[1:], BF16) for _ in range(own.shape[0])),
        2,
        moved=6 * own.size,
    )(own, got)


def add_rows_kernel(n, *refs):
    pieces, outs = refs[:n], refs[n:]
    for z, out in enumerate(outs):
        out[...] = sum(piece[z].astype(F32) for piece in pieces).astype(BF16)


def add_rows(pieces):
    far, depth, w = pieces[0].shape
    return call(
        partial(add_rows_kernel, len(pieces)),
        "add_rows",
        tuple(shape((depth, w), BF16) for _ in range(far)),
        len(pieces),
        moved=10 * far * depth * w,
    )(*pieces)


def add_far_kernel(n, parts, *refs):
    pieces, (qkv_ref, mix_ref, small_ref) = refs[:n], refs[n:]
    total = sum(piece[...].astype(F32) for piece in pieces)
    first, second = parts
    qkv_ref[...] = total[:first]
    mix_ref[...] = total[first : first + second]
    small_ref[...] = total[first + second : first + second + E + 8]


def add_far(pieces, parts):
    w = pieces[0].shape[1]
    return call(
        partial(add_far_kernel, len(pieces), parts),
        "add_far",
        tuple(shape((part, w), F32) for part in (*parts, E + 8)),
        len(pieces),
        moved=12 * pieces[0].size,
    )(*pieces)


def hidden_block(w_ref, i, rows, near):
    m = w_ref.shape[1] // 2
    k = w_ref.shape[2]
    per = near // rows
    chunks = per
    h = k // chunks
    columns = []
    for c in range(per):
        columns.append(
            jnp.concatenate(
                [
                    w_ref[r * near + i * per + c, :m, j * h : (j + 1) * h]
                    for r in range(rows)
                    for j in range(chunks)
                ],
                axis=0,
            )
        )
    w_in = jnp.concatenate(columns, axis=1)
    w_out_t = jnp.concatenate([w_ref[i * near + c, m:, :] for c in range(near)], axis=0)
    return w_in, w_out_t


def assemble(got_ref, rows_s, rows, near):
    w = got_ref.shape[2]
    for c in range(near):
        for r in range(rows):
            rows_s[c * CAP : (c + 1) * CAP, r * w : (r + 1) * w] = got_ref[r * near + c].astype(F32)


def disperse(values_s, sent_ref, rows, near):
    w = sent_ref.shape[2]
    for c in range(near):
        for r in range(rows):
            piece = values_s[c * CAP : (c + 1) * CAP, r * w : (r + 1) * w]
            sent_ref[r * near + c] = piece.astype(BF16)


ERF = (0.254829592, -0.284496736, 1.421413741, -1.453152027, 1.061405429)


def gelu_pair(x):
    size = jnp.abs(x)
    t = 1.0 / (1.0 + (0.3275911 * 0.5**0.5) * size)
    bell = jnp.exp(-0.5 * x * x)
    tail = ERF[4]
    for coefficient in ERF[3::-1]:
        tail = tail * t + coefficient
    tail = (0.5 * tail) * (t * bell)
    below = jnp.where(x < 0, tail, 1.0 - tail)
    return x * below, below + x * bell * (0.5 / math.pi) ** 0.5


def expert_forward_kernel(
    rows, near, e_ref, got_ref, w_ref, router_ref,
    sent_ref, x_ref, act_ref, slope_ref, res_ref, gates_ref, f_s, in_s, out_s,
):
    assemble(got_ref, f_s, rows, near)
    x_ref[...] = f_s[...].astype(BF16)
    logits = dot(x_ref[...], router_ref[...], ((1,), (1,)))
    powers = jnp.exp(logits - jnp.max(logits, axis=1, keepdims=True))
    gates = powers / jnp.sum(powers, axis=1, keepdims=True)
    gates_ref[...] = gates
    res_ref[...] = jnp.zeros_like(res_ref)

    def step(i, carry):
        in_s[...], out_s[...] = hidden_block(w_ref, i, rows, near)

        def tile(j, carry):
            at = block(j, TILE)
            pre = dot(x_ref[at, :], in_s[...], ((1,), (0,)))
            act, slope = gelu_pair(pre)
            act = act.astype(BF16)
            act_ref[i, at, :] = act
            slope_ref[i, at, :] = slope.astype(BF16)
            res_ref[at, :] += dot(act, out_s[...], ((1,), (1,)))
            return carry

        return lax.fori_loop(0, x_ref.shape[0] // TILE, tile, carry)

    lax.fori_loop(0, rows, step, 0)
    own = lax.broadcasted_iota(jnp.int32, (1, E), 1) == e_ref[0]
    chosen = jnp.sum(jnp.where(own, gates, 0.0), axis=1, keepdims=True)
    f_s[...] = chosen * res_ref[...]
    disperse(f_s, sent_ref, rows, near)


def expert_forward(expert, got, w_got, router_t, rows, near):
    e, _, w = got.shape
    n, width, part = near * CAP, rows * w, w_got.shape[2]
    return call(
        partial(expert_forward_kernel, rows, near),
        "expert_forward",
        (
            shape(got.shape, BF16),
            shape((n, width), BF16),
            shape((rows, n, part), BF16),
            shape((rows, n, part), BF16),
            shape((n, width), F32),
            shape((n, E), F32),
        ),
        3,
        scalars=1,
        scratch=[pltpu.VMEM((n, width), F32)] + [pltpu.VMEM((width, part), BF16)] * 2,
        flops=16 * n * width * rows * part // 4,
        moved=2**24,
    )(expert, got, w_got, router_t)


def expert_backward_kernel(
    rows, near, e_ref, got_ref, w_ref, router_ref, x_ref, slope_ref, res_ref, gates_ref,
    sent_ref, pre_ref, grad_res_ref, router_grad_ref, f_s,
):
    assemble(got_ref, f_s, rows, near)
    cot = f_s[...]
    gates = gates_ref[...]
    own = jnp.where(lax.broadcasted_iota(jnp.int32, (1, E), 1) == e_ref[0], 1.0, 0.0)
    chosen = jnp.sum(gates * own, axis=1, keepdims=True)
    grad_chosen = jnp.sum(cot * res_ref[...], axis=1, keepdims=True)
    grad_logits = (grad_chosen * chosen * (own - gates)).astype(BF16)
    grad_res_ref[...] = (chosen * cot).astype(BF16)
    router_grad_ref[...] = dot(grad_logits, x_ref[...], ((0,), (0,)))
    f_s[...] = dot(grad_logits, router_ref[...], ((1,), (0,)))

    def step(i, carry):
        w_in, w_out_t = hidden_block(w_ref, i, rows, near)
        grad_act = dot(grad_res_ref[...], w_out_t, ((1,), (0,)))
        grad_pre = (grad_act * slope_ref[i].astype(F32)).astype(BF16)
        pre_ref[i] = grad_pre
        f_s[...] += dot(grad_pre, w_in, ((1,), (1,)))
        return carry

    lax.fori_loop(0, rows, step, 0)
    disperse(f_s, sent_ref, rows, near)


def expert_backward(expert, got, w_got, router_t, x_rows, slope, res, gates, rows, near):
    e, _, w = got.shape
    n, width, part = near * CAP, rows * w, w_got.shape[2]
    return call(
        partial(expert_backward_kernel, rows, near),
        "expert_backward",
        (
            shape(got.shape, BF16),
            shape((rows, n, part), BF16),
            shape((n, width), BF16),
            shape((E, width), F32),
        ),
        7,
        scalars=1,
        scratch=[pltpu.VMEM((n, width), F32)],
        flops=16 * n * width * rows * part // 4,
        moved=2**24,
    )(expert, got, w_got, router_t, x_rows, slope, res, gates)


def expert_grads_kernel(rows, near, x_ref, pre_ref, grad_res_ref, act_ref, sent_ref):
    m = sent_ref.shape[1] // 2
    k = sent_ref.shape[2]
    per = near // rows
    h = k // per

    def step(i, carry):
        in_grad = dot(x_ref[...], pre_ref[i], ((0,), (0,))).astype(BF16)
        for r in range(rows):
            for c in range(per):
                for j in range(per):
                    first = (r * per + j) * m
                    sent_ref[r * near + i * per + c, :m, j * h : (j + 1) * h] = in_grad[
                        first : first + m, c * h : (c + 1) * h
                    ]
        out_grad_t = dot(grad_res_ref[...], act_ref[i], ((0,), (0,))).astype(BF16)
        for c in range(near):
            sent_ref[i * near + c, m:, :] = out_grad_t[c * m : (c + 1) * m, :]
        return carry

    lax.fori_loop(0, rows, step, 0)


def expert_grads(x_rows, grad_pre, grad_res, act, like, rows, near):
    n, width = x_rows.shape
    return call(
        partial(expert_grads_kernel, rows, near),
        "expert_grads",
        shape(like.shape, BF16),
        4,
        flops=4 * n * width * rows * like.shape[2],
        moved=2**24,
    )(x_rows, grad_pre, grad_res, act)


def local(
    tokens,
    ln1_gain,
    ln1_bias,
    qkv_weight,
    out_weight,
    ln2_gain,
    ln2_bias,
    router_weight,
    expert_in,
    expert_out,
    routes,
    keep,
    cotangent,
):
    rows, cols = lax.axis_size("row"), lax.axis_size("col")
    groups, near = col_groups()
    width_part = tokens.shape[1]
    width = width_part * rows
    hid_part = expert_in.shape[2]
    out_part = expert_out.shape[2]
    qkv_part, mix_part = qkv_weight.shape[1], out_weight.shape[1]
    chunks = width_part // out_part
    half = cols // 2
    parts = (qkv_part, mix_part)
    tiled = half <= 8 and all(part % 16 == 0 for part in (out_part, *parts))
    row, col = lax.axis_index("row"), lax.axis_index("col")
    here = jnp.stack([row, col // 2, col % 2]).astype(jnp.int32)
    nowhere = jnp.zeros((1,), jnp.int32)
    expert = (row * near + col % near).astype(jnp.int32)[None]

    near_parts = jnp.concatenate([qkv_weight.T, out_weight.T], axis=0)
    norms = jnp.stack([ln1_gain, ln1_bias, ln2_gain, ln2_bias])
    if tiled:
        shared = [router_weight.T, *split_three(norms), jnp.zeros_like(norms, BF16)]
        far = jnp.concatenate(far_swap([near_parts] * half) + shared)
    else:
        far = far_spread(near_parts)
    tok = pad_images(after(tokens, near_parts))
    cot = pad_images(after(cotangent, near_parts))
    pieces = row_swap(for_rows(tok.reshape(rows, -1, width_part)))
    cot_pieces = for_rows(cot.reshape(rows, -1, width_part))
    out_t = expert_out.transpose(0, 2, 1)
    if tiled:
        w_sent = pack_weights(expert_in, out_t)
    else:
        w_sent = jnp.concatenate([pack_in(expert_in, chunks), out_t], axis=1)
    w_got = exchange(after(w_sent, far))
    w_got = all_experts(w_got, rows, near, chunks)
    if tiled:
        mine = row_swap([far] * rows)
        qkv_t, mix_t, router_t, norms = gather_weights(
            here, mine + [core_swap(x) for x in mine], half, parts
        )
    else:
        small = gather_all(far)
        qkv_t = small[:, :, :qkv_part].transpose(1, 2, 0, 3).reshape(3 * width, width)
        mix_t = small[:, :, qkv_part:].transpose(1, 2, 0, 3).reshape(width, width)
        norms = row_spread(jnp.concatenate([norms, router_weight.T.astype(F32)]))
        norms = norms.transpose(1, 0, 2).reshape(4 + E, width)
        router_t = norms[4:].astype(BF16)
        norms = norms[:4]

    routes_t = jnp.pad(
        routes.T.reshape(2, -1, SEQ), ((0, 0), (0, 0), (0, ROWS - SEQ)), constant_values=-1
    ).reshape(2, -1)
    keep_t = jnp.pad(keep.T.reshape(2, -1, SEQ), ((0, 0), (0, 0), (0, ROWS - SEQ))).reshape(2, -1)
    slots = slot_table(routes_t, keep_t)
    columns = slots.T

    sends, laters, saved = attention_forward(here, pieces, cot_pieces, qkv_t, mix_t, norms)
    normed = row_swap(sends)
    others = row_swap(laters)

    def to_experts(x, *earlier):
        return exchange(after(x.reshape(E, CAP, width_part), *earlier))

    x_got = to_experts(dispatch(here, slots, normed), w_got)
    cot_got = to_experts(dispatch(nowhere, slots, [cot]), x_got, *others)
    moved, x_rows, act, slope, res, gates = expert_forward(
        expert, x_got, w_got, router_t, rows, near
    )
    moved = to_experts(moved, cot_got).reshape(E * CAP, width_part)
    grads, grad_pre, grad_res, router_part = expert_backward(
        expert, cot_got, w_got, router_t, x_rows, slope, res, gates, rows, near
    )
    grads = to_experts(grads, moved).reshape(E * CAP, width_part)
    w_grads = expert_grads(x_rows, grad_pre, grad_res, act, w_got, rows, near)
    w_grads = exchange(after(own_experts(w_grads, rows, near, chunks), grads))
    if tiled:
        expert_in_grad, out_grad_t = unpack_grads(w_grads, width_part, hid_part)
    else:
        expert_in_grad = unpack_in(w_grads[:, :out_part], chunks).astype(F32)
        out_grad_t = w_grads[:, out_part:].astype(F32)
    expert_out_grad = out_grad_t.transpose(0, 2, 1)

    back = row_swap(combine(here, columns, grads, rows))
    layer_out = cut_images(finish(here, columns, moved, tok, others))
    back[0] = after(back[0], layer_out)
    sends, outs = attention_backward(
        here, back, pieces, others, qkv_t, mix_t, norms, saved, router_part, half, parts if tiled else None
    )

    if tiled:
        own, other = outs
        got = row_swap(add_core(own, core_swap(other)))
        got = far_swap(add_rows(got))
        qkv_grad, mix_grad, tail = add_far(got, parts)
    else:
        qkv_grad_t, mix_grad_t, tail = outs
        shares = jnp.concatenate(
            [
                qkv_grad_t.reshape(cols, qkv_part, width),
                mix_grad_t.reshape(cols, mix_part, width),
                jnp.broadcast_to(tail[None], (cols,) + tail.shape),
            ],
            axis=1,
        )
        sums = reduce_all(shares)
        qkv_grad, mix_grad, tail = jnp.split(sums, [qkv_part, qkv_part + mix_part])
    thin = width_part // cols
    tail = lax.dynamic_slice_in_dim(tail, col * thin, thin, axis=1)
    tokens_grad = jnp.concatenate(in_order(row_swap(sends), row), axis=0)
    tokens_grad = cut_images(tokens_grad).astype(F32)
    return (
        layer_out,
        tokens_grad,
        tail[E],
        tail[E + 1],
        qkv_grad.T,
        mix_grad.T,
        tail[E + 2],
        tail[E + 3],
        tail[:E].T,
        expert_in_grad,
        expert_out_grad,
    )


def solution(mesh):
    in_specs = (
        P("col", "row"),
        P("row"),
        P("row"),
        P("row", "col"),
        P("row", "col"),
        P("row"),
        P("row"),
        P("row", None),
        P(None, "row", "col"),
        P(None, "row", "col"),
        P("col", None),
        P("col", None),
        P("col", "row"),
    )
    out_specs = (
        P("col", "row"),
        P("col", "row"),
        P(("row", "col")),
        P(("row", "col")),
        P("row", "col"),
        P("row", "col"),
        P(("row", "col")),
        P(("row", "col")),
        P(("row", "col"), None),
        P(None, "row", "col"),
        P(None, "row", "col"),
    )
    return jax.shard_map(local, mesh=mesh, in_specs=in_specs, out_specs=out_specs, check_vma=False)
```

```python
import math
from functools import partial

import jax
import jax.numpy as jnp
from jax import lax
from jax.experimental import pallas as pl
from jax.experimental.pallas import tpu as pltpu
from jax.sharding import PartitionSpec as P

E = 32
SEQ = 197
ROWS = 208
HD = 64
CAP = 120
EPS_NORM = 1e-06
VMEM = 60 * 2**20
SMALL = 24 * 2**20
TILE = 480
UNROLL = 4
F32 = jnp.float32
BF16 = jnp.bfloat16

def dot(a, b, dims):
    return lax.dot_general(a, b, (dims, ((), ())), preferred_element_type=F32)


def col_groups():
    rows, cols = lax.axis_size("row"), lax.axis_size("col")
    near = E // rows
    return cols // near, near


def exchange(pieces):
    groups, near = col_groups()
    if groups == 1:
        return lax.all_to_all(pieces, ("row", "col"), 0, 0, tiled=True)
    rows = lax.axis_size("row")
    index = [[g * near + c for c in range(near)] for g in range(groups)]
    parts = pieces.reshape((rows, near) + pieces.shape[1:])
    parts = lax.all_to_all(parts, "row", 0, 0, tiled=True)
    parts = lax.all_to_all(parts, "col", 1, 1, tiled=True, axis_index_groups=index)
    return parts.reshape(pieces.shape)


def far_groups():
    groups, near = col_groups()
    return [[g * near + c for g in range(groups)] for c in range(near)]


def collect_far(x):
    if col_groups()[0] == 1:
        return x[None]
    return lax.all_gather(x, "col", axis=0, axis_index_groups=far_groups())


def reduce_far(x):
    if col_groups()[0] == 1:
        return x[0]
    return lax.psum_scatter(x, "col", scatter_dimension=0, axis_index_groups=far_groups())


def after(x, *earlier):
    return lax.optimization_barrier((x,) + earlier)[0]


def swaps(axis, distance):
    return [(i, i ^ distance) for i in range(lax.axis_size(axis))]


def pick(pieces, at):
    return lax.dynamic_index_in_dim(pieces, at, 0, keepdims=False)


def in_order(got, here):
    pieces, step = list(got), 1
    while step < len(pieces):
        odd = (here & step) != 0
        pieces = [jnp.where(odd, pieces[k ^ step], pieces[k]) for k in range(len(pieces))]
        step *= 2
    return pieces


def row_exchange(pieces):
    here = lax.axis_index("row")
    got = [pick(pieces, here)]
    for k in range(1, lax.axis_size("row")):
        got.append(lax.ppermute(pick(pieces, here ^ k), "row", swaps("row", k)))
    return in_order(got, here)


def row_swap(pieces):
    got = [lax.ppermute(x, "row", swaps("row", k)) for k, x in enumerate(pieces) if k]
    return [pieces[0]] + got


def for_rows(x):
    here = lax.axis_index("row")
    return [pick(x, here ^ k) for k in range(x.shape[0])]


def row_spread(x):
    got = [x] + [lax.ppermute(x, "row", swaps("row", k)) for k in range(1, lax.axis_size("row"))]
    return jnp.stack(in_order(got, lax.axis_index("row")))


def far_swap(pieces):
    got = [lax.ppermute(x, "col", swaps("col", 2 * k)) for k, x in enumerate(pieces) if k]
    return [pieces[0]] + got


def core_swap(x):
    return lax.ppermute(x, "col", swaps("col", 1))


def parity_groups():
    cols = lax.axis_size("col")
    return [[2 * i + k for i in range(cols // 2)] for k in range(2)]


def far_spread(x):
    half = lax.axis_size("col") // 2
    if half > 8:
        return lax.all_gather(x, "col", axis=0, axis_index_groups=parity_groups())
    got = [x] + [lax.ppermute(x, "col", swaps("col", 2 * k)) for k in range(1, half)]
    return jnp.stack(in_order(got, lax.axis_index("col") // 2))


def far_sum(pieces):
    half = lax.axis_size("col") // 2
    if half > 8:
        got = lax.all_to_all(pieces, "col", 0, 0, tiled=True, axis_index_groups=parity_groups())
        return jnp.sum(got.astype(F32), axis=0)
    here = lax.axis_index("col") // 2
    total = pick(pieces, here).astype(F32)
    for k in range(1, half):
        sent = lax.ppermute(pick(pieces, here ^ k), "col", swaps("col", 2 * k))
        total = total + sent.astype(F32)
    return total


def gather_all(x):
    half = lax.axis_size("col") // 2
    mine = row_spread(x)
    other = lax.ppermute(mine, "col", swaps("col", 1))
    first = lax.axis_index("col") % 2 == 0
    both = jnp.stack([jnp.where(first, mine, other), jnp.where(first, other, mine)], axis=2)
    return both.reshape((both.shape[0], 2 * half) + x.shape[1:])


def reduce_all(x):
    cols, n, width = x.shape
    rows = lax.axis_size("row")
    core = lax.axis_index("col") % 2
    pairs = x.reshape(cols // 2, 2, n, width).transpose(1, 0, 2, 3).astype(BF16)
    sent = lax.ppermute(pick(pairs, 1 - core), "col", swaps("col", 1))
    mine = pick(pairs, core).astype(F32) + sent.astype(F32)
    mine = mine.astype(BF16).reshape(cols // 2, n, rows, width // rows).transpose(2, 0, 1, 3)
    mine = sum(piece.astype(F32) for piece in row_exchange(mine))
    return far_sum(mine.astype(BF16))


def pack_in(x, chunks):
    e, n, h = x.shape
    return x.reshape(e, chunks, n // chunks, h).transpose(0, 2, 1, 3).reshape(e, n // chunks, -1)


def unpack_in(x, chunks):
    e, n, h = x.shape
    x = x.reshape(e, n, chunks, h // chunks).transpose(0, 2, 1, 3)
    return x.reshape(e, n * chunks, h // chunks)


def pack_in(x, chunks):
    e, n, h = x.shape
    return x.reshape(e, chunks, n // chunks, h).transpose(0, 2, 1, 3).reshape(e, n // chunks, -1)


def unpack_in(x, chunks):
    e, n, h = x.shape
    x = x.reshape(e, n, chunks, h // chunks).transpose(0, 2, 1, 3)
    return x.reshape(e, n * chunks, h // chunks)


def all_experts(got, rows, near, chunks):
    groups = col_groups()[0]
    if groups == 1:
        return got
    m = got.shape[1] // 2
    k = got.shape[2]
    w_in = unpack_in(got[:, :m], chunks)
    _, n, h = w_in.shape
    w_in = collect_far(w_in.reshape(rows, near, n, h)).transpose(1, 3, 0, 2, 4)
    w_in = w_in.reshape(rows, n, near, groups * h).transpose(0, 2, 1, 3).reshape(E, n, groups * h)
    w_out_t = collect_far(got[:, m:].reshape(rows, near, m, k)).transpose(1, 0, 2, 3, 4)
    w_out_t = w_out_t.reshape(E, groups * m, k)
    return jnp.concatenate([pack_in(w_in, near // rows), w_out_t], axis=1)


def own_experts(sent, rows, near, chunks):
    groups = col_groups()[0]
    if groups == 1:
        return sent
    m = sent.shape[1] // 2
    k = sent.shape[2]
    w_in = unpack_in(sent[:, :m], near // rows)
    _, n, h = w_in.shape
    w_in = w_in.reshape(rows, near, n, h).transpose(0, 2, 1, 3)
    w_in = w_in.reshape(rows, n, groups, near, h // groups).transpose(2, 0, 3, 1, 4)
    w_in = reduce_far(w_in).reshape(E, n, h // groups)
    w_out_t = sent[:, m:].reshape(rows, groups, near, m // groups, k).transpose(1, 0, 2, 3, 4)
    w_out_t = reduce_far(w_out_t).reshape(E, m // groups, k)
    return jnp.concatenate([pack_in(w_in, chunks), w_out_t], axis=1)


def pad_images(x):
    t, w = x.shape
    return jnp.pad(x.reshape(t // SEQ, SEQ, w), ((0, 0), (0, ROWS - SEQ), (0, 0))).reshape(-1, w)


def cut_images(x):
    t, w = x.shape
    return x.reshape(t // ROWS, ROWS, w)[:, :SEQ].reshape(-1, w)


def call(kernel, name, out_shape, n_in, scalars=0, scratch=(), flops=0, moved=0, limit=VMEM, **kw):
    smem = pl.BlockSpec(memory_space=pltpu.SMEM)
    vmem = pl.BlockSpec(memory_space=pltpu.VMEM)
    return pl.pallas_call(
        kernel,
        name=name,
        out_shape=out_shape,
        in_specs=[smem] * scalars + [vmem] * n_in,
        out_specs=jax.tree.map(lambda _: vmem, out_shape),
        scratch_shapes=list(scratch),
        compiler_params=pltpu.CompilerParams(vmem_limit_bytes=limit),
        cost_estimate=pl.CostEstimate(flops=flops, bytes_accessed=moved, transcendentals=0),
        **kw,
    )


def shape(dims, dtype):
    return jax.ShapeDtypeStruct(tuple(dims), dtype)


def block(i, n):
    if isinstance(i, int):
        return slice(i * n, (i + 1) * n)
    return pl.ds(pl.multiple_of(i * n, n), n)


def pack_kernel(chunks, in_ref, out_ref, sent_ref):
    n = in_ref.shape[1] // chunks
    h = in_ref.shape[2]
    for c in range(chunks):
        sent_ref[:, :n, c * h : (c + 1) * h] = in_ref[:, c * n : (c + 1) * n, :]
    sent_ref[:, n:, :] = out_ref[...]


def unpack_kernel(chunks, got_ref, in_ref, out_ref):
    n = in_ref.shape[1] // chunks
    h = in_ref.shape[2]
    for c in range(chunks):
        in_ref[:, c * n : (c + 1) * n, :] = got_ref[:, :n, c * h : (c + 1) * h].astype(F32)
    out_ref[...] = got_ref[:, n:, :].astype(F32)


def pack_weights(w_in, w_out_t):
    e, n, h = w_in.shape
    _, m, k = w_out_t.shape
    step = 16
    spec = lambda a, b: pl.BlockSpec((step, a, b), lambda i: (i, 0, 0))
    return pl.pallas_call(
        partial(pack_kernel, n // m),
        name="pack_weights",
        grid=(e // step,),
        out_shape=shape((e, 2 * m, k), BF16),
        in_specs=[spec(n, h), spec(m, k)],
        out_specs=spec(2 * m, k),
        compiler_params=pltpu.CompilerParams(vmem_limit_bytes=VMEM),
        cost_estimate=pl.CostEstimate(flops=0, bytes_accessed=8 * e * m * k, transcendentals=0),
    )(w_in, w_out_t)


def unpack_grads(got, n, h):
    e, m2, k = got.shape
    m = m2 // 2
    step = 16
    spec = lambda a, b: pl.BlockSpec((step, a, b), lambda i: (i, 0, 0))
    return pl.pallas_call(
        partial(unpack_kernel, n // m),
        name="unpack_grads",
        grid=(e // step,),
        out_shape=(shape((e, n, h), F32), shape((e, m, k), F32)),
        in_specs=[spec(m2, k)],
        out_specs=(spec(n, h), spec(m, k)),
        compiler_params=pltpu.CompilerParams(vmem_limit_bytes=VMEM),
        cost_estimate=pl.CostEstimate(flops=0, bytes_accessed=12 * e * m * k, transcendentals=0),
    )(got)


def slots_kernel(routes_ref, keep_ref, slots_ref):
    tokens = routes_ref.shape[1]
    experts = lax.broadcasted_iota(jnp.int32, (E, tokens), 0)
    named = [experts == routes_ref[j : j + 1, :] for j in range(2)]
    both = jnp.where(named[0] | named[1], 1.0, 0.0).astype(BF16)
    width = 128
    upper = lax.broadcasted_iota(jnp.int32, (width, width), 0) < lax.broadcasted_iota(
        jnp.int32, (width, width), 1
    )
    upper = jnp.where(upper, 1.0, 0.0).astype(BF16)
    before = jnp.zeros((E, 1), F32)
    counts = []
    for i in range(tokens // width):
        part = both[:, i * width : (i + 1) * width]
        counts.append(dot(part, upper, ((1,), (0,))) + before)
        before = before + jnp.sum(part.astype(F32), axis=1, keepdims=True)
    place = jnp.concatenate(counts, axis=1) + (experts * CAP).astype(F32)
    for j in range(2):
        slot = jnp.sum(jnp.where(named[j], place, 0.0), axis=0, keepdims=True).astype(jnp.int32)
        slots_ref[j : j + 1, :] = jnp.where(keep_ref[j : j + 1, :] != 0, slot, -1)


def slot_table(routes, keep):
    return call(slots_kernel, "slots", shape(routes.shape, jnp.int32), 2, limit=SMALL)(routes, keep)


def dispatch_kernel(n, where_ref, slots_ref, *refs):
    pieces, (sent_ref, values) = refs[:n], refs[n:]
    here = where_ref[0]
    part = pieces[0].shape[0]
    for k in range(n):
        values[block(here ^ k, part), :] = pieces[k][...]
    tokens = values.shape[0]
    step = 4

    def experts(i, carry):
        hits = []
        for j in range(step):
            first = (i * step + j) * CAP
            place = [slots_ref[p : p + 1, :] - first for p in range(2)]
            mine = [(p >= 0) & (p < CAP) for p in place]
            at = jnp.where(mine[0], place[0], jnp.where(mine[1], place[1], -1))
            rows = lax.broadcasted_iota(jnp.int32, (CAP, tokens), 0)
            hits.append(jnp.where(rows == at, 1.0, 0.0))
        hits = jnp.concatenate(hits, axis=0).astype(BF16)
        out = dot(hits, values[...], ((1,), (0,))).astype(BF16)
        sent_ref[block(i, step * CAP), :] = out
        return carry

    lax.fori_loop(0, E // step, experts, 0)


def dispatch(here, slots, pieces):
    n = len(pieces)
    part, w = pieces[0].shape
    return call(
        partial(dispatch_kernel, n),
        "dispatch",
        shape((E * CAP, w), BF16),
        1 + n,
        scalars=1,
        scratch=[pltpu.VMEM((n * part, w), BF16)],
        flops=2 * E * CAP * n * part * w,
        moved=2 * (E * CAP + n * part) * w,
        limit=SMALL,
    )(here, slots, *pieces)


def combine_rows(columns, got_ref):
    places = lax.broadcasted_iota(jnp.int32, (columns.shape[0], E * CAP), 1)
    hits = (places == columns[:, 0:1]) | (places == columns[:, 1:2])
    hits = jnp.where(hits, 1.0, 0.0).astype(BF16)
    return dot(hits, got_ref[...], ((1,), (0,)))


def combine_kernel(n, where_ref, columns_ref, got_ref, *outs):
    here = where_ref[0]
    part = outs[0].shape[0]
    tile = part // 2
    for k in range(n):
        base = (here ^ k) * part
        for half in range(2):
            rows = pl.ds(pl.multiple_of(base + half * tile, tile), tile)
            out = combine_rows(columns_ref[rows, :], got_ref)
            outs[k][half * tile : (half + 1) * tile, :] = out.astype(BF16)


def combine(here, columns, got, n):
    w = got.shape[1]
    part = columns.shape[0] // n
    return call(
        partial(combine_kernel, n),
        "combine",
        tuple(shape((part, w), BF16) for _ in range(n)),
        2,
        scalars=1,
        flops=2 * E * CAP * n * part * w,
        moved=2 * (E * CAP + n * part) * w,
        limit=SMALL,
    )(here, columns, got)


def finish_kernel(n, where_ref, columns_ref, got_ref, tokens_ref, *refs):
    pieces, (out_ref,) = refs[:n], refs[n:]
    here = where_ref[0]
    part = pieces[0].shape[1]
    tile = part // 2
    for k in range(n):
        base = (here ^ k) * part
        for half in range(2):
            rows = pl.ds(pl.multiple_of(base + half * tile, tile), tile)
            out = combine_rows(columns_ref[rows, :], got_ref)
            out = out + pieces[k][0, half * tile : (half + 1) * tile, :].astype(F32)
            out = out + tokens_ref[rows, :].astype(F32)
            out_ref[rows, :] = out.astype(BF16)


def finish(here, columns, got, tokens, pieces):
    n = len(pieces)
    t, w = tokens.shape
    return call(
        partial(finish_kernel, n),
        "finish",
        shape((t, w), BF16),
        3 + n,
        scalars=1,
        flops=2 * E * CAP * t * w,
        moved=2 * (E * CAP + 3 * t) * w,
        limit=SMALL,
    )(here, columns, got, tokens, *pieces)


def means(x):
    return jnp.mean(x, axis=1, keepdims=True)


def normalize(values):
    centred = values - means(values)
    inverse = lax.rsqrt(means(centred * centred) + EPS_NORM)
    return centred * inverse, inverse


def norm_backward(grad_normed, normalized, inverse, gain):
    scaled = grad_normed * gain
    return inverse * (scaled - means(scaled) - normalized * means(scaled * normalized))


def head_scores(q_pair, k_pair, low, head):
    keys = k_pair.shape[0]
    q_head = jnp.where(low if head % 2 == 0 else ~low, q_pair, jnp.zeros_like(q_pair))
    scores = dot(q_head, k_pair, ((1,), (1,))) * HD ** (-0.5)
    real = lax.broadcasted_iota(jnp.int32, (1, keys), 1) < SEQ
    return jnp.where(real, scores, -1e30)


def forward_kernel(n, where_ref, *refs):
    pieces, others = refs[:n], refs[n : 2 * n]
    qkv_ref, mix_ref, norms_ref = refs[2 * n : 2 * n + 3]
    sends, laters = refs[2 * n + 3 : 3 * n + 3], refs[3 * n + 3 : 4 * n + 3]
    project_ref, attended_ref, residual_ref, totals_ref, x_s, n2_s, ao_s = refs[4 * n + 3 :]
    here = where_ref[0]
    w = pieces[0].shape[1]
    for k in range(n):
        x_s[:, block(here ^ k, w)] = pieces[k][...].astype(F32)
    width = n * w
    pairs = width // (2 * HD)
    low = lax.broadcasted_iota(jnp.int32, (1, 2 * HD), 1) < HD
    lanes = lax.broadcasted_iota(jnp.int32, (1, 128), 1)

    def image(i, carry):
        rows = block(i, ROWS)
        normed = normalize(x_s[rows, :])[0] * norms_ref[0:1, :] + norms_ref[1:2, :]
        project_ref[rows, :] = dot(normed.astype(BF16), qkv_ref[...], ((1,), (1,))).astype(BF16)

        def head_pair(pair, totals):
            q_pair, k_pair, v_pair = (
                project_ref[rows, block(j * pairs + pair, 2 * HD)] for j in range(3)
            )
            heads = []
            for head in range(2):
                scores = head_scores(q_pair, k_pair, low, head)
                top = jnp.max(scores, axis=1, keepdims=True)
                powers = jnp.exp(scores - top)
                total = jnp.sum(powers, axis=1, keepdims=True)
                probs = (powers / total).astype(BF16)
                heads.append(dot(probs, v_pair, ((1,), (0,))))
                totals = jnp.where(lanes == 2 * pair + head, top + jnp.log(total), totals)
            mixed = jnp.where(low, heads[0], heads[1])
            attended_ref[rows, block(pair, 2 * HD)] = mixed.astype(BF16)
            return totals

        totals = jnp.zeros((ROWS, 128), F32)
        for pair in range(pairs):
            totals = head_pair(pair, totals)
        totals_ref[rows, :] = totals
        attn_out = dot(attended_ref[rows, :], mix_ref[...], ((1,), (1,)))
        residual = x_s[rows, :] + attn_out
        residual_ref[rows, :] = residual
        normed = normalize(residual)[0] * norms_ref[2:3, :] + norms_ref[3:4, :]
        n2_s[rows, :] = normed.astype(BF16)
        ao_s[rows, :] = attn_out.astype(BF16)
        return carry

    lax.fori_loop(0, x_s.shape[0] // ROWS, image, 0)
    for k in range(n):
        sends[k][...] = n2_s[:, block(here ^ k, w)]
        laters[k][0] = ao_s[:, block(here ^ k, w)]
        laters[k][1] = others[k][...]


def attention_forward(where, pieces, others, qkv_t, mix_t, norms):
    n = len(pieces)
    t, w = pieces[0].shape
    width = n * w
    out = call(
        partial(forward_kernel, n),
        "attention_forward",
        tuple(shape((t, w), BF16) for _ in range(n))
        + tuple(shape((2, t, w), BF16) for _ in range(n))
        + (
            shape((t, 3 * width), BF16),
            shape((t, width), BF16),
            shape((t, width), F32),
            shape((t, 128), F32),
        ),
        2 * n + 3,
        scalars=1,
        scratch=[
            pltpu.VMEM((t, width), F32),
            pltpu.VMEM((t, width), BF16),
            pltpu.VMEM((t, width), BF16),
        ],
        flops=12 * t * width * width,
        moved=2**22,
    )(where, *pieces, *others, qkv_t, mix_t, norms)
    return out[:n], out[n : 2 * n], out[2 * n :]


def backward_kernel(n, far, parts, where_ref, *refs):
    grads, pieces, others = refs[:n], refs[n : 2 * n], refs[2 * n : 3 * n]
    (
        qkv_ref, mix_ref, norms_ref, project_ref, attended_ref, residual_ref, totals_ref, router_ref,
    ) = refs[3 * n : 3 * n + 8]
    sends = refs[3 * n + 8 : 4 * n + 8]
    refs = refs[4 * n + 8 :]
    outs, (x_s, c_s, g_s, n1_s, ga_s, gp_s, tg_s, sums_s, totals_s) = refs[:-9], refs[-9:]
    here = where_ref[0]
    w = pieces[0].shape[1]
    for k in range(n):
        x_s[:, block(here ^ k, w)] = pieces[k][...].astype(F32)
        c_s[:, block(here ^ k, w)] = others[k][1].astype(F32)
        g_s[:, block(here ^ k, w)] = grads[k][...].astype(F32)
    width = n * w
    pairs = width // (2 * HD)
    low = lax.broadcasted_iota(jnp.int32, (1, 2 * HD), 1) < HD
    real = lax.broadcasted_iota(jnp.int32, (ROWS, 1), 0) < SEQ
    scale = HD ** (-0.5)
    sums_s[...] = jnp.zeros_like(sums_s)

    def image(i, carry):
        rows = block(i, ROWS)
        normal2, inverse2 = normalize(residual_ref[rows, :])
        grad_norm2 = g_s[rows, :]
        sums_s[2:3, :] += jnp.sum(grad_norm2 * normal2, axis=0, keepdims=True)
        sums_s[3:4, :] += jnp.sum(grad_norm2, axis=0, keepdims=True)
        grad_resid = c_s[rows, :] + norm_backward(grad_norm2, normal2, inverse2, norms_ref[2:3, :])
        c_s[rows, :] = grad_resid
        grad_attn = grad_resid.astype(BF16)
        ga_s[rows, :] = grad_attn
        tg_s[rows, :] = dot(grad_attn, mix_ref[...], ((1,), (0,))).astype(BF16)

        totals_s[...] = totals_ref[rows, :].T

        def head_pair(pair, carry):
            q_pair, k_pair, v_pair = (
                project_ref[rows, block(j * pairs + pair, 2 * HD)] for j in range(3)
            )
            g_pair = tg_s[rows, block(pair, 2 * HD)]
            got = []
            for head in range(2):
                mine = low if head == 0 else ~low
                q_head = jnp.where(mine, q_pair, jnp.zeros_like(q_pair))
                g_head = jnp.where(mine, g_pair, jnp.zeros_like(g_pair))
                scores = dot(k_pair, q_head, ((1,), (1,))) * scale
                probs = jnp.exp(scores - totals_s[pl.ds(2 * pair + head, 1), :])
                probs = jnp.where(real, probs, 0.0)
                grad_probs = dot(v_pair, g_head, ((1,), (1,)))
                dots = jnp.sum(probs * grad_probs, axis=0, keepdims=True)
                grad_scores = (probs * (grad_probs - dots)).astype(BF16)
                got.append(
                    (
                        dot(grad_scores, k_pair, ((0,), (0,))) * scale,
                        dot(grad_scores, q_pair, ((1,), (0,))) * scale,
                        dot(probs.astype(BF16), g_pair, ((1,), (0,))),
                    )
                )
            for j in range(3):
                out = jnp.where(low, got[0][j], got[1][j])
                gp_s[rows, block(j * pairs + pair, 2 * HD)] = out.astype(BF16)
            return carry

        lax.fori_loop(0, pairs, head_pair, 0, unroll=UNROLL)
        normal1, inverse1 = normalize(x_s[rows, :])
        n1_s[rows, :] = (normal1 * norms_ref[0:1, :] + norms_ref[1:2, :]).astype(BF16)
        grad_norm1 = dot(gp_s[rows, :], qkv_ref[...], ((1,), (0,)))
        sums_s[0:1, :] += jnp.sum(grad_norm1 * normal1, axis=0, keepdims=True)
        sums_s[1:2, :] += jnp.sum(grad_norm1, axis=0, keepdims=True)
        tokens_grad = c_s[rows, :] + norm_backward(
            grad_norm1, normal1, inverse1, norms_ref[0:1, :]
        )
        tg_s[rows, :] = tokens_grad.astype(BF16)
        return carry

    lax.fori_loop(0, x_s.shape[0] // ROWS, image, 0)
    for k in range(n):
        sends[k][...] = tg_s[:, block(here ^ k, w)]
    qkv_grad = dot(gp_s[...], n1_s[...], ((0,), (0,)))
    mix_grad = dot(ga_s[...], attended_ref[...], ((0,), (0,)))
    if parts is None:
        outs[0][...] = qkv_grad
        outs[1][...] = mix_grad
        outs[2][:E, :] = router_ref[...]
        outs[2][E : E + 8, :] = sums_s[...]
        return
    outs, (qkv_s, mix_s, small_s) = outs[:2], outs[2:]
    qkv_s[...] = qkv_grad.astype(BF16)
    mix_s[...] = mix_grad.astype(BF16)
    small_s[...] = jnp.concatenate(
        [router_ref[...], sums_s[...], jnp.zeros((8, width), F32)], axis=0
    ).astype(BF16)
    first, second = parts

    def piece(at, carry):
        k, z = at // far, at % far
        part = block(here ^ k, w)
        for p in range(2):
            c = 2 * (where_ref[1] ^ z) + (where_ref[2] ^ p)
            outs[p][k, z, :first, :] = qkv_s[block(c, first), part]
            outs[p][k, z, first : first + second, :] = mix_s[block(c, second), part]
            outs[p][k, z, first + second :, :] = small_s[:, part]
        return carry

    lax.fori_loop(0, n * far, piece, 0)


def attention_backward(
    where, grads, pieces, others, qkv_t, mix_t, norms, saved, router_part, far, parts
):
    n = len(pieces)
    t, w = pieces[0].shape
    width = n * w
    scratch = [pltpu.VMEM((t, width), F32)] * 3 + [pltpu.VMEM((t, width), BF16)] * 2
    scratch += [pltpu.VMEM((t, 3 * width), BF16), pltpu.VMEM((t, width), BF16)]
    scratch += [pltpu.VMEM((8, width), F32), pltpu.VMEM((128, ROWS), F32)]
    if parts is None:
        outs = (
            shape((3 * width, width), F32),
            shape((width, width), F32),
            shape((E + 8, width), F32),
        )
    else:
        outs = (shape((n, far, sum(parts) + E + 16, w), BF16),) * 2
        scratch = [
            pltpu.VMEM((3 * width, width), BF16),
            pltpu.VMEM((width, width), BF16),
            pltpu.VMEM((E + 16, width), BF16),
        ] + scratch
    out = call(
        partial(backward_kernel, n, far, parts),
        "attention_backward",
        tuple(shape((t, w), BF16) for _ in range(n)) + outs,
        3 * n + 8,
        scalars=1,
        scratch=scratch,
        flops=30 * t * width * width,
        moved=2**23,
    )(where, *grads, *pieces, *others, qkv_t, mix_t, norms, *saved, router_part)
    return out[:n], out[n:]


def split_three(x):
    parts = []
    for _ in range(3):
        part = lax.reduce_precision(x, 8, 7)
        parts.append(part.astype(BF16))
        x = x - part
    return parts


def gather_kernel(n, far, parts, where_ref, *refs):
    qkv_ref, mix_ref, router_ref, norms_ref = refs[2 * n :]
    first, second = parts
    depth = first + second
    w = refs[0].shape[1]
    for k in range(n):
        part = block(where_ref[0] ^ k, w)
        for p in range(2):
            piece = refs[p * n + k]
            for z in range(far):
                c = 2 * (where_ref[1] ^ z) + (where_ref[2] ^ p)
                qkv_ref[block(c, first), part] = piece[z * depth : z * depth + first, :]
                mix_ref[block(c, second), part] = piece[z * depth + first : (z + 1) * depth, :]
        router_ref[:, part] = refs[k][far * depth : far * depth + E, :]
        extra = refs[k][far * depth + E :, :].astype(F32)
        norms_ref[:, part] = extra[0:4] + extra[4:8] + extra[8:12]


def gather_weights(where, pieces, far, parts):
    n = len(pieces) // 2
    _, w = pieces[0].shape
    return call(
        partial(gather_kernel, n, far, parts),
        "gather_weights",
        tuple(shape((2 * far * part, n * w), BF16) for part in parts)
        + (shape((E, n * w), BF16), shape((4, n * w), F32)),
        2 * n,
        scalars=1,
        moved=2**22,
    )(where, *pieces)


def add_core_kernel(own_ref, got_ref, *outs):
    for k, out in enumerate(outs):
        out[...] = (own_ref[k].astype(F32) + got_ref[k].astype(F32)).astype(BF16)


def add_core(own, got):
    return call(
        add_core_kernel,
        "add_core",
        tuple(shape(own.shape[1:], BF16) for _ in range(own.shape[0])),
        2,
        moved=6 * own.size,
        limit=SMALL,
    )(own, got)


def add_rows_kernel(n, *refs):
    pieces, outs = refs[:n], refs[n:]
    for z, out in enumerate(outs):
        out[...] = sum(piece[z].astype(F32) for piece in pieces).astype(BF16)


def add_rows(pieces):
    far, depth, w = pieces[0].shape
    return call(
        partial(add_rows_kernel, len(pieces)),
        "add_rows",
        tuple(shape((depth, w), BF16) for _ in range(far)),
        len(pieces),
        moved=10 * far * depth * w,
        limit=SMALL,
    )(*pieces)


def add_far_kernel(n, parts, *refs):
    pieces, (qkv_ref, mix_ref, small_ref) = refs[:n], refs[n:]
    total = sum(piece[...].astype(F32) for piece in pieces)
    first, second = parts
    qkv_ref[...] = total[:first]
    mix_ref[...] = total[first : first + second]
    small_ref[...] = total[first + second : first + second + E + 8]


def add_far(pieces, parts):
    w = pieces[0].shape[1]
    return call(
        partial(add_far_kernel, len(pieces), parts),
        "add_far",
        tuple(shape((part, w), F32) for part in (*parts, E + 8)),
        len(pieces),
        moved=12 * pieces[0].size,
        limit=SMALL,
    )(*pieces)


def hidden_block(w_ref, i, rows, near):
    m = w_ref.shape[1] // 2
    k = w_ref.shape[2]
    per = near // rows
    chunks = per
    h = k // chunks
    columns = []
    for c in range(per):
        columns.append(
            jnp.concatenate(
                [
                    w_ref[r * near + i * per + c, :m, j * h : (j + 1) * h]
                    for r in range(rows)
                    for j in range(chunks)
                ],
                axis=0,
            )
        )
    w_in = jnp.concatenate(columns, axis=1)
    w_out_t = jnp.concatenate([w_ref[i * near + c, m:, :] for c in range(near)], axis=0)
    return w_in, w_out_t


def assemble(got_ref, rows_s, rows, near):
    w = got_ref.shape[2]
    for c in range(near):
        for r in range(rows):
            rows_s[c * CAP : (c + 1) * CAP, r * w : (r + 1) * w] = got_ref[r * near + c].astype(F32)


def disperse(values_s, sent_ref, rows, near):
    w = sent_ref.shape[2]
    for c in range(near):
        for r in range(rows):
            piece = values_s[c * CAP : (c + 1) * CAP, r * w : (r + 1) * w]
            sent_ref[r * near + c] = piece.astype(BF16)


ERF = (0.254829592, -0.284496736, 1.421413741, -1.453152027, 1.061405429)


def gelu_pair(x):
    size = jnp.abs(x)
    t = 1.0 / (1.0 + (0.3275911 * 0.5**0.5) * size)
    bell = jnp.exp(-0.5 * x * x)
    tail = ERF[4]
    for coefficient in ERF[3::-1]:
        tail = tail * t + coefficient
    tail = (0.5 * tail) * (t * bell)
    below = jnp.where(x < 0, tail, 1.0 - tail)
    return x * below, below + x * bell * (0.5 / math.pi) ** 0.5


def expert_forward_kernel(
    rows, near, e_ref, got_ref, w_ref, router_ref,
    sent_ref, x_ref, act_ref, slope_ref, res_ref, gates_ref, f_s, in_s, out_s,
):
    assemble(got_ref, f_s, rows, near)
    x_ref[...] = f_s[...].astype(BF16)
    logits = dot(x_ref[...], router_ref[...], ((1,), (1,)))
    powers = jnp.exp(logits - jnp.max(logits, axis=1, keepdims=True))
    gates = powers / jnp.sum(powers, axis=1, keepdims=True)
    gates_ref[...] = gates
    res_ref[...] = jnp.zeros_like(res_ref)

    def step(i, carry):
        in_s[...], out_s[...] = hidden_block(w_ref, i, rows, near)

        def tile(j, carry):
            at = block(j, TILE)
            pre = dot(x_ref[at, :], in_s[...], ((1,), (0,)))
            act, slope = gelu_pair(pre)
            act = act.astype(BF16)
            act_ref[i, at, :] = act
            slope_ref[i, at, :] = slope.astype(BF16)
            res_ref[at, :] += dot(act, out_s[...], ((1,), (1,)))
            return carry

        return lax.fori_loop(0, x_ref.shape[0] // TILE, tile, carry)

    lax.fori_loop(0, rows, step, 0)
    own = lax.broadcasted_iota(jnp.int32, (1, E), 1) == e_ref[0]
    chosen = jnp.sum(jnp.where(own, gates, 0.0), axis=1, keepdims=True)
    f_s[...] = chosen * res_ref[...]
    disperse(f_s, sent_ref, rows, near)


def expert_forward(expert, got, w_got, router_t, rows, near):
    e, _, w = got.shape
    n, width, part = near * CAP, rows * w, w_got.shape[2]
    return call(
        partial(expert_forward_kernel, rows, near),
        "expert_forward",
        (
            shape(got.shape, BF16),
            shape((n, width), BF16),
            shape((rows, n, part), BF16),
            shape((rows, n, part), BF16),
            shape((n, width), F32),
            shape((n, E), F32),
        ),
        3,
        scalars=1,
        scratch=[pltpu.VMEM((n, width), F32)] + [pltpu.VMEM((width, part), BF16)] * 2,
        flops=16 * n * width * rows * part // 4,
        moved=2**24,
    )(expert, got, w_got, router_t)


def expert_backward_kernel(
    rows, near, e_ref, got_ref, w_ref, router_ref, x_ref, slope_ref, res_ref, gates_ref,
    sent_ref, pre_ref, grad_res_ref, router_grad_ref, f_s,
):
    assemble(got_ref, f_s, rows, near)
    cot = f_s[...]
    gates = gates_ref[...]
    own = jnp.where(lax.broadcasted_iota(jnp.int32, (1, E), 1) == e_ref[0], 1.0, 0.0)
    chosen = jnp.sum(gates * own, axis=1, keepdims=True)
    grad_chosen = jnp.sum(cot * res_ref[...], axis=1, keepdims=True)
    grad_logits = (grad_chosen * chosen * (own - gates)).astype(BF16)
    grad_res_ref[...] = (chosen * cot).astype(BF16)
    router_grad_ref[...] = dot(grad_logits, x_ref[...], ((0,), (0,)))
    f_s[...] = dot(grad_logits, router_ref[...], ((1,), (0,)))

    def step(i, carry):
        w_in, w_out_t = hidden_block(w_ref, i, rows, near)
        grad_act = dot(grad_res_ref[...], w_out_t, ((1,), (0,)))
        grad_pre = (grad_act * slope_ref[i].astype(F32)).astype(BF16)
        pre_ref[i] = grad_pre
        f_s[...] += dot(grad_pre, w_in, ((1,), (1,)))
        return carry

    lax.fori_loop(0, rows, step, 0)
    disperse(f_s, sent_ref, rows, near)


def expert_backward(expert, got, w_got, router_t, x_rows, slope, res, gates, rows, near):
    e, _, w = got.shape
    n, width, part = near * CAP, rows * w, w_got.shape[2]
    return call(
        partial(expert_backward_kernel, rows, near),
        "expert_backward",
        (
            shape(got.shape, BF16),
            shape((rows, n, part), BF16),
            shape((n, width), BF16),
            shape((E, width), F32),
        ),
        7,
        scalars=1,
        scratch=[pltpu.VMEM((n, width), F32)],
        flops=16 * n * width * rows * part // 4,
        moved=2**24,
    )(expert, got, w_got, router_t, x_rows, slope, res, gates)


def expert_grads_kernel(rows, near, x_ref, pre_ref, grad_res_ref, act_ref, sent_ref):
    m = sent_ref.shape[1] // 2
    k = sent_ref.shape[2]
    per = near // rows
    h = k // per

    def step(i, carry):
        in_grad = dot(x_ref[...], pre_ref[i], ((0,), (0,))).astype(BF16)
        for r in range(rows):
            for c in range(per):
                for j in range(per):
                    first = (r * per + j) * m
                    sent_ref[r * near + i * per + c, :m, j * h : (j + 1) * h] = in_grad[
                        first : first + m, c * h : (c + 1) * h
                    ]
        out_grad_t = dot(grad_res_ref[...], act_ref[i], ((0,), (0,))).astype(BF16)
        for c in range(near):
            sent_ref[i * near + c, m:, :] = out_grad_t[c * m : (c + 1) * m, :]
        return carry

    lax.fori_loop(0, rows, step, 0)


def expert_grads(x_rows, grad_pre, grad_res, act, like, rows, near):
    n, width = x_rows.shape
    return call(
        partial(expert_grads_kernel, rows, near),
        "expert_grads",
        shape(like.shape, BF16),
        4,
        flops=4 * n * width * rows * like.shape[2],
        moved=2**24,
    )(x_rows, grad_pre, grad_res, act)


def local(
    tokens,
    ln1_gain,
    ln1_bias,
    qkv_weight,
    out_weight,
    ln2_gain,
    ln2_bias,
    router_weight,
    expert_in,
    expert_out,
    routes,
    keep,
    cotangent,
):
    rows, cols = lax.axis_size("row"), lax.axis_size("col")
    groups, near = col_groups()
    width_part = tokens.shape[1]
    width = width_part * rows
    hid_part = expert_in.shape[2]
    out_part = expert_out.shape[2]
    qkv_part, mix_part = qkv_weight.shape[1], out_weight.shape[1]
    chunks = width_part // out_part
    half = cols // 2
    parts = (qkv_part, mix_part)
    tiled = half <= 8 and all(part % 16 == 0 for part in (out_part, *parts))
    row, col = lax.axis_index("row"), lax.axis_index("col")
    here = jnp.stack([row, col // 2, col % 2]).astype(jnp.int32)
    nowhere = jnp.zeros((1,), jnp.int32)
    expert = (row * near + col % near).astype(jnp.int32)[None]

    near_parts = jnp.concatenate([qkv_weight.T, out_weight.T], axis=0)
    norms = jnp.stack([ln1_gain, ln1_bias, ln2_gain, ln2_bias])
    if tiled:
        shared = [router_weight.T, *split_three(norms), jnp.zeros_like(norms, BF16)]
        far = jnp.concatenate(far_swap([near_parts] * half) + shared)
    else:
        far = far_spread(near_parts)
    tok = pad_images(after(tokens, near_parts))
    cot = pad_images(after(cotangent, near_parts))
    pieces = row_swap(for_rows(tok.reshape(rows, -1, width_part)))
    cot_pieces = for_rows(cot.reshape(rows, -1, width_part))
    out_t = expert_out.transpose(0, 2, 1)
    if tiled:
        w_sent = pack_weights(expert_in, out_t)
    else:
        w_sent = jnp.concatenate([pack_in(expert_in, chunks), out_t], axis=1)
    w_got = exchange(after(w_sent, far))
    w_got = all_experts(w_got, rows, near, chunks)
    if tiled:
        mine = row_swap([far] * rows)
        qkv_t, mix_t, router_t, norms = gather_weights(
            here, mine + [core_swap(x) for x in mine], half, parts
        )
    else:
        small = gather_all(far)
        qkv_t = small[:, :, :qkv_part].transpose(1, 2, 0, 3).reshape(3 * width, width)
        mix_t = small[:, :, qkv_part:].transpose(1, 2, 0, 3).reshape(width, width)
        norms = row_spread(jnp.concatenate([norms, router_weight.T.astype(F32)]))
        norms = norms.transpose(1, 0, 2).reshape(4 + E, width)
        router_t = norms[4:].astype(BF16)
        norms = norms[:4]

    routes_t = jnp.pad(
        routes.T.reshape(2, -1, SEQ), ((0, 0), (0, 0), (0, ROWS - SEQ)), constant_values=-1
    ).reshape(2, -1)
    keep_t = jnp.pad(keep.T.reshape(2, -1, SEQ), ((0, 0), (0, 0), (0, ROWS - SEQ))).reshape(2, -1)
    slots = slot_table(routes_t, keep_t)
    columns = slots.T

    sends, laters, saved = attention_forward(here, pieces, cot_pieces, qkv_t, mix_t, norms)
    normed = row_swap(sends)
    others = row_swap(laters)

    def to_experts(x, *earlier):
        return exchange(after(x.reshape(E, CAP, width_part), *earlier))

    x_got = to_experts(dispatch(here, slots, normed), w_got, columns)
    cot_got = to_experts(dispatch(nowhere, slots, [cot]), x_got, *others)
    moved, x_rows, act, slope, res, gates = expert_forward(
        expert, x_got, w_got, router_t, rows, near
    )
    moved = to_experts(moved, cot_got).reshape(E * CAP, width_part)
    grads, grad_pre, grad_res, router_part = expert_backward(
        expert, cot_got, w_got, router_t, x_rows, slope, res, gates, rows, near
    )
    grads = to_experts(grads, moved).reshape(E * CAP, width_part)
    w_grads = expert_grads(x_rows, grad_pre, grad_res, act, w_got, rows, near)
    w_grads = exchange(after(own_experts(w_grads, rows, near, chunks), grads))
    if tiled:
        expert_in_grad, out_grad_t = unpack_grads(w_grads, width_part, hid_part)
    else:
        expert_in_grad = unpack_in(w_grads[:, :out_part], chunks).astype(F32)
        out_grad_t = w_grads[:, out_part:].astype(F32)
    expert_out_grad = out_grad_t.transpose(0, 2, 1)

    back = row_swap(combine(here, columns, grads, rows))
    layer_out = cut_images(finish(here, columns, moved, tok, others))
    back[0] = after(back[0], layer_out)
    sends, outs = attention_backward(
        here, back, pieces, others, qkv_t, mix_t, norms, saved, router_part, half, parts if tiled else None
    )

    if tiled:
        own, other = outs
        mine = add_core(own, core_swap(other))
        sends = [after(x, mine) for x in sends]
        got = far_swap(add_rows(row_swap(mine)))
        got[0] = after(got[0], expert_in_grad)
        qkv_grad, mix_grad, tail = add_far(got, parts)
    else:
        qkv_grad_t, mix_grad_t, tail = outs
        shares = jnp.concatenate(
            [
                qkv_grad_t.reshape(cols, qkv_part, width),
                mix_grad_t.reshape(cols, mix_part, width),
                jnp.broadcast_to(tail[None], (cols,) + tail.shape),
            ],
            axis=1,
        )
        sums = reduce_all(shares)
        qkv_grad, mix_grad, tail = jnp.split(sums, [qkv_part, qkv_part + mix_part])
    thin = width_part // cols
    tail = lax.dynamic_slice_in_dim(tail, col * thin, thin, axis=1)
    tokens_grad = jnp.concatenate(in_order(row_swap(sends), row), axis=0)
    tokens_grad = cut_images(tokens_grad).astype(F32)
    return (
        layer_out,
        tokens_grad,
        tail[E],
        tail[E + 1],
        qkv_grad.T,
        mix_grad.T,
        tail[E + 2],
        tail[E + 3],
        tail[:E].T,
        expert_in_grad,
        expert_out_grad,
    )


def solution(mesh):
    in_specs = (
        P("col", "row"),
        P("row"),
        P("row"),
        P("row", "col"),
        P("row", "col"),
        P("row"),
        P("row"),
        P("row", None),
        P(None, "row", "col"),
        P(None, "row", "col"),
        P("col", None),
        P("col", None),
        P("col", "row"),
    )
    out_specs = (
        P("col", "row"),
        P("col", "row"),
        P(("row", "col")),
        P(("row", "col")),
        P("row", "col"),
        P("row", "col"),
        P(("row", "col")),
        P(("row", "col")),
        P(("row", "col"), None),
        P(None, "row", "col"),
        P(None, "row", "col"),
    )
    return jax.shard_map(local, mesh=mesh, in_specs=in_specs, out_specs=out_specs, check_vma=False)
```

```python
import math
from functools import partial

import jax
import jax.numpy as jnp
from jax import lax
from jax.experimental import pallas as pl
from jax.experimental.pallas import tpu as pltpu
from jax.sharding import PartitionSpec as P

E = 32
SEQ = 197
ROWS = 208
HD = 64
CAP = 120
EPS_NORM = 1e-06
VMEM = 60 * 2**20
SMALL = 24 * 2**20
TILE = 480
UNROLL = 4
F32 = jnp.float32
BF16 = jnp.bfloat16

def dot(a, b, dims):
    return lax.dot_general(a, b, (dims, ((), ())), preferred_element_type=F32)


def col_groups():
    rows, cols = lax.axis_size("row"), lax.axis_size("col")
    near = E // rows
    return cols // near, near


def exchange(pieces):
    groups, near = col_groups()
    if groups == 1:
        return lax.all_to_all(pieces, ("row", "col"), 0, 0, tiled=True)
    rows = lax.axis_size("row")
    index = [[g * near + c for c in range(near)] for g in range(groups)]
    parts = pieces.reshape((rows, near) + pieces.shape[1:])
    parts = lax.all_to_all(parts, "row", 0, 0, tiled=True)
    parts = lax.all_to_all(parts, "col", 1, 1, tiled=True, axis_index_groups=index)
    return parts.reshape(pieces.shape)


def far_groups():
    groups, near = col_groups()
    return [[g * near + c for g in range(groups)] for c in range(near)]


def collect_far(x):
    if col_groups()[0] == 1:
        return x[None]
    return lax.all_gather(x, "col", axis=0, axis_index_groups=far_groups())


def reduce_far(x):
    if col_groups()[0] == 1:
        return x[0]
    return lax.psum_scatter(x, "col", scatter_dimension=0, axis_index_groups=far_groups())


def after(x, *earlier):
    return lax.optimization_barrier((x,) + earlier)[0]


def swaps(axis, distance):
    return [(i, i ^ distance) for i in range(lax.axis_size(axis))]


def pick(pieces, at):
    return lax.dynamic_index_in_dim(pieces, at, 0, keepdims=False)


def in_order(got, here):
    pieces, step = list(got), 1
    while step < len(pieces):
        odd = (here & step) != 0
        pieces = [jnp.where(odd, pieces[k ^ step], pieces[k]) for k in range(len(pieces))]
        step *= 2
    return pieces


def row_exchange(pieces):
    here = lax.axis_index("row")
    got = [pick(pieces, here)]
    for k in range(1, lax.axis_size("row")):
        got.append(lax.ppermute(pick(pieces, here ^ k), "row", swaps("row", k)))
    return in_order(got, here)


def row_swap(pieces):
    got = [lax.ppermute(x, "row", swaps("row", k)) for k, x in enumerate(pieces) if k]
    return [pieces[0]] + got


def for_rows(x):
    here = lax.axis_index("row")
    return [pick(x, here ^ k) for k in range(x.shape[0])]


def row_spread(x):
    got = [x] + [lax.ppermute(x, "row", swaps("row", k)) for k in range(1, lax.axis_size("row"))]
    return jnp.stack(in_order(got, lax.axis_index("row")))


def far_swap(pieces):
    got = [lax.ppermute(x, "col", swaps("col", 2 * k)) for k, x in enumerate(pieces) if k]
    return [pieces[0]] + got


def core_swap(x):
    return lax.ppermute(x, "col", swaps("col", 1))


def parity_groups():
    cols = lax.axis_size("col")
    return [[2 * i + k for i in range(cols // 2)] for k in range(2)]


def far_spread(x):
    half = lax.axis_size("col") // 2
    if half > 8:
        return lax.all_gather(x, "col", axis=0, axis_index_groups=parity_groups())
    got = [x] + [lax.ppermute(x, "col", swaps("col", 2 * k)) for k in range(1, half)]
    return jnp.stack(in_order(got, lax.axis_index("col") // 2))


def far_sum(pieces):
    half = lax.axis_size("col") // 2
    if half > 8:
        got = lax.all_to_all(pieces, "col", 0, 0, tiled=True, axis_index_groups=parity_groups())
        return jnp.sum(got.astype(F32), axis=0)
    here = lax.axis_index("col") // 2
    total = pick(pieces, here).astype(F32)
    for k in range(1, half):
        sent = lax.ppermute(pick(pieces, here ^ k), "col", swaps("col", 2 * k))
        total = total + sent.astype(F32)
    return total


def gather_all(x):
    half = lax.axis_size("col") // 2
    mine = row_spread(x)
    other = lax.ppermute(mine, "col", swaps("col", 1))
    first = lax.axis_index("col") % 2 == 0
    both = jnp.stack([jnp.where(first, mine, other), jnp.where(first, other, mine)], axis=2)
    return both.reshape((both.shape[0], 2 * half) + x.shape[1:])


def reduce_all(x):
    cols, n, width = x.shape
    rows = lax.axis_size("row")
    core = lax.axis_index("col") % 2
    pairs = x.reshape(cols // 2, 2, n, width).transpose(1, 0, 2, 3).astype(BF16)
    sent = lax.ppermute(pick(pairs, 1 - core), "col", swaps("col", 1))
    mine = pick(pairs, core).astype(F32) + sent.astype(F32)
    mine = mine.astype(BF16).reshape(cols // 2, n, rows, width // rows).transpose(2, 0, 1, 3)
    mine = sum(piece.astype(F32) for piece in row_exchange(mine))
    return far_sum(mine.astype(BF16))


def pack_in(x, chunks):
    e, n, h = x.shape
    return x.reshape(e, chunks, n // chunks, h).transpose(0, 2, 1, 3).reshape(e, n // chunks, -1)


def unpack_in(x, chunks):
    e, n, h = x.shape
    x = x.reshape(e, n, chunks, h // chunks).transpose(0, 2, 1, 3)
    return x.reshape(e, n * chunks, h // chunks)


def pack_in(x, chunks):
    e, n, h = x.shape
    return x.reshape(e, chunks, n // chunks, h).transpose(0, 2, 1, 3).reshape(e, n // chunks, -1)


def unpack_in(x, chunks):
    e, n, h = x.shape
    x = x.reshape(e, n, chunks, h // chunks).transpose(0, 2, 1, 3)
    return x.reshape(e, n * chunks, h // chunks)


def all_experts(got, rows, near, chunks):
    groups = col_groups()[0]
    if groups == 1:
        return got
    m = got.shape[1] // 2
    k = got.shape[2]
    w_in = unpack_in(got[:, :m], chunks)
    _, n, h = w_in.shape
    w_in = collect_far(w_in.reshape(rows, near, n, h)).transpose(1, 3, 0, 2, 4)
    w_in = w_in.reshape(rows, n, near, groups * h).transpose(0, 2, 1, 3).reshape(E, n, groups * h)
    w_out_t = collect_far(got[:, m:].reshape(rows, near, m, k)).transpose(1, 0, 2, 3, 4)
    w_out_t = w_out_t.reshape(E, groups * m, k)
    return jnp.concatenate([pack_in(w_in, near // rows), w_out_t], axis=1)


def own_experts(sent, rows, near, chunks):
    groups = col_groups()[0]
    if groups == 1:
        return sent
    m = sent.shape[1] // 2
    k = sent.shape[2]
    w_in = unpack_in(sent[:, :m], near // rows)
    _, n, h = w_in.shape
    w_in = w_in.reshape(rows, near, n, h).transpose(0, 2, 1, 3)
    w_in = w_in.reshape(rows, n, groups, near, h // groups).transpose(2, 0, 3, 1, 4)
    w_in = reduce_far(w_in).reshape(E, n, h // groups)
    w_out_t = sent[:, m:].reshape(rows, groups, near, m // groups, k).transpose(1, 0, 2, 3, 4)
    w_out_t = reduce_far(w_out_t).reshape(E, m // groups, k)
    return jnp.concatenate([pack_in(w_in, chunks), w_out_t], axis=1)


def pad_images(x):
    t, w = x.shape
    return jnp.pad(x.reshape(t // SEQ, SEQ, w), ((0, 0), (0, ROWS - SEQ), (0, 0))).reshape(-1, w)


def cut_images(x):
    t, w = x.shape
    return x.reshape(t // ROWS, ROWS, w)[:, :SEQ].reshape(-1, w)


def call(kernel, name, out_shape, n_in, scalars=0, scratch=(), flops=0, moved=0, limit=VMEM, **kw):
    smem = pl.BlockSpec(memory_space=pltpu.SMEM)
    vmem = pl.BlockSpec(memory_space=pltpu.VMEM)
    return pl.pallas_call(
        kernel,
        name=name,
        out_shape=out_shape,
        in_specs=[smem] * scalars + [vmem] * n_in,
        out_specs=jax.tree.map(lambda _: vmem, out_shape),
        scratch_shapes=list(scratch),
        compiler_params=pltpu.CompilerParams(vmem_limit_bytes=limit),
        cost_estimate=pl.CostEstimate(flops=flops, bytes_accessed=moved, transcendentals=0),
        **kw,
    )


def shape(dims, dtype):
    return jax.ShapeDtypeStruct(tuple(dims), dtype)


def block(i, n):
    if isinstance(i, int):
        return slice(i * n, (i + 1) * n)
    return pl.ds(pl.multiple_of(i * n, n), n)


def pack_kernel(chunks, in_ref, out_ref, sent_ref):
    n = in_ref.shape[1] // chunks
    h = in_ref.shape[2]
    for c in range(chunks):
        sent_ref[:, :n, c * h : (c + 1) * h] = in_ref[:, c * n : (c + 1) * n, :]
    sent_ref[:, n:, :] = out_ref[...]


def unpack_kernel(chunks, got_ref, in_ref, out_ref):
    n = in_ref.shape[1] // chunks
    h = in_ref.shape[2]
    for c in range(chunks):
        in_ref[:, c * n : (c + 1) * n, :] = got_ref[:, :n, c * h : (c + 1) * h].astype(F32)
    out_ref[...] = got_ref[:, n:, :].astype(F32)


def pack_weights(w_in, w_out_t):
    e, n, h = w_in.shape
    _, m, k = w_out_t.shape
    step = 16
    spec = lambda a, b: pl.BlockSpec((step, a, b), lambda i: (i, 0, 0))
    return pl.pallas_call(
        partial(pack_kernel, n // m),
        name="pack_weights",
        grid=(e // step,),
        out_shape=shape((e, 2 * m, k), BF16),
        in_specs=[spec(n, h), spec(m, k)],
        out_specs=spec(2 * m, k),
        compiler_params=pltpu.CompilerParams(vmem_limit_bytes=VMEM),
        cost_estimate=pl.CostEstimate(flops=0, bytes_accessed=8 * e * m * k, transcendentals=0),
    )(w_in, w_out_t)


def unpack_grads(got, n, h):
    e, m2, k = got.shape
    m = m2 // 2
    step = 16
    spec = lambda a, b: pl.BlockSpec((step, a, b), lambda i: (i, 0, 0))
    return pl.pallas_call(
        partial(unpack_kernel, n // m),
        name="unpack_grads",
        grid=(e // step,),
        out_shape=(shape((e, n, h), F32), shape((e, m, k), F32)),
        in_specs=[spec(m2, k)],
        out_specs=(spec(n, h), spec(m, k)),
        compiler_params=pltpu.CompilerParams(vmem_limit_bytes=VMEM),
        cost_estimate=pl.CostEstimate(flops=0, bytes_accessed=12 * e * m * k, transcendentals=0),
    )(got)


def slots_kernel(routes_ref, keep_ref, slots_ref):
    tokens = routes_ref.shape[1]
    experts = lax.broadcasted_iota(jnp.int32, (E, tokens), 0)
    named = [experts == routes_ref[j : j + 1, :] for j in range(2)]
    both = jnp.where(named[0] | named[1], 1.0, 0.0).astype(BF16)
    width = 128
    upper = lax.broadcasted_iota(jnp.int32, (width, width), 0) < lax.broadcasted_iota(
        jnp.int32, (width, width), 1
    )
    upper = jnp.where(upper, 1.0, 0.0).astype(BF16)
    before = jnp.zeros((E, 1), F32)
    counts = []
    for i in range(tokens // width):
        part = both[:, i * width : (i + 1) * width]
        counts.append(dot(part, upper, ((1,), (0,))) + before)
        before = before + jnp.sum(part.astype(F32), axis=1, keepdims=True)
    place = jnp.concatenate(counts, axis=1) + (experts * CAP).astype(F32)
    for j in range(2):
        slot = jnp.sum(jnp.where(named[j], place, 0.0), axis=0, keepdims=True).astype(jnp.int32)
        slots_ref[j : j + 1, :] = jnp.where(keep_ref[j : j + 1, :] != 0, slot, -1)


def slot_table(routes, keep):
    return call(slots_kernel, "slots", shape(routes.shape, jnp.int32), 2, limit=SMALL)(routes, keep)


def dispatch_kernel(n, where_ref, slots_ref, *refs):
    pieces, (sent_ref, values) = refs[:n], refs[n:]
    here = where_ref[0]
    part = pieces[0].shape[0]
    for k in range(n):
        values[block(here ^ k, part), :] = pieces[k][...]
    tokens = values.shape[0]
    step = 4

    def experts(i, carry):
        hits = []
        for j in range(step):
            first = (i * step + j) * CAP
            place = [slots_ref[p : p + 1, :] - first for p in range(2)]
            mine = [(p >= 0) & (p < CAP) for p in place]
            at = jnp.where(mine[0], place[0], jnp.where(mine[1], place[1], -1))
            rows = lax.broadcasted_iota(jnp.int32, (CAP, tokens), 0)
            hits.append(jnp.where(rows == at, 1.0, 0.0))
        hits = jnp.concatenate(hits, axis=0).astype(BF16)
        out = dot(hits, values[...], ((1,), (0,))).astype(BF16)
        sent_ref[block(i, step * CAP), :] = out
        return carry

    lax.fori_loop(0, E // step, experts, 0)


def dispatch(here, slots, pieces):
    n = len(pieces)
    part, w = pieces[0].shape
    return call(
        partial(dispatch_kernel, n),
        "dispatch",
        shape((E * CAP, w), BF16),
        1 + n,
        scalars=1,
        scratch=[pltpu.VMEM((n * part, w), BF16)],
        flops=2 * E * CAP * n * part * w,
        moved=2 * (E * CAP + n * part) * w,
        limit=SMALL,
    )(here, slots, *pieces)


def combine_rows(columns, got_ref):
    places = lax.broadcasted_iota(jnp.int32, (columns.shape[0], E * CAP), 1)
    hits = (places == columns[:, 0:1]) | (places == columns[:, 1:2])
    hits = jnp.where(hits, 1.0, 0.0).astype(BF16)
    return dot(hits, got_ref[...], ((1,), (0,)))


def combine_kernel(n, where_ref, columns_ref, got_ref, *outs):
    here = where_ref[0]
    part = outs[0].shape[0]
    tile = part // 2
    for k in range(n):
        base = (here ^ k) * part
        for half in range(2):
            rows = pl.ds(pl.multiple_of(base + half * tile, tile), tile)
            out = combine_rows(columns_ref[rows, :], got_ref)
            outs[k][half * tile : (half + 1) * tile, :] = out.astype(BF16)


def combine(here, columns, got, n):
    w = got.shape[1]
    part = columns.shape[0] // n
    return call(
        partial(combine_kernel, n),
        "combine",
        tuple(shape((part, w), BF16) for _ in range(n)),
        2,
        scalars=1,
        flops=2 * E * CAP * n * part * w,
        moved=2 * (E * CAP + n * part) * w,
        limit=SMALL,
    )(here, columns, got)


def finish_kernel(n, where_ref, columns_ref, got_ref, tokens_ref, *refs):
    pieces, (out_ref,) = refs[:n], refs[n:]
    here = where_ref[0]
    part = pieces[0].shape[1]
    tile = part // 2
    for k in range(n):
        base = (here ^ k) * part
        for half in range(2):
            rows = pl.ds(pl.multiple_of(base + half * tile, tile), tile)
            out = combine_rows(columns_ref[rows, :], got_ref)
            out = out + pieces[k][0, half * tile : (half + 1) * tile, :].astype(F32)
            out = out + tokens_ref[rows, :].astype(F32)
            out_ref[rows, :] = out.astype(BF16)


def finish(here, columns, got, tokens, pieces):
    n = len(pieces)
    t, w = tokens.shape
    return call(
        partial(finish_kernel, n),
        "finish",
        shape((t, w), BF16),
        3 + n,
        scalars=1,
        flops=2 * E * CAP * t * w,
        moved=2 * (E * CAP + 3 * t) * w,
        limit=SMALL,
    )(here, columns, got, tokens, *pieces)


def means(x):
    return jnp.mean(x, axis=1, keepdims=True)


def normalize(values):
    centred = values - means(values)
    inverse = lax.rsqrt(means(centred * centred) + EPS_NORM)
    return centred * inverse, inverse


def norm_backward(grad_normed, normalized, inverse, gain):
    scaled = grad_normed * gain
    return inverse * (scaled - means(scaled) - normalized * means(scaled * normalized))


def head_scores(q_pair, k_pair, low, head):
    keys = k_pair.shape[0]
    q_head = jnp.where(low if head % 2 == 0 else ~low, q_pair, jnp.zeros_like(q_pair))
    scores = dot(q_head, k_pair, ((1,), (1,))) * HD ** (-0.5)
    real = lax.broadcasted_iota(jnp.int32, (1, keys), 1) < SEQ
    return jnp.where(real, scores, -1e30)


def forward_kernel(n, where_ref, *refs):
    pieces, others = refs[:n], refs[n : 2 * n]
    qkv_ref, mix_ref, norms_ref = refs[2 * n : 2 * n + 3]
    sends, laters = refs[2 * n + 3 : 3 * n + 3], refs[3 * n + 3 : 4 * n + 3]
    project_ref, attended_ref, residual_ref, totals_ref, x_s, n2_s, ao_s = refs[4 * n + 3 :]
    here = where_ref[0]
    w = pieces[0].shape[1]
    for k in range(n):
        x_s[:, block(here ^ k, w)] = pieces[k][...].astype(F32)
    width = n * w
    pairs = width // (2 * HD)
    low = lax.broadcasted_iota(jnp.int32, (1, 2 * HD), 1) < HD
    lanes = lax.broadcasted_iota(jnp.int32, (1, 128), 1)

    def image(i, carry):
        rows = block(i, ROWS)
        normed = normalize(x_s[rows, :])[0] * norms_ref[0:1, :] + norms_ref[1:2, :]
        project_ref[rows, :] = dot(normed.astype(BF16), qkv_ref[...], ((1,), (1,))).astype(BF16)

        def head_pair(pair, totals):
            q_pair, k_pair, v_pair = (
                project_ref[rows, block(j * pairs + pair, 2 * HD)] for j in range(3)
            )
            heads = []
            for head in range(2):
                scores = head_scores(q_pair, k_pair, low, head)
                top = jnp.max(scores, axis=1, keepdims=True)
                powers = jnp.exp(scores - top)
                total = jnp.sum(powers, axis=1, keepdims=True)
                probs = (powers / total).astype(BF16)
                heads.append(dot(probs, v_pair, ((1,), (0,))))
                totals = jnp.where(lanes == 2 * pair + head, top + jnp.log(total), totals)
            mixed = jnp.where(low, heads[0], heads[1])
            attended_ref[rows, block(pair, 2 * HD)] = mixed.astype(BF16)
            return totals

        totals = jnp.zeros((ROWS, 128), F32)
        for pair in range(pairs):
            totals = head_pair(pair, totals)
        totals_ref[rows, :] = totals
        attn_out = dot(attended_ref[rows, :], mix_ref[...], ((1,), (1,)))
        residual = x_s[rows, :] + attn_out
        residual_ref[rows, :] = residual
        normed = normalize(residual)[0] * norms_ref[2:3, :] + norms_ref[3:4, :]
        n2_s[rows, :] = normed.astype(BF16)
        ao_s[rows, :] = attn_out.astype(BF16)
        return carry

    lax.fori_loop(0, x_s.shape[0] // ROWS, image, 0)
    for k in range(n):
        sends[k][...] = n2_s[:, block(here ^ k, w)]
        laters[k][0] = ao_s[:, block(here ^ k, w)]
        laters[k][1] = others[k][...]


def attention_forward(where, pieces, others, qkv_t, mix_t, norms):
    n = len(pieces)
    t, w = pieces[0].shape
    width = n * w
    out = call(
        partial(forward_kernel, n),
        "attention_forward",
        tuple(shape((t, w), BF16) for _ in range(n))
        + tuple(shape((2, t, w), BF16) for _ in range(n))
        + (
            shape((t, 3 * width), BF16),
            shape((t, width), BF16),
            shape((t, width), F32),
            shape((t, 128), F32),
        ),
        2 * n + 3,
        scalars=1,
        scratch=[
            pltpu.VMEM((t, width), F32),
            pltpu.VMEM((t, width), BF16),
            pltpu.VMEM((t, width), BF16),
        ],
        flops=12 * t * width * width,
        moved=2**22,
    )(where, *pieces, *others, qkv_t, mix_t, norms)
    return out[:n], out[n : 2 * n], out[2 * n :]


def backward_kernel(n, far, parts, where_ref, *refs):
    grads, pieces, others = refs[:n], refs[n : 2 * n], refs[2 * n : 3 * n]
    (
        qkv_ref, mix_ref, norms_ref, project_ref, attended_ref, residual_ref, totals_ref, router_ref,
    ) = refs[3 * n : 3 * n + 8]
    sends = refs[3 * n + 8 : 4 * n + 8]
    refs = refs[4 * n + 8 :]
    outs, (x_s, c_s, g_s, n1_s, ga_s, gp_s, tg_s, sums_s, totals_s) = refs[:-9], refs[-9:]
    here = where_ref[0]
    w = pieces[0].shape[1]
    for k in range(n):
        x_s[:, block(here ^ k, w)] = pieces[k][...].astype(F32)
        c_s[:, block(here ^ k, w)] = others[k][1].astype(F32)
        g_s[:, block(here ^ k, w)] = grads[k][...].astype(F32)
    width = n * w
    pairs = width // (2 * HD)
    low = lax.broadcasted_iota(jnp.int32, (1, 2 * HD), 1) < HD
    real = lax.broadcasted_iota(jnp.int32, (ROWS, 1), 0) < SEQ
    scale = HD ** (-0.5)
    sums_s[...] = jnp.zeros_like(sums_s)

    def image(i, carry):
        rows = block(i, ROWS)
        normal2, inverse2 = normalize(residual_ref[rows, :])
        grad_norm2 = g_s[rows, :]
        sums_s[2:3, :] += jnp.sum(grad_norm2 * normal2, axis=0, keepdims=True)
        sums_s[3:4, :] += jnp.sum(grad_norm2, axis=0, keepdims=True)
        grad_resid = c_s[rows, :] + norm_backward(grad_norm2, normal2, inverse2, norms_ref[2:3, :])
        c_s[rows, :] = grad_resid
        grad_attn = grad_resid.astype(BF16)
        ga_s[rows, :] = grad_attn
        tg_s[rows, :] = dot(grad_attn, mix_ref[...], ((1,), (0,))).astype(BF16)

        totals_s[...] = totals_ref[rows, :].T

        def head_pair(pair, carry):
            q_pair, k_pair, v_pair = (
                project_ref[rows, block(j * pairs + pair, 2 * HD)] for j in range(3)
            )
            g_pair = tg_s[rows, block(pair, 2 * HD)]
            got = []
            for head in range(2):
                mine = low if head == 0 else ~low
                q_head = jnp.where(mine, q_pair, jnp.zeros_like(q_pair))
                g_head = jnp.where(mine, g_pair, jnp.zeros_like(g_pair))
                scores = dot(k_pair, q_head, ((1,), (1,))) * scale
                probs = jnp.exp(scores - totals_s[pl.ds(2 * pair + head, 1), :])
                probs = jnp.where(real, probs, 0.0)
                grad_probs = dot(v_pair, g_head, ((1,), (1,)))
                dots = jnp.sum(probs * grad_probs, axis=0, keepdims=True)
                grad_scores = (probs * (grad_probs - dots)).astype(BF16)
                got.append(
                    (
                        dot(grad_scores, k_pair, ((0,), (0,))) * scale,
                        dot(grad_scores, q_pair, ((1,), (0,))) * scale,
                        dot(probs.astype(BF16), g_pair, ((1,), (0,))),
                    )
                )
            for j in range(3):
                out = jnp.where(low, got[0][j], got[1][j])
                gp_s[rows, block(j * pairs + pair, 2 * HD)] = out.astype(BF16)
            return carry

        lax.fori_loop(0, pairs, head_pair, 0, unroll=UNROLL)
        normal1, inverse1 = normalize(x_s[rows, :])
        n1_s[rows, :] = (normal1 * norms_ref[0:1, :] + norms_ref[1:2, :]).astype(BF16)
        grad_norm1 = dot(gp_s[rows, :], qkv_ref[...], ((1,), (0,)))
        sums_s[0:1, :] += jnp.sum(grad_norm1 * normal1, axis=0, keepdims=True)
        sums_s[1:2, :] += jnp.sum(grad_norm1, axis=0, keepdims=True)
        tokens_grad = c_s[rows, :] + norm_backward(
            grad_norm1, normal1, inverse1, norms_ref[0:1, :]
        )
        tg_s[rows, :] = tokens_grad.astype(BF16)
        return carry

    lax.fori_loop(0, x_s.shape[0] // ROWS, image, 0)
    for k in range(n):
        sends[k][...] = tg_s[:, block(here ^ k, w)]
    qkv_grad = dot(gp_s[...], n1_s[...], ((0,), (0,)))
    mix_grad = dot(ga_s[...], attended_ref[...], ((0,), (0,)))
    if parts is None:
        outs[0][...] = qkv_grad
        outs[1][...] = mix_grad
        outs[2][:E, :] = router_ref[...]
        outs[2][E : E + 8, :] = sums_s[...]
        return
    outs, (qkv_s, mix_s, small_s) = outs[:2], outs[2:]
    qkv_s[...] = qkv_grad.astype(BF16)
    mix_s[...] = mix_grad.astype(BF16)
    small_s[...] = jnp.concatenate(
        [router_ref[...], sums_s[...], jnp.zeros((8, width), F32)], axis=0
    ).astype(BF16)
    first, second = parts

    def piece(at, carry):
        k, z = at // far, at % far
        part = block(here ^ k, w)
        for p in range(2):
            c = 2 * (where_ref[1] ^ z) + (where_ref[2] ^ p)
            outs[p][k, z, :first, :] = qkv_s[block(c, first), part]
            outs[p][k, z, first : first + second, :] = mix_s[block(c, second), part]
            outs[p][k, z, first + second :, :] = small_s[:, part]
        return carry

    lax.fori_loop(0, n * far, piece, 0)


def attention_backward(
    where, grads, pieces, others, qkv_t, mix_t, norms, saved, router_part, far, parts
):
    n = len(pieces)
    t, w = pieces[0].shape
    width = n * w
    scratch = [pltpu.VMEM((t, width), F32)] * 3 + [pltpu.VMEM((t, width), BF16)] * 2
    scratch += [pltpu.VMEM((t, 3 * width), BF16), pltpu.VMEM((t, width), BF16)]
    scratch += [pltpu.VMEM((8, width), F32), pltpu.VMEM((128, ROWS), F32)]
    if parts is None:
        outs = (
            shape((3 * width, width), F32),
            shape((width, width), F32),
            shape((E + 8, width), F32),
        )
    else:
        outs = (shape((n, far, sum(parts) + E + 16, w), BF16),) * 2
        scratch = [
            pltpu.VMEM((3 * width, width), BF16),
            pltpu.VMEM((width, width), BF16),
            pltpu.VMEM((E + 16, width), BF16),
        ] + scratch
    out = call(
        partial(backward_kernel, n, far, parts),
        "attention_backward",
        tuple(shape((t, w), BF16) for _ in range(n)) + outs,
        3 * n + 8,
        scalars=1,
        scratch=scratch,
        flops=30 * t * width * width,
        moved=2**23,
    )(where, *grads, *pieces, *others, qkv_t, mix_t, norms, *saved, router_part)
    return out[:n], out[n:]


def split_three(x):
    parts = []
    for _ in range(3):
        part = lax.reduce_precision(x, 8, 7)
        parts.append(part.astype(BF16))
        x = x - part
    return parts


def gather_kernel(n, far, parts, where_ref, *refs):
    qkv_ref, mix_ref, router_ref, norms_ref = refs[2 * n :]
    first, second = parts
    depth = first + second
    w = refs[0].shape[1]
    for k in range(n):
        part = block(where_ref[0] ^ k, w)
        for p in range(2):
            piece = refs[p * n + k]
            for z in range(far):
                c = 2 * (where_ref[1] ^ z) + (where_ref[2] ^ p)
                qkv_ref[block(c, first), part] = piece[z * depth : z * depth + first, :]
                mix_ref[block(c, second), part] = piece[z * depth + first : (z + 1) * depth, :]
        router_ref[:, part] = refs[k][far * depth : far * depth + E, :]
        extra = refs[k][far * depth + E :, :].astype(F32)
        norms_ref[:, part] = extra[0:4] + extra[4:8] + extra[8:12]


def gather_weights(where, pieces, far, parts):
    n = len(pieces) // 2
    _, w = pieces[0].shape
    return call(
        partial(gather_kernel, n, far, parts),
        "gather_weights",
        tuple(shape((2 * far * part, n * w), BF16) for part in parts)
        + (shape((E, n * w), BF16), shape((4, n * w), F32)),
        2 * n,
        scalars=1,
        moved=2**22,
    )(where, *pieces)


def add_core_kernel(own_ref, got_ref, *outs):
    for k, out in enumerate(outs):
        out[...] = (own_ref[k].astype(F32) + got_ref[k].astype(F32)).astype(BF16)


def add_core(own, got):
    return call(
        add_core_kernel,
        "add_core",
        tuple(shape(own.shape[1:], BF16) for _ in range(own.shape[0])),
        2,
        moved=6 * own.size,
        limit=SMALL,
    )(own, got)


def add_rows_kernel(n, *refs):
    pieces, outs = refs[:n], refs[n:]
    for z, out in enumerate(outs):
        out[...] = sum(piece[z].astype(F32) for piece in pieces).astype(BF16)


def add_rows(pieces):
    far, depth, w = pieces[0].shape
    return call(
        partial(add_rows_kernel, len(pieces)),
        "add_rows",
        tuple(shape((depth, w), BF16) for _ in range(far)),
        len(pieces),
        moved=10 * far * depth * w,
        limit=SMALL,
    )(*pieces)


def add_far_kernel(n, parts, thin, where_ref, *refs):
    pieces, (qkv_ref, mix_ref, router_ref, *norm_refs) = refs[:n], refs[n:]
    total = sum(piece[...].astype(F32) for piece in pieces)
    first, second = parts
    qkv_ref[...] = total[:first]
    mix_ref[...] = total[first : first + second]
    tail = total[first + second : first + second + E + 8]
    w = tail.shape[1]
    col = 2 * where_ref[1] + where_ref[2]
    tail = pltpu.roll(tail, lax.rem(w - col * thin, w), 1)
    router_ref[...] = tail[:E].T[:thin]
    for j, norm_ref in enumerate(norm_refs):
        norm_ref[...] = tail[E + j : E + j + 1, :thin]


def add_far(where, pieces, parts, thin):
    w = pieces[0].shape[1]
    return call(
        partial(add_far_kernel, len(pieces), parts, thin),
        "add_far",
        tuple(shape((part, w), F32) for part in parts)
        + (shape((thin, E), F32),)
        + tuple(shape((1, thin), F32) for _ in range(4)),
        len(pieces),
        scalars=1,
        moved=12 * pieces[0].size,
        limit=SMALL,
    )(where, *pieces)


def hidden_block(w_ref, i, rows, near):
    m = w_ref.shape[1] // 2
    k = w_ref.shape[2]
    per = near // rows
    chunks = per
    h = k // chunks
    columns = []
    for c in range(per):
        columns.append(
            jnp.concatenate(
                [
                    w_ref[r * near + i * per + c, :m, j * h : (j + 1) * h]
                    for r in range(rows)
                    for j in range(chunks)
                ],
                axis=0,
            )
        )
    w_in = jnp.concatenate(columns, axis=1)
    w_out_t = jnp.concatenate([w_ref[i * near + c, m:, :] for c in range(near)], axis=0)
    return w_in, w_out_t


def assemble(got_ref, rows_s, rows, near):
    w = got_ref.shape[2]
    for c in range(near):
        for r in range(rows):
            rows_s[c * CAP : (c + 1) * CAP, r * w : (r + 1) * w] = got_ref[r * near + c].astype(F32)


def disperse(values_s, sent_ref, rows, near):
    w = sent_ref.shape[2]
    for c in range(near):
        for r in range(rows):
            piece = values_s[c * CAP : (c + 1) * CAP, r * w : (r + 1) * w]
            sent_ref[r * near + c] = piece.astype(BF16)


ERF = (0.254829592, -0.284496736, 1.421413741, -1.453152027, 1.061405429)


def gelu_pair(x):
    size = jnp.abs(x)
    t = 1.0 / (1.0 + (0.3275911 * 0.5**0.5) * size)
    bell = jnp.exp(-0.5 * x * x)
    tail = ERF[4]
    for coefficient in ERF[3::-1]:
        tail = tail * t + coefficient
    tail = (0.5 * tail) * (t * bell)
    below = jnp.where(x < 0, tail, 1.0 - tail)
    return x * below, below + x * bell * (0.5 / math.pi) ** 0.5


def expert_forward_kernel(
    rows, near, e_ref, got_ref, w_ref, router_ref,
    sent_ref, x_ref, act_ref, slope_ref, res_ref, gates_ref, f_s, in_s, out_s,
):
    assemble(got_ref, f_s, rows, near)
    x_ref[...] = f_s[...].astype(BF16)
    logits = dot(x_ref[...], router_ref[...], ((1,), (1,)))
    powers = jnp.exp(logits - jnp.max(logits, axis=1, keepdims=True))
    gates = powers / jnp.sum(powers, axis=1, keepdims=True)
    gates_ref[...] = gates
    res_ref[...] = jnp.zeros_like(res_ref)

    def step(i, carry):
        in_s[...], out_s[...] = hidden_block(w_ref, i, rows, near)

        def tile(j, carry):
            at = block(j, TILE)
            pre = dot(x_ref[at, :], in_s[...], ((1,), (0,)))
            act, slope = gelu_pair(pre)
            act = act.astype(BF16)
            act_ref[i, at, :] = act
            slope_ref[i, at, :] = slope.astype(BF16)
            res_ref[at, :] += dot(act, out_s[...], ((1,), (1,)))
            return carry

        return lax.fori_loop(0, x_ref.shape[0] // TILE, tile, carry)

    lax.fori_loop(0, rows, step, 0)
    own = lax.broadcasted_iota(jnp.int32, (1, E), 1) == e_ref[0]
    chosen = jnp.sum(jnp.where(own, gates, 0.0), axis=1, keepdims=True)
    f_s[...] = chosen * res_ref[...]
    disperse(f_s, sent_ref, rows, near)


def expert_forward(expert, got, w_got, router_t, rows, near):
    e, _, w = got.shape
    n, width, part = near * CAP, rows * w, w_got.shape[2]
    return call(
        partial(expert_forward_kernel, rows, near),
        "expert_forward",
        (
            shape(got.shape, BF16),
            shape((n, width), BF16),
            shape((rows, n, part), BF16),
            shape((rows, n, part), BF16),
            shape((n, width), F32),
            shape((n, E), F32),
        ),
        3,
        scalars=1,
        scratch=[pltpu.VMEM((n, width), F32)] + [pltpu.VMEM((width, part), BF16)] * 2,
        flops=16 * n * width * rows * part // 4,
        moved=2**24,
    )(expert, got, w_got, router_t)


def expert_backward_kernel(
    rows, near, e_ref, got_ref, w_ref, router_ref, x_ref, slope_ref, res_ref, gates_ref,
    sent_ref, pre_ref, grad_res_ref, router_grad_ref, f_s,
):
    assemble(got_ref, f_s, rows, near)
    cot = f_s[...]
    gates = gates_ref[...]
    own = jnp.where(lax.broadcasted_iota(jnp.int32, (1, E), 1) == e_ref[0], 1.0, 0.0)
    chosen = jnp.sum(gates * own, axis=1, keepdims=True)
    grad_chosen = jnp.sum(cot * res_ref[...], axis=1, keepdims=True)
    grad_logits = (grad_chosen * chosen * (own - gates)).astype(BF16)
    grad_res_ref[...] = (chosen * cot).astype(BF16)
    router_grad_ref[...] = dot(grad_logits, x_ref[...], ((0,), (0,)))
    f_s[...] = dot(grad_logits, router_ref[...], ((1,), (0,)))

    def step(i, carry):
        w_in, w_out_t = hidden_block(w_ref, i, rows, near)
        grad_act = dot(grad_res_ref[...], w_out_t, ((1,), (0,)))
        grad_pre = (grad_act * slope_ref[i].astype(F32)).astype(BF16)
        pre_ref[i] = grad_pre
        f_s[...] += dot(grad_pre, w_in, ((1,), (1,)))
        return carry

    lax.fori_loop(0, rows, step, 0)
    disperse(f_s, sent_ref, rows, near)


def expert_backward(expert, got, w_got, router_t, x_rows, slope, res, gates, rows, near):
    e, _, w = got.shape
    n, width, part = near * CAP, rows * w, w_got.shape[2]
    return call(
        partial(expert_backward_kernel, rows, near),
        "expert_backward",
        (
            shape(got.shape, BF16),
            shape((rows, n, part), BF16),
            shape((n, width), BF16),
            shape((E, width), F32),
        ),
        7,
        scalars=1,
        scratch=[pltpu.VMEM((n, width), F32)],
        flops=16 * n * width * rows * part // 4,
        moved=2**24,
    )(expert, got, w_got, router_t, x_rows, slope, res, gates)


def expert_grads_kernel(rows, near, x_ref, pre_ref, grad_res_ref, act_ref, sent_ref):
    m = sent_ref.shape[1] // 2
    k = sent_ref.shape[2]
    per = near // rows
    h = k // per

    def step(i, carry):
        in_grad = dot(x_ref[...], pre_ref[i], ((0,), (0,))).astype(BF16)
        for r in range(rows):
            for c in range(per):
                for j in range(per):
                    first = (r * per + j) * m
                    sent_ref[r * near + i * per + c, :m, j * h : (j + 1) * h] = in_grad[
                        first : first + m, c * h : (c + 1) * h
                    ]
        out_grad_t = dot(grad_res_ref[...], act_ref[i], ((0,), (0,))).astype(BF16)
        for c in range(near):
            sent_ref[i * near + c, m:, :] = out_grad_t[c * m : (c + 1) * m, :]
        return carry

    lax.fori_loop(0, rows, step, 0)


def expert_grads(x_rows, grad_pre, grad_res, act, like, rows, near):
    n, width = x_rows.shape
    return call(
        partial(expert_grads_kernel, rows, near),
        "expert_grads",
        shape(like.shape, BF16),
        4,
        flops=4 * n * width * rows * like.shape[2],
        moved=2**24,
    )(x_rows, grad_pre, grad_res, act)


def local(
    tokens,
    ln1_gain,
    ln1_bias,
    qkv_weight,
    out_weight,
    ln2_gain,
    ln2_bias,
    router_weight,
    expert_in,
    expert_out,
    routes,
    keep,
    cotangent,
):
    rows, cols = lax.axis_size("row"), lax.axis_size("col")
    groups, near = col_groups()
    width_part = tokens.shape[1]
    width = width_part * rows
    hid_part = expert_in.shape[2]
    out_part = expert_out.shape[2]
    qkv_part, mix_part = qkv_weight.shape[1], out_weight.shape[1]
    chunks = width_part // out_part
    half = cols // 2
    parts = (qkv_part, mix_part)
    tiled = half <= 8 and all(part % 16 == 0 for part in (out_part, *parts))
    row, col = lax.axis_index("row"), lax.axis_index("col")
    here = jnp.stack([row, col // 2, col % 2]).astype(jnp.int32)
    nowhere = jnp.zeros((1,), jnp.int32)
    expert = (row * near + col % near).astype(jnp.int32)[None]

    near_parts = jnp.concatenate([qkv_weight.T, out_weight.T], axis=0)
    norms = jnp.stack([ln1_gain, ln1_bias, ln2_gain, ln2_bias])
    if tiled:
        shared = [router_weight.T, *split_three(norms), jnp.zeros_like(norms, BF16)]
        far = jnp.concatenate(far_swap([near_parts] * half) + shared)
    else:
        far = far_spread(near_parts)
    tok = pad_images(after(tokens, near_parts))
    cot = pad_images(after(cotangent, near_parts))
    pieces = row_swap(for_rows(tok.reshape(rows, -1, width_part)))
    cot_pieces = for_rows(cot.reshape(rows, -1, width_part))
    out_t = expert_out.transpose(0, 2, 1)
    if tiled:
        w_sent = pack_weights(expert_in, out_t)
    else:
        w_sent = jnp.concatenate([pack_in(expert_in, chunks), out_t], axis=1)
    w_got = exchange(after(w_sent, far))
    w_got = all_experts(w_got, rows, near, chunks)
    if tiled:
        mine = row_swap([far] * rows)
        qkv_t, mix_t, router_t, norms = gather_weights(
            here, mine + [core_swap(x) for x in mine], half, parts
        )
    else:
        small = gather_all(far)
        qkv_t = small[:, :, :qkv_part].transpose(1, 2, 0, 3).reshape(3 * width, width)
        mix_t = small[:, :, qkv_part:].transpose(1, 2, 0, 3).reshape(width, width)
        norms = row_spread(jnp.concatenate([norms, router_weight.T.astype(F32)]))
        norms = norms.transpose(1, 0, 2).reshape(4 + E, width)
        router_t = norms[4:].astype(BF16)
        norms = norms[:4]

    routes_t = jnp.pad(
        routes.T.reshape(2, -1, SEQ), ((0, 0), (0, 0), (0, ROWS - SEQ)), constant_values=-1
    ).reshape(2, -1)
    keep_t = jnp.pad(keep.T.reshape(2, -1, SEQ), ((0, 0), (0, 0), (0, ROWS - SEQ))).reshape(2, -1)
    slots = slot_table(routes_t, keep_t)
    columns = slots.T

    sends, laters, saved = attention_forward(here, pieces, cot_pieces, qkv_t, mix_t, norms)
    normed = row_swap(sends)
    others = row_swap(laters)

    def to_experts(x, *earlier):
        return exchange(after(x.reshape(E, CAP, width_part), *earlier))

    x_got = to_experts(dispatch(here, slots, normed), w_got, columns)
    cot_got = to_experts(dispatch(nowhere, slots, [cot]), x_got, *others)
    moved, x_rows, act, slope, res, gates = expert_forward(
        expert, x_got, w_got, router_t, rows, near
    )
    moved = to_experts(moved, cot_got).reshape(E * CAP, width_part)
    grads, grad_pre, grad_res, router_part = expert_backward(
        expert, cot_got, w_got, router_t, x_rows, slope, res, gates, rows, near
    )
    grads = to_experts(grads, moved).reshape(E * CAP, width_part)
    w_grads = expert_grads(x_rows, grad_pre, grad_res, act, w_got, rows, near)
    w_grads = exchange(after(own_experts(w_grads, rows, near, chunks), grads))
    if tiled:
        expert_in_grad, out_grad_t = unpack_grads(w_grads, width_part, hid_part)
    else:
        expert_in_grad = unpack_in(w_grads[:, :out_part], chunks).astype(F32)
        out_grad_t = w_grads[:, out_part:].astype(F32)
    expert_out_grad = out_grad_t.transpose(0, 2, 1)

    back = row_swap(combine(here, columns, grads, rows))
    layer_out = cut_images(finish(here, columns, moved, tok, others))
    back[0] = after(back[0], layer_out)
    sends, outs = attention_backward(
        here, back, pieces, others, qkv_t, mix_t, norms, saved, router_part, half, parts if tiled else None
    )

    if tiled:
        own, other = outs
        mine = add_core(own, core_swap(other))
        sends = [after(x, mine) for x in sends]
        got = far_swap(add_rows(row_swap(mine)))
        got[0] = after(got[0], expert_in_grad)
        qkv_grad, mix_grad, router_grad, *norm_grads = add_far(
            here, got, parts, width_part // cols
        )
        norm_grads = [x.reshape(-1) for x in norm_grads]
    else:
        qkv_grad_t, mix_grad_t, tail = outs
        shares = jnp.concatenate(
            [
                qkv_grad_t.reshape(cols, qkv_part, width),
                mix_grad_t.reshape(cols, mix_part, width),
                jnp.broadcast_to(tail[None], (cols,) + tail.shape),
            ],
            axis=1,
        )
        sums = reduce_all(shares)
        qkv_grad, mix_grad, tail = jnp.split(sums, [qkv_part, qkv_part + mix_part])
        thin = width_part // cols
        tail = lax.dynamic_slice_in_dim(tail, col * thin, thin, axis=1)
        router_grad = tail[:E].T
        norm_grads = [tail[E + j] for j in range(4)]
    tokens_grad = jnp.concatenate(in_order(row_swap(sends), row), axis=0)
    tokens_grad = cut_images(tokens_grad).astype(F32)
    return (
        layer_out,
        tokens_grad,
        norm_grads[0],
        norm_grads[1],
        qkv_grad.T,
        mix_grad.T,
        norm_grads[2],
        norm_grads[3],
        router_grad,
        expert_in_grad,
        expert_out_grad,
    )


def solution(mesh):
    in_specs = (
        P("col", "row"),
        P("row"),
        P("row"),
        P("row", "col"),
        P("row", "col"),
        P("row"),
        P("row"),
        P("row", None),
        P(None, "row", "col"),
        P(None, "row", "col"),
        P("col", None),
        P("col", None),
        P("col", "row"),
    )
    out_specs = (
        P("col", "row"),
        P("col", "row"),
        P(("row", "col")),
        P(("row", "col")),
        P("row", "col"),
        P("row", "col"),
        P(("row", "col")),
        P(("row", "col")),
        P(("row", "col"), None),
        P(None, "row", "col"),
        P(None, "row", "col"),
    )
    return jax.shard_map(local, mesh=mesh, in_specs=in_specs, out_specs=out_specs, check_vma=False)
```
